32 devices in a mesh: tm: 8 (over z, y), head: 4 (over x, core).
Axes of the slice: x: 2, y: 2, z: 4, core: 2. Of those that a mesh axis runs over, the one named last changes fastest.
Arguments:
- query: bfloat16 [1024, 3072], P(('tm', 'head')), may hold values from -100 to 100
- key_cur: bfloat16 [1024, 3072], P(('tm', 'head')), may hold values from -6 to 6
- value_cur: bfloat16 [1024, 3072], P(('tm', 'head')), may hold values from -6 to 6
- d_out: bfloat16 [1024, 3072], P(('tm', 'head')), may hold values from -6 to 6
- key_hist: bfloat16 [2048, 3072], P('tm', 'head'), may hold values from -10 to 10
- value_hist: bfloat16 [2048, 3072], P('tm', 'head'), may hold values from -6 to 6
- hist_len: int32 [8], P('tm'), may hold values from 1 to 256, 1024 in all
Outputs:
- grad_query: bfloat16 [1024, 3072], P(('tm', 'head'))
- grad_key_cur: bfloat16 [1024, 3072], P(('tm', 'head'))
- grad_value_cur: bfloat16 [1024, 3072], P(('tm', 'head'))
- grad_key_hist: bfloat16 [2048, 3072], P('tm', 'head')
- grad_value_hist: bfloat16 [2048, 3072], P('tm', 'head')
The draws below stay inside these ranges and needn't reach their ends.
Inputs may be any that keep to these rules, and one draw needn't show every extreme that they name: `hist_len`: every time shard has at least one filled slot; filled slots come first.
All inputs are finite; a program needn't handle non-finite values.
Results may differ from the reference program's by a relative error of at most 0.019.
Values may be sent and summed in bfloat16 or wider, within the bound.
A program may use at most 128 MiB of HBM per device.

```python
import math
import jax
import jax.numpy as jnp
import numpy as np
from jax import lax

D = 3072
HEADS = 24
HS = 128
HIST_DEV = 256
TOKENS = 1024
HIST = 2048
N_TM = 8


def shared_keys(key):
    base_keys = jax.random.normal(key, (HIST, D), jnp.float32)
    return jnp.clip(base_keys, -6.0, 6.0)


def draw_key_hist(key, part):
    key_table = shared_keys(key)
    return jnp.clip(key_table, -10.0, 10.0).astype(jnp.bfloat16)


def draw_query(key, part):
    key = jax.random.fold_in(key, 3)
    drawn = jnp.clip(jax.random.normal(key, (TOKENS, D), jnp.float32), -6.0, 6.0)
    return drawn.astype(jnp.bfloat16)


def level_of(rng, dims, pieces, low, top_value):
    gain, own = 1.0, jax.random.fold_in(rng, 6)
    for dim, shards_of in pieces:
        draws = jnp.exp(jax.random.uniform(jax.random.fold_in(own, dim), (shards_of,), jnp.float32, low / len(pieces), top_value / len(pieces)))
        gain = gain * jnp.repeat(draws, dims[dim] // shards_of).reshape([-1 if axis == dim else 1 for axis in range(len(dims))])
    return gain


def split_up(count, total, most, lean):
    weights = [(1 << 20) // math.isqrt(rank ** lean) + 1 for rank in range(2, count + 1)]
    rest, holding = total - most - (count - 1), [1] * (count - 1)
    while rest > 0:
        free = [i for i in range(count - 1) if holding[i] < most]
        pool, left = sum([weights[i] for i in free]), rest
        for i in free:
            more = min(most - holding[i], max(1, left * weights[i] // pool), rest)
            holding[i] = holding[i] + more
            rest = rest - more
    return np.array([most] + holding)


def uneven_parts(stream_key, count, total, most, skew):
    if count == 2:
        one = jax.random.randint(stream_key, (), max(1, total - most), min(most, total - 1) + 1)
        return jnp.stack([one, total - one])
    lengths = jnp.asarray(split_up(count, total, most, skew), jnp.int32)
    couples = (count - 1) // 2
    source_of, sink = lengths[1:1 + 2 * couples:2], lengths[2:2 + 2 * couples:2]
    slack = jnp.minimum(source_of - 1, most - sink)
    passed = jax.random.randint(jax.random.fold_in(stream_key, 1), (couples,), 0, 1 << 20) % (slack + 1)
    lengths = lengths.at[1:1 + 2 * couples:2].set(source_of - passed).at[2:2 + 2 * couples:2].set(sink + passed)
    return lengths[jax.random.permutation(jax.random.fold_in(stream_key, 2), count)]


def scatter_about(key, dims, deviation, limit, cuts=(), held_as=jnp.bfloat16):
    loudness = level_of(key, dims, cuts, -0.22, 0.18) if cuts else 1.0
    values = jax.random.normal(key, dims, jnp.float32) * deviation * loudness
    return jnp.minimum(jnp.maximum(values, -limit), limit).astype(held_as)


def setup_inputs(seed: int = 0) -> dict:
    key_list = jax.random.split(jax.random.key(seed), 8)
    query = draw_query(jax.random.fold_in(key_list[7], 71), 0)
    key_cur = scatter_about(key_list[1], (TOKENS, D), 1.0, 6.0, ((0, 32),))
    value_cur = scatter_about(key_list[2], (TOKENS, D), 1.0, 6.0, ((0, 32),))
    d_out = scatter_about(key_list[3], (TOKENS, D), 1.0, 6.0, ((0, 32),))
    key_hist = draw_key_hist(jax.random.fold_in(key_list[7], 71), 0)
    value_hist = scatter_about(key_list[5], (HIST, D), 1.0, 6.0, ((0, 8), (1, 4)))
    hist_len = uneven_parts(key_list[6], N_TM, HIST_DEV * N_TM // 2, HIST_DEV, 2).astype(jnp.int32)
    return dict(query=query, key_cur=key_cur, value_cur=value_cur, d_out=d_out, key_hist=key_hist, value_hist=value_hist, hist_len=hist_len)


def reference(query, key_cur, value_cur, d_out, key_hist, value_hist, hist_len):
    score_scale = 1.0 / math.sqrt(HS)
    slot_index = jnp.arange(HIST)
    live_hist = slot_index % HIST_DEV < hist_len[slot_index // HIST_DEV]
    live_mask = jnp.concatenate([jnp.ones((TOKENS,), dtype=bool), live_hist])
    all_keys = jnp.concatenate([key_cur, key_hist], axis=0)
    all_values = jnp.concatenate([value_cur, value_hist], axis=0)

    def by_heads(array):
        return array.reshape(array.shape[0], HEADS, HS).transpose(1, 0, 2)

    def head_grads(inputs):
        query_head, key_head, value_head, grad_head = inputs
        scores = jnp.dot(query_head, key_head.T, preferred_element_type=jnp.float32) * score_scale
        row_max = lax.optimization_barrier(jnp.max(jnp.where(live_mask[None, :], scores, -jnp.inf), axis=1, keepdims=True))
        weights = jnp.where(live_mask[None, :], jnp.exp(scores - row_max), 0.0)
        row_total = lax.optimization_barrier(jnp.sum(weights, axis=1, keepdims=True))
        grad_scores = jnp.dot(grad_head, value_head.T, preferred_element_type=jnp.float32)
        row_delta = lax.optimization_barrier(jnp.sum(weights * grad_scores, axis=1, keepdims=True)) / row_total
        full_prob = weights / row_total
        prob_low = full_prob.astype(jnp.bfloat16)
        score_grad = (score_scale * full_prob * (grad_scores - row_delta)).astype(jnp.bfloat16)
        grad_q = jnp.dot(score_grad, key_head, preferred_element_type=jnp.float32).astype(jnp.bfloat16)
        grad_k = jnp.dot(score_grad.T, query_head, preferred_element_type=jnp.float32).astype(jnp.bfloat16)
        grad_v = jnp.dot(prob_low.T, grad_head, preferred_element_type=jnp.float32).astype(jnp.bfloat16)
        return (grad_q, grad_k, grad_v)
    grad_q, grad_k, grad_v = lax.map(head_grads, (by_heads(query), by_heads(all_keys), by_heads(all_values), by_heads(d_out)))

    def joined(array):
        return array.transpose(1, 0, 2).reshape(array.shape[1], D)
    grad_q = joined(grad_q)
    grad_k = joined(grad_k)
    grad_v = joined(grad_v)
    return (grad_q, grad_k[:TOKENS], grad_v[:TOKENS], grad_k[TOKENS:], grad_v[TOKENS:])
```

```python
import math

import jax
import jax.numpy as jnp
from jax import lax
from jax.sharding import PartitionSpec as P

HS = 128


def to_heads(x, axis_name="head"):
    return lax.all_to_all(x, axis_name, split_axis=1, concat_axis=0, tiled=True)


def shards(query, key_cur, value_cur, d_out, key_hist, value_hist, hist_len):
    n_head = lax.axis_size("head")
    rows, width = query.shape
    feat = width // n_head
    heads = feat // HS
    scale = 1.0 / math.sqrt(HS)

    both = jnp.stack([query, d_out], axis=0).reshape(2, rows, n_head, feat)
    both = lax.all_to_all(both, "head", split_axis=2, concat_axis=1, tiled=True)
    both = both.reshape(2, rows * n_head, feat)
    both = lax.all_gather(both, "tm", axis=1, tiled=True)
    queries, grads = both[0], both[1]
    n_q = queries.shape[0]

    kv = jnp.stack([key_cur, value_cur], axis=0).reshape(2, rows, n_head, feat)
    kv = lax.all_to_all(kv, "head", split_axis=2, concat_axis=1, tiled=True)
    kv = kv.reshape(2, rows * n_head, feat)
    cur = rows * n_head
    keys = jnp.concatenate([kv[0], key_hist], axis=0)
    values = jnp.concatenate([kv[1], value_hist], axis=0)
    n_k = keys.shape[0]

    def by_head(x):
        return x.reshape(x.shape[0], heads, HS).transpose(1, 0, 2)

    qh, gh, kh, vh = by_head(queries), by_head(grads), by_head(keys), by_head(values)
    slot = jnp.arange(n_k)
    live = (slot < cur) | (slot - cur < hist_len[0])
    s = jnp.einsum("hqd,hkd->hqk", qh, kh, preferred_element_type=jnp.float32) * scale
    g = jnp.einsum("hqd,hkd->hqk", gh, vh, preferred_element_type=jnp.float32)
    m = jnp.max(jnp.where(live, s, -jnp.inf), axis=2)
    w = jnp.where(live, jnp.exp(s - m[:, :, None]), 0.0)
    total = jnp.sum(w, axis=2)
    dots = jnp.sum(w * g, axis=2)
    stats = lax.all_gather(jnp.stack([m, total, dots]), "tm", axis=0, tiled=False)
    row_max = jnp.max(stats[:, 0], axis=0)
    back = jnp.exp(stats[:, 0] - row_max[None])
    row_total = jnp.sum(stats[:, 1] * back, axis=0)
    delta = jnp.sum(stats[:, 2] * back, axis=0) / row_total
    factor = jnp.exp(m - row_max) / row_total
    p = w * factor[:, :, None]
    prob = p.astype(jnp.bfloat16)
    sg = (scale * p * (g - delta[:, :, None])).astype(jnp.bfloat16)
    gq = jnp.einsum("hqk,hkd->qhd", sg, kh, preferred_element_type=jnp.float32)
    gq = gq.reshape(n_q, feat).astype(jnp.bfloat16)
    gq = lax.psum_scatter(gq, "tm", scatter_dimension=0, tiled=True)
    gk = jnp.einsum("hqk,hqd->khd", sg, qh, preferred_element_type=jnp.float32)
    gv = jnp.einsum("hqk,hqd->khd", prob, gh, preferred_element_type=jnp.float32)
    gk = gk.reshape(n_k, feat).astype(jnp.bfloat16)
    gv = gv.reshape(n_k, feat).astype(jnp.bfloat16)

    def to_tokens(x):
        return lax.all_to_all(x, "head", split_axis=0, concat_axis=1, tiled=True)

    return (to_tokens(gq), to_tokens(gk[:cur]), to_tokens(gv[:cur]), gk[cur:], gv[cur:])


def solution(mesh):
    tok, hist = P(("tm", "head"), None), P("tm", "head")
    return jax.shard_map(
        shards,
        mesh=mesh,
        in_specs=(tok, tok, tok, tok, hist, hist, P("tm")),
        out_specs=(tok, tok, tok, hist, hist),
        check_vma=False,
    )
```

```python
import functools
import math

import jax
import jax.numpy as jnp
from jax import lax
from jax.experimental import pallas as pl
from jax.experimental.pallas import tpu as pltpu
from jax.sharding import PartitionSpec as P

HS = 128
NZ = 4
SLOTS = 8
MESH = pl.DeviceIdType.MESH


def kernel(
    nt, nh,
    query, d_out, key_cur, value_cur, key_hist, value_hist, bias,
    out_q, out_k, out_v, out_kh, out_vh,
    qd, kv, dkv, dq, ry, rz, sz, st, st_in, fin, acc, fq, fkv,
    s_a, r_a, s_kv, r_kv, s_z, r_z, s_y, r_y, s_st, r_st, s_f, r_f,
    s_ry, r_ry, s_rz, r_rz, s_b, r_b, s_c, r_c,
):
    ny = nt // NZ
    rows = query.shape[0]
    feat = query.shape[1] // nh
    heads = feat // HS
    cur = rows * nh
    scale = 1.0 / math.sqrt(HS)
    scale2 = scale * math.log2(math.e)
    t, h = lax.axis_index("tm"), lax.axis_index("head")
    z, y = t // ny, t % ny

    def copy(src, dst, ss, rs, tm, hd):
        return pltpu.make_async_remote_copy(
            src_ref=src, dst_ref=dst, send_sem=ss, recv_sem=rs,
            device_id=(tm, hd), device_id_type=MESH,
        )

    barrier = pltpu.get_barrier_semaphore()
    for k in range(1, nt):
        pl.semaphore_signal(barrier, inc=1, device_id=((t + k) % nt, h), device_id_type=MESH)
    for k in range(1, nh):
        pl.semaphore_signal(barrier, inc=1, device_id=(t, (h + k) % nh), device_id_type=MESH)
    pl.semaphore_wait(barrier, nt + nh - 2)

    def cols(i):
        return pl.ds(pl.multiple_of(i * feat, HS), feat)

    def band(i):
        return pl.ds(pl.multiple_of(i * rows, rows), rows)

    def a_copy(k, i):
        src = (query, d_out)[i]
        p = (h + k) % nh
        return copy(src.at[:, cols(p)], qd.at[t, i, band(h), :], s_a.at[k - 1, i], r_a.at[k - 1, i], t, p)

    def kv_copy(k, i):
        src = (key_cur, value_cur)[i]
        p = (h + k) % nh
        return copy(src.at[:, cols(p)], kv.at[i, band(h), :], s_kv.at[k - 1, i], r_kv.at[k - 1, i], t, p)

    for start in (a_copy, kv_copy):
        for k in range(1, nh):
            for i in range(2):
                start(k, i).start()
    qd[t, 0, band(h), :] = query[:, cols(h)]
    qd[t, 1, band(h), :] = d_out[:, cols(h)]
    kv[0, band(h), :] = key_cur[:, cols(h)]
    kv[1, band(h), :] = value_cur[:, cols(h)]
    kv[0, cur:, :] = key_hist[...]
    kv[1, cur:, :] = value_hist[...]
    st[...] = jnp.zeros_like(st)
    dkv[...] = jnp.zeros_like(dkv)
    for k in range(1, nh):
        for i in range(2):
            a_copy(k, i).wait_recv()

    n_slot = 2 * NZ - 1

    def at_slot(slot):
        dist = (slot + 1) // 2
        up = slot % 2
        zz = jnp.where(up == 1, z - dist, z + dist)
        return zz, dist, up, (zz >= 0) & (zz < NZ)

    def z_copy(zz, way, hop):
        to = jnp.clip(z + (1 if way == 0 else -1), 0, NZ - 1)
        b = zz * ny + y
        return copy(qd.at[b], qd.at[b], s_z.at[way, hop], r_z.at[way, hop], to * ny + y, h)

    def y_copy(zz, slot, k):
        b = zz * ny + y
        return copy(qd.at[b], qd.at[b], s_y.at[slot, k - 1], r_y.at[slot, k - 1], z * ny + (y + k) % ny, h)

    def st_copy(b):
        return copy(st.at[b], st_in.at[t], s_st.at[b], r_st.at[t], b, h)

    def head_cols(i):
        return pl.ds(pl.multiple_of(i * HS, HS), HS)

    def nt_dot(a, b):
        return lax.dot_general(a, b, (((1,), (1,)), ((), ())), preferred_element_type=jnp.float32)

    def pass1(b):
        def one(i, c):
            hc = head_cols(i)
            s = nt_dot(kv[0, :, hc], qd[b, 0, :, hc]) * scale2 + bias[:, :cur]
            g = nt_dot(kv[1, :, hc], qd[b, 1, :, hc])
            m = jnp.max(s, axis=0, keepdims=True)
            w = jnp.exp2(s - m)
            st[b, 0, pl.ds(i, 1), :] = m
            st[b, 1, pl.ds(i, 1), :] = jnp.sum(w, axis=0, keepdims=True)
            st[b, 2, pl.ds(i, 1), :] = jnp.sum(w * g, axis=0, keepdims=True)
            return c

        lax.fori_loop(0, heads, one, 0)

        @pl.when(b != t)
        def _():
            st_copy(b).start()

    def gather_step(n, c):
        zz, dist, up, ok = at_slot(n)

        @pl.when((n < n_slot) & ok)
        def _():
            @pl.when(n == 0)
            def _():
                @pl.when(z + 1 < NZ)
                def _():
                    z_copy(zz, 0, 0).start()

                @pl.when(z > 0)
                def _():
                    z_copy(zz, 1, 0).start()

            for way in range(2):
                @pl.when((n > 0) & (up == 1 - way))
                def _():
                    z_copy(zz, way, dist - 1).wait_recv()

                    @pl.when((z + 1 < NZ) if way == 0 else (z > 0))
                    def _():
                        z_copy(zz, way, dist).start()

            for k in range(1, ny):
                y_copy(zz, n, k).start()

            @pl.when(n == 0)
            def _():
                for k in range(1, nh):
                    for i in range(2):
                        kv_copy(k, i).wait_recv()

            pass1(zz * ny + y)

        m = n - 2
        zm, _, _, okm = at_slot(jnp.maximum(m, 0))

        @pl.when((m >= 0) & okm)
        def _():
            def from_peer(k, cc):
                y_copy(zm, m, k).wait_recv()
                pass1(zm * ny + (y + ny - k) % ny)
                return cc

            lax.fori_loop(1, ny, from_peer, 0)

        return c

    lax.fori_loop(0, n_slot + 2, gather_step, 0)

    st_in[t] = st[t]
    for k in range(1, nt):
        src = (t + nt - k) % nt
        copy(st.at[t], st_in.at[src], s_st.at[src], r_st.at[src], src, h).wait_recv()
    top = jnp.max(st_in[:, 0], axis=0)
    back = jnp.exp2(st_in[:, 0] - top[None])
    total = jnp.sum(st_in[:, 1] * back, axis=0)
    total = jnp.where(total > 0, total, 1.0)
    fin[t, 0] = top
    fin[t, 1] = 1.0 / total
    fin[t, 2] = jnp.sum(st_in[:, 2] * back, axis=0) / total

    def f_copy(k):
        return copy(fin.at[t], fin.at[t], s_f.at[k - 1], r_f.at[k - 1], (t + k) % nt, h)

    for k in range(1, nt):
        f_copy(k).start()
    for k in range(1, nt):
        f_copy(k).wait_recv()

    tile = 2 * cur

    def order(i):
        return jnp.where(z < NZ // 2, NZ - 1 - i, i)

    def ry_copy(d, k):
        p = (y + k) % ny
        return copy(dq.at[d * ny + p], ry.at[d, k - 1], s_ry.at[d, k - 1], r_ry.at[d, k - 1], z * ny + p, h)

    def pass2(n, c):
        d = order(n)

        def pair(j, cc):
            b = d * ny + 2 * j

            def one(i, ccc):
                hc = head_cols(i)
                key, val = kv[0, :, hc], kv[1, :, hc]
                q = jnp.concatenate([qd[b, 0, :, hc], qd[b + 1, 0, :, hc]], axis=0)
                do = jnp.concatenate([qd[b, 1, :, hc], qd[b + 1, 1, :, hc]], axis=0)

                def stat(r):
                    return jnp.concatenate([fin[b, r, pl.ds(i, 1), :], fin[b + 1, r, pl.ds(i, 1), :]], axis=1)

                s = nt_dot(key, q) * scale2 + bias[...]
                g = nt_dot(val, do)
                p = jnp.exp2(s - stat(0)) * stat(1)
                sg = (p * scale * (g - stat(2))).astype(jnp.bfloat16)
                dkv[0, :, hc] += jnp.dot(sg, q, preferred_element_type=jnp.float32)
                dkv[1, :, hc] += jnp.dot(p.astype(jnp.bfloat16), do, preferred_element_type=jnp.float32)
                part = lax.dot_general(
                    sg, key, (((0,), (0,)), ((), ())), preferred_element_type=jnp.float32
                ).astype(jnp.bfloat16)
                dq[b, :, hc] = part[:cur]
                dq[b + 1, :, hc] = part[cur:]
                return ccc

            lax.fori_loop(0, heads, one, 0)
            return cc

        lax.fori_loop(0, ny // 2, pair, 0)
        for k in range(1, ny):
            ry_copy(d, k).start()
        return c

    lax.fori_loop(0, NZ, pass2, 0)

    def b_copy(k, i):
        p = (h + k) % nh
        dst = (out_k, out_v)[i]
        return copy(fkv.at[i, band(p), :], dst.at[:, cols(h)], s_b.at[k - 1, i], r_b.at[k - 1, i], t, p)

    fkv[...] = dkv[:, :cur, :].astype(jnp.bfloat16)
    for k in range(1, nh):
        for i in range(2):
            b_copy(k, i).start()
    out_k[:, cols(h)] = fkv[0, band(h), :]
    out_v[:, cols(h)] = fkv[1, band(h), :]
    out_kh[...] = dkv[0, cur:, :].astype(jnp.bfloat16)
    out_vh[...] = dkv[1, cur:, :].astype(jnp.bfloat16)

    def rz_copy(d, way):
        to = jnp.clip(z + (1 if way == 0 else -1), 0, NZ - 1)
        return copy(sz.at[d], rz.at[way, d], s_rz.at[way, d], r_rz.at[way, d], to * ny + y, h)

    def own_sum(d):
        acc[...] = dq[d * ny + y].astype(jnp.float32)
        for k in range(1, ny):
            ry_copy(d, k).wait_recv()
            acc[...] += ry[d, k - 1].astype(jnp.float32)

        @pl.when((z <= d) & (z > 0))
        def _():
            rz_copy(d, 0).wait_recv()
            acc[...] += rz[0, d].astype(jnp.float32)

        @pl.when((z >= d) & (z < NZ - 1))
        def _():
            rz_copy(d, 1).wait_recv()
            acc[...] += rz[1, d].astype(jnp.float32)

    def chain(n, c):
        d = order(n)

        @pl.when(d != z)
        def _():
            own_sum(d)
            sz[d] = acc[...].astype(jnp.bfloat16)

            @pl.when(z < d)
            def _():
                rz_copy(d, 0).start()

            @pl.when(z > d)
            def _():
                rz_copy(d, 1).start()

        return c

    lax.fori_loop(0, NZ, chain, 0)
    own_sum(z)
    fq[...] = acc[...].astype(jnp.bfloat16)

    def c_copy(k):
        p = (h + k) % nh
        return copy(fq.at[band(p), :], out_q.at[:, cols(h)], s_c.at[k - 1], r_c.at[k - 1], t, p)

    for k in range(1, nh):
        c_copy(k).start()
    out_q[:, cols(h)] = fq[band(h), :]

    for k in range(1, nh):
        c_copy(k).wait()
        for i in range(2):
            b_copy(k, i).wait()
            a_copy(k, i).wait_send()
            kv_copy(k, i).wait_send()
    for k in range(1, nt):
        f_copy(k).wait_send()
        st_copy((t + k) % nt).wait_send()

    def sent(n, c):
        zz, dist, up, ok = at_slot(n)

        @pl.when(ok)
        def _():
            for k in range(1, ny):
                y_copy(zz, n, k).wait_send()
            for way in range(2):
                @pl.when(((n == 0) | (up == 1 - way)) & ((z + 1 < NZ) if way == 0 else (z > 0)))
                def _():
                    z_copy(zz, way, dist).wait_send()

        return c

    lax.fori_loop(0, n_slot, sent, 0)

    def reduced(d, c):
        for k in range(1, ny):
            ry_copy(d, k).wait_send()

        @pl.when(z < d)
        def _():
            rz_copy(d, 0).wait_send()

        @pl.when(z > d)
        def _():
            rz_copy(d, 1).wait_send()

        return c

    lax.fori_loop(0, NZ, reduced, 0)


def shards(query, key_cur, value_cur, d_out, key_hist, value_hist, hist_len):
    nt, nh = lax.axis_size("tm"), lax.axis_size("head")
    ny = nt // NZ
    rows, width = query.shape
    feat = width // nh
    cur = rows * nh
    n_k = cur + key_hist.shape[0]
    slot = jnp.arange(n_k)
    live = (slot < cur) | (slot - cur < hist_len[0])
    bias = jnp.broadcast_to(jnp.where(live, 0.0, -1e30).astype(jnp.float32)[:, None], (n_k, 2 * cur))
    bf, f32 = jnp.bfloat16, jnp.float32
    vmem = pl.BlockSpec(memory_space=pltpu.VMEM)

    def sems(*dims):
        return pltpu.SemaphoreType.DMA(dims)

    out = jax.ShapeDtypeStruct
    return pl.pallas_call(
        functools.partial(kernel, nt, nh),
        out_shape=(
            out((rows, width), bf), out((rows, width), bf), out((rows, width), bf),
            out(key_hist.shape, bf), out(value_hist.shape, bf),
        ),
        in_specs=[vmem] * 7,
        out_specs=(vmem,) * 5,
        scratch_shapes=[
            pltpu.VMEM((nt, 2, cur, feat), bf),
            pltpu.VMEM((2, n_k, feat), bf),
            pltpu.VMEM((2, n_k, feat), f32),
            pltpu.VMEM((nt, cur, feat), bf),
            pltpu.VMEM((NZ, ny - 1, cur, feat), bf),
            pltpu.VMEM((2, NZ, cur, feat), bf),
            pltpu.VMEM((NZ, cur, feat), bf),
            pltpu.VMEM((nt, 3, SLOTS, cur), f32),
            pltpu.VMEM((nt, 3, SLOTS, cur), f32),
            pltpu.VMEM((nt, 3, SLOTS, cur), f32),
            pltpu.VMEM((cur, feat), f32),
            pltpu.VMEM((cur, feat), bf),
            pltpu.VMEM((2, cur, feat), bf),
            sems(nh - 1, 2), sems(nh - 1, 2), sems(nh - 1, 2), sems(nh - 1, 2),
            sems(2, NZ), sems(2, NZ), sems(2 * NZ - 1, ny - 1), sems(2 * NZ - 1, ny - 1),
            sems(nt), sems(nt), sems(nt - 1), sems(nt - 1),
            sems(NZ, ny - 1), sems(NZ, ny - 1), sems(2, NZ), sems(2, NZ),
            sems(nh - 1, 2), sems(nh - 1, 2), sems(nh - 1), sems(nh - 1),
        ],
        compiler_params=pltpu.CompilerParams(
            collective_id=0, has_side_effects=True, vmem_limit_bytes=52 * 1024 * 1024
        ),
        name="attention_backward",
    )(query, d_out, key_cur, value_cur, key_hist, value_hist, bias)


def solution(mesh):
    tok, hist = P(("tm", "head"), None), P("tm", "head")
    return jax.shard_map(
        shards,
        mesh=mesh,
        in_specs=(tok, tok, tok, tok, hist, hist, P("tm")),
        out_specs=(tok, tok, tok, hist, hist),
        check_vma=False,
    )
```

```python
import functools
import math

import jax
import jax.numpy as jnp
from jax import lax
from jax.experimental import pallas as pl
from jax.experimental.pallas import tpu as pltpu
from jax.sharding import PartitionSpec as P

HS = 128
NZ = 4
SLOTS = 8
MESH = pl.DeviceIdType.MESH


def kernel(
    nt, nh, nc,
    hist_len, query, d_out, key_cur, value_cur, key_hist, value_hist,
    out_q, out_k, out_v, out_kh, out_vh,
    qd, kv, dkv, dq, ry, rz, sz, st, st_in, fin, acc, fq, fkv, bias,
    s_a, r_a, s_kv, r_kv, s_z, r_z, s_y, r_y, s_st, r_st, s_f, r_f,
    s_ry, r_ry, s_rz, r_rz, s_b, r_b, s_c, r_c, s_own, s_hist, s_oc,
):
    ny = nt // NZ
    rows = query.shape[0]
    feat = query.shape[1] // nh
    heads = feat // HS
    hpc = heads // nc
    width = hpc * HS
    cur = rows * nh
    n_k = kv.shape[1]
    scale = 1.0 / math.sqrt(HS)
    scale2 = scale * math.log2(math.e)
    t, h = lax.axis_index("tm"), lax.axis_index("head")
    z, y = t // ny, t % ny

    def copy(src, dst, ss, rs, tm, hd):
        return pltpu.make_async_remote_copy(
            src_ref=src, dst_ref=dst, send_sem=ss, recv_sem=rs,
            device_id=(tm, hd), device_id_type=MESH,
        )

    def cols(i, c):
        return pl.ds(pl.multiple_of(i * feat + c * width, HS), width)

    def part(c):
        return pl.ds(pl.multiple_of(c * width, HS), width)

    def band(i):
        return pl.ds(pl.multiple_of(i * rows, rows), rows)

    def own_copy(c, i):
        src = (query, d_out)[i]
        return pltpu.make_async_copy(src.at[:, cols(h, c)], qd.at[c, t, i, band(h), :], s_own.at[c, i])

    def own_kv(i):
        src = (key_cur, value_cur)[i]
        return pltpu.make_async_copy(
            src.at[:, pl.ds(pl.multiple_of(h * feat, HS), feat)], kv.at[i, band(h), :], s_oc.at[i]
        )

    def hist_copy(i):
        return pltpu.make_async_copy((key_hist, value_hist)[i], kv.at[i, pl.ds(cur, n_k - cur), :], s_hist.at[i])

    def a_copy(c, k, i):
        src = (query, d_out)[i]
        p = (h + k) % nh
        return copy(
            src.at[:, cols(p, c)], qd.at[c, t, i, band(h), :], s_a.at[c, k - 1, i], r_a.at[c, k - 1, i], t, p
        )

    def kv_copy(c, k, i):
        src = (key_cur, value_cur)[i]
        p = (h + k) % nh
        return copy(
            src.at[:, cols(p, c)], kv.at[i, band(h), part(c)], s_kv.at[c, k - 1, i], r_kv.at[c, k - 1, i], t, p
        )

    for i in range(2):
        for c in range(nc):
            own_copy(c, i).start()
        own_kv(i).start()
        hist_copy(i).start()

    barrier = pltpu.get_barrier_semaphore()
    for k in range(1, nt):
        pl.semaphore_signal(barrier, inc=1, device_id=((t + k) % nt, h), device_id_type=MESH)
    for k in range(1, nh):
        pl.semaphore_signal(barrier, inc=1, device_id=(t, (h + k) % nh), device_id_type=MESH)
    pl.semaphore_wait(barrier, nt + nh - 2)

    def exchange(c, cc):
        for start in (a_copy, kv_copy):
            for k in range(1, nh):
                for i in range(2):
                    start(c, k, i).start()
        return cc

    lax.fori_loop(0, nc, exchange, 0)
    st[...] = jnp.zeros_like(st)
    dkv[...] = jnp.zeros_like(dkv)
    slot_row = lax.broadcasted_iota(jnp.int32, bias.shape, 0)
    bias[...] = jnp.where(slot_row < cur + hist_len[0], 0.0, -1e30)
    for i in range(2):
        own_kv(i).wait()
        hist_copy(i).wait()

    n_slot = 2 * NZ - 1

    def at_slot(slot):
        dist = (slot + 1) // 2
        up = slot % 2
        zz = jnp.where(up == 1, z - dist, z + dist)
        return zz, dist, up, (zz >= 0) & (zz < NZ)

    def z_copy(c, zz, way, hop):
        to = jnp.clip(z + (1 if way == 0 else -1), 0, NZ - 1)
        b = zz * ny + y
        return copy(qd.at[c, b], qd.at[c, b], s_z.at[c, way, hop], r_z.at[c, way, hop], to * ny + y, h)

    def y_copy(c, zz, slot, k):
        b = zz * ny + y
        p = z * ny + (y + k) % ny
        return copy(qd.at[c, b], qd.at[c, b], s_y.at[c, slot, k - 1], r_y.at[c, slot, k - 1], p, h)

    def st_copy(c, b):
        return copy(st.at[c, b], st_in.at[c, t], s_st.at[c, b], r_st.at[c, t], b, h)

    def head_cols(i):
        return pl.ds(pl.multiple_of(i * HS, HS), HS)

    def nt_dot(a, b):
        return lax.dot_general(a, b, (((1,), (1,)), ((), ())), preferred_element_type=jnp.float32)

    def pass1(c, b):
        for i in range(hpc):
            hc, lc = head_cols(c * hpc + i), slice(i * HS, (i + 1) * HS)
            s = nt_dot(kv[0, :, hc], qd[c, b, 0, :, lc]) * scale2 + bias[:, :cur]
            g = nt_dot(kv[1, :, hc], qd[c, b, 1, :, lc])
            m = jnp.max(s, axis=0, keepdims=True)
            w = jnp.exp2(s - m)
            st[c, b, i : i + 1, :] = m
            st[c, b, hpc + i : hpc + i + 1, :] = jnp.sum(w, axis=0, keepdims=True)
            st[c, b, 2 * hpc + i : 2 * hpc + i + 1, :] = jnp.sum(w * g, axis=0, keepdims=True)

        @pl.when(b != t)
        def _():
            st_copy(c, b).start()

    def own_sends(c):
        for i in range(2):
            own_copy(c, i).wait()
            for k in range(1, nh):
                a_copy(c, k, i).wait_recv()

        @pl.when(z + 1 < NZ)
        def _():
            z_copy(c, z, 0, 0).start()

        @pl.when(z > 0)
        def _():
            z_copy(c, z, 1, 0).start()

        for k in range(1, ny):
            y_copy(c, z, 0, k).start()

    def gather_step(n, c):
        zz, dist, up, ok = at_slot(n)

        @pl.when((n < n_slot) & ok)
        def _():
            for way in range(2):
                @pl.when((n > 0) & (up == 1 - way))
                def _():
                    z_copy(c, zz, way, dist - 1).wait_recv()

                    @pl.when((z + 1 < NZ) if way == 0 else (z > 0))
                    def _():
                        z_copy(c, zz, way, dist).start()

            @pl.when(n > 0)
            def _():
                for k in range(1, ny):
                    y_copy(c, zz, n, k).start()

            @pl.when(n == 0)
            def _():
                for k in range(1, nh):
                    for i in range(2):
                        kv_copy(c, k, i).wait_recv()

            pass1(c, zz * ny + y)

        m = n - 2
        zm, _, _, okm = at_slot(jnp.maximum(m, 0))

        @pl.when((m >= 0) & okm)
        def _():
            def from_peer(k, cc):
                y_copy(c, zm, m, k).wait_recv()
                pass1(c, zm * ny + (y + ny - k) % ny)
                return cc

            lax.fori_loop(1, ny, from_peer, 0)

        return c

    def f_copy(c, k):
        return copy(fin.at[c, t], fin.at[c, t], s_f.at[c, k - 1], r_f.at[c, k - 1], (t + k) % nt, h)

    def join(c):
        st_in[c, t] = st[c, t]
        for k in range(1, nt):
            src = (t + nt - k) % nt
            copy(st.at[c, t], st_in.at[c, src], s_st.at[c, src], r_st.at[c, src], src, h).wait_recv()
        local = st_in[c]
        top = jnp.max(local[:, :hpc], axis=0)
        back = jnp.exp2(local[:, :hpc] - top[None])
        total = jnp.sum(local[:, hpc : 2 * hpc] * back, axis=0)
        dots = jnp.sum(local[:, 2 * hpc : 3 * hpc] * back, axis=0)
        fin[c, t] = jnp.zeros_like(fin[c, t])
        fin[c, t, :hpc, :] = top
        fin[c, t, hpc : 2 * hpc, :] = 1.0 / total
        fin[c, t, 2 * hpc : 3 * hpc, :] = dots / total
        for k in range(1, nt):
            f_copy(c, k).start()

    def order(i):
        return jnp.where(z < NZ // 2, NZ - 1 - i, i)

    def ry_copy(c, d, k):
        p = (y + k) % ny
        return copy(
            dq.at[c, d * ny + p], ry.at[c, d, k - 1], s_ry.at[c, d, k - 1], r_ry.at[c, d, k - 1], z * ny + p, h
        )

    def b_copy(c, k, i):
        p = (h + k) % nh
        dst = (out_k, out_v)[i]
        return copy(
            fkv.at[i, band(p), part(c)], dst.at[:, cols(h, c)], s_b.at[c, k - 1, i], r_b.at[c, k - 1, i], t, p
        )

    def pass2(c):
        for k in range(1, nt):
            f_copy(c, k).wait_recv()

        def group(n, cc):
            d = order(n)

            def pair(j, ccc):
                b = d * ny + 2 * j
                for i in range(hpc):
                    hc, lc = head_cols(c * hpc + i), slice(i * HS, (i + 1) * HS)
                    key, val = kv[0, :, hc], kv[1, :, hc]
                    q = jnp.concatenate([qd[c, b, 0, :, lc], qd[c, b + 1, 0, :, lc]], axis=0)
                    do = jnp.concatenate([qd[c, b, 1, :, lc], qd[c, b + 1, 1, :, lc]], axis=0)

                    def stat(r):
                        row = r * hpc + i
                        return jnp.concatenate(
                            [fin[c, b, row : row + 1, :], fin[c, b + 1, row : row + 1, :]], axis=1
                        )

                    s = nt_dot(key, q) * scale2 + bias[...]
                    g = nt_dot(val, do)
                    p = jnp.exp2(s - stat(0)) * stat(1)
                    sg = (p * scale * (g - stat(2))).astype(jnp.bfloat16)
                    dkv[0, :, hc] += jnp.dot(sg, q, preferred_element_type=jnp.float32)
                    dkv[1, :, hc] += jnp.dot(p.astype(jnp.bfloat16), do, preferred_element_type=jnp.float32)
                    term = lax.dot_general(
                        sg, key, (((0,), (0,)), ((), ())), preferred_element_type=jnp.float32
                    ).astype(jnp.bfloat16)
                    dq[c, b, :, lc] = term[:cur]
                    dq[c, b + 1, :, lc] = term[cur:]
                return ccc

            lax.fori_loop(0, ny // 2, pair, 0)
            for k in range(1, ny):
                ry_copy(c, d, k).start()
            return cc

        lax.fori_loop(0, NZ, group, 0)
        for i in range(2):
            fkv[i, :, part(c)] = dkv[i, :cur, part(c)].astype(jnp.bfloat16)
            for k in range(1, nh):
                b_copy(c, k, i).start()
            out = (out_k, out_v)[i]
            out[:, cols(h, c)] = fkv[i, band(h), part(c)]
            out = (out_kh, out_vh)[i]
            out[:, part(c)] = dkv[i, cur:, part(c)].astype(jnp.bfloat16)

    def rz_copy(c, d, way):
        to = jnp.clip(z + (1 if way == 0 else -1), 0, NZ - 1)
        return copy(sz.at[c, d], rz.at[c, way, d], s_rz.at[c, way, d], r_rz.at[c, way, d], to * ny + y, h)

    def own_sum(c, d):
        acc[...] = dq[c, d * ny + y].astype(jnp.float32)
        for k in range(1, ny):
            ry_copy(c, d, k).wait_recv()
            acc[...] += ry[c, d, k - 1].astype(jnp.float32)

        @pl.when((z <= d) & (z > 0))
        def _():
            rz_copy(c, d, 0).wait_recv()
            acc[...] += rz[c, 0, d].astype(jnp.float32)

        @pl.when((z >= d) & (z < NZ - 1))
        def _():
            rz_copy(c, d, 1).wait_recv()
            acc[...] += rz[c, 1, d].astype(jnp.float32)

    def c_copy(c, k):
        p = (h + k) % nh
        return copy(fq.at[c, band(p), :], out_q.at[:, cols(h, c)], s_c.at[c, k - 1], r_c.at[c, k - 1], t, p)

    def reduce_query(c):
        def chain(n, cc):
            d = order(n)

            @pl.when(d != z)
            def _():
                own_sum(c, d)
                sz[c, d] = acc[...].astype(jnp.bfloat16)

                @pl.when(z < d)
                def _():
                    rz_copy(c, d, 0).start()

                @pl.when(z > d)
                def _():
                    rz_copy(c, d, 1).start()

            return cc

        lax.fori_loop(0, NZ, chain, 0)
        own_sum(c, z)
        fq[c] = acc[...].astype(jnp.bfloat16)
        for k in range(1, nh):
            c_copy(c, k).start()
        out_q[:, cols(h, c)] = fq[c, band(h), :]

    own_sends(0)

    def stage(c, cc):
        @pl.when(c < nc)
        def _():
            lax.fori_loop(0, n_slot + 2, gather_step, c)

        @pl.when(c + 1 < nc)
        def _():
            own_sends(c + 1)

        @pl.when((c >= 1) & (c <= nc))
        def _():
            pass2(c - 1)

        @pl.when(c < nc)
        def _():
            join(c)

        @pl.when(c >= 2)
        def _():
            reduce_query(c - 2)

        return cc

    lax.fori_loop(0, nc + 2, stage, 0)

    def finish(c, cc):
        for k in range(1, nh):
            c_copy(c, k).wait()
            for i in range(2):
                b_copy(c, k, i).wait()
                a_copy(c, k, i).wait_send()
                kv_copy(c, k, i).wait_send()
        for k in range(1, nt):
            f_copy(c, k).wait_send()
            st_copy(c, (t + k) % nt).wait_send()

        def sent(n, ccc):
            zz, dist, up, ok = at_slot(n)

            @pl.when(ok)
            def _():
                for k in range(1, ny):
                    y_copy(c, zz, n, k).wait_send()
                for way in range(2):
                    @pl.when(((n == 0) | (up == 1 - way)) & ((z + 1 < NZ) if way == 0 else (z > 0)))
                    def _():
                        z_copy(c, zz, way, dist).wait_send()

            return ccc

        lax.fori_loop(0, n_slot, sent, 0)

        def reduced(d, ccc):
            for k in range(1, ny):
                ry_copy(c, d, k).wait_send()

            @pl.when(z < d)
            def _():
                rz_copy(c, d, 0).wait_send()

            @pl.when(z > d)
            def _():
                rz_copy(c, d, 1).wait_send()

            return ccc

        lax.fori_loop(0, NZ, reduced, 0)
        return cc

    lax.fori_loop(0, nc, finish, 0)


def shards(query, key_cur, value_cur, d_out, key_hist, value_hist, hist_len):
    nt, nh = lax.axis_size("tm"), lax.axis_size("head")
    ny = nt // NZ
    rows, width = query.shape
    feat = width // nh
    cur = rows * nh
    n_k = cur + key_hist.shape[0]
    nc = 3 if feat % (3 * HS) == 0 else 1
    wide = feat // nc
    hbm = pl.BlockSpec(memory_space=pl.ANY)
    bf, f32 = jnp.bfloat16, jnp.float32
    vmem = pl.BlockSpec(memory_space=pltpu.VMEM)

    def sems(*dims):
        return pltpu.SemaphoreType.DMA(dims)

    out = jax.ShapeDtypeStruct
    return pl.pallas_call(
        functools.partial(kernel, nt, nh, nc),
        out_shape=(
            out((rows, width), bf), out((rows, width), bf), out((rows, width), bf),
            out(key_hist.shape, bf), out(value_hist.shape, bf),
        ),
        in_specs=[pl.BlockSpec(memory_space=pltpu.SMEM)] + [hbm] * 6,
        out_specs=(vmem,) * 5,
        scratch_shapes=[
            pltpu.VMEM((nc, nt, 2, cur, wide), bf),
            pltpu.VMEM((2, n_k, feat), bf),
            pltpu.VMEM((2, n_k, feat), f32),
            pltpu.VMEM((nc, nt, cur, wide), bf),
            pltpu.VMEM((nc, NZ, ny - 1, cur, wide), bf),
            pltpu.VMEM((nc, 2, NZ, cur, wide), bf),
            pltpu.VMEM((nc, NZ, cur, wide), bf),
            pltpu.VMEM((nc, nt, SLOTS, cur), f32),
            pltpu.VMEM((nc, nt, SLOTS, cur), f32),
            pltpu.VMEM((nc, nt, SLOTS, cur), f32),
            pltpu.VMEM((cur, wide), f32),
            pltpu.VMEM((nc, cur, wide), bf),
            pltpu.VMEM((2, cur, feat), bf),
            pltpu.VMEM((n_k, 2 * cur), f32),
            sems(nc, nh - 1, 2), sems(nc, nh - 1, 2), sems(nc, nh - 1, 2), sems(nc, nh - 1, 2),
            sems(nc, 2, NZ), sems(nc, 2, NZ), sems(nc, 2 * NZ - 1, ny - 1), sems(nc, 2 * NZ - 1, ny - 1),
            sems(nc, nt), sems(nc, nt), sems(nc, nt - 1), sems(nc, nt - 1),
            sems(nc, NZ, ny - 1), sems(nc, NZ, ny - 1), sems(nc, 2, NZ), sems(nc, 2, NZ),
            sems(nc, nh - 1, 2), sems(nc, nh - 1, 2), sems(nc, nh - 1), sems(nc, nh - 1),
            sems(nc, 2), sems(2), sems(2),
        ],
        compiler_params=pltpu.CompilerParams(
            collective_id=0, has_side_effects=True, vmem_limit_bytes=52 * 1024 * 1024
        ),
        name="attention_backward",
    )(hist_len, query, d_out, key_cur, value_cur, key_hist, value_hist)


def solution(mesh):
    tok, hist = P(("tm", "head"), None), P("tm", "head")
    return jax.shard_map(
        shards,
        mesh=mesh,
        in_specs=(tok, tok, tok, tok, hist, hist, P("tm")),
        out_specs=(tok, tok, tok, hist, hist),
        check_vma=False,
    )
```

```python
import functools
import math

import jax
import jax.numpy as jnp
from jax import lax
from jax.experimental import pallas as pl
from jax.experimental.pallas import tpu as pltpu
from jax.sharding import PartitionSpec as P

HS = 128
NZ = 4
SLOTS = 8
MESH = pl.DeviceIdType.MESH


def kernel(
    nt, nh, nc,
    hist_len, query, d_out, key_cur, value_cur, key_hist, value_hist,
    out_q, out_k, out_v, out_kh, out_vh,
    qd, kv, dkv, dq, ry, rz, sz, st, st_in, fin, acc, fq, fkv, bias,
    s_a, r_a, s_kv, r_kv, s_z, r_z, s_y, r_y, s_st, r_st, s_f, r_f,
    s_ry, r_ry, s_rz, r_rz, s_b, r_b, s_c, r_c, s_own, s_hist, s_oc,
):
    ny = nt // NZ
    rows = query.shape[0]
    feat = query.shape[1] // nh
    heads = feat // HS
    hpc = heads // nc
    width = hpc * HS
    cur = rows * nh
    n_k = kv.shape[1]
    scale = 1.0 / math.sqrt(HS)
    scale2 = scale * math.log2(math.e)
    t, h = lax.axis_index("tm"), lax.axis_index("head")
    z, y = t // ny, t % ny

    def copy(src, dst, ss, rs, tm, hd):
        return pltpu.make_async_remote_copy(
            src_ref=src, dst_ref=dst, send_sem=ss, recv_sem=rs,
            device_id=(tm, hd), device_id_type=MESH,
        )

    def cols(i, c):
        return pl.ds(pl.multiple_of(i * feat + c * width, HS), width)

    def part(c):
        return pl.ds(pl.multiple_of(c * width, HS), width)

    def band(i):
        return pl.ds(pl.multiple_of(i * rows, rows), rows)

    def own_copy(c, i):
        src = (query, d_out)[i]
        return pltpu.make_async_copy(src.at[:, cols(h, c)], qd.at[c, t, i, band(h), :], s_own.at[c, i])

    def own_kv(i):
        src = (key_cur, value_cur)[i]
        return pltpu.make_async_copy(
            src.at[:, pl.ds(pl.multiple_of(h * feat, HS), feat)], kv.at[i, band(h), :], s_oc.at[i]
        )

    def hist_copy(i):
        return pltpu.make_async_copy((key_hist, value_hist)[i], kv.at[i, pl.ds(cur, n_k - cur), :], s_hist.at[i])

    def a_copy(c, k, i):
        src = (query, d_out)[i]
        p = (h + k) % nh
        return copy(
            src.at[:, cols(p, c)], qd.at[c, t, i, band(h), :], s_a.at[c, k - 1, i], r_a.at[c, k - 1, i], t, p
        )

    def kv_copy(c, k, i):
        src = (key_cur, value_cur)[i]
        p = (h + k) % nh
        return copy(
            src.at[:, cols(p, c)], kv.at[i, band(h), part(c)], s_kv.at[c, k - 1, i], r_kv.at[c, k - 1, i], t, p
        )

    for i in range(2):
        for c in range(nc):
            own_copy(c, i).start()
        own_kv(i).start()
        hist_copy(i).start()

    barrier = pltpu.get_barrier_semaphore()
    for k in range(1, nt):
        pl.semaphore_signal(barrier, inc=1, device_id=((t + k) % nt, h), device_id_type=MESH)
    for k in range(1, nh):
        pl.semaphore_signal(barrier, inc=1, device_id=(t, (h + k) % nh), device_id_type=MESH)
    pl.semaphore_wait(barrier, nt + nh - 2)

    def exchange(c, cc):
        for start in (a_copy, kv_copy):
            for k in range(1, nh):
                for i in range(2):
                    start(c, k, i).start()
        return cc

    lax.fori_loop(0, nc, exchange, 0)
    st[...] = jnp.zeros_like(st)
    dkv[...] = jnp.zeros_like(dkv)
    slot_row = lax.broadcasted_iota(jnp.int32, bias.shape, 0)
    bias[...] = jnp.where(slot_row < cur + hist_len[0], 0.0, -1e30)
    for i in range(2):
        own_kv(i).wait()
        hist_copy(i).wait()

    n_slot = 2 * NZ - 1

    def at_slot(slot):
        dist = (slot + 1) // 2
        up = slot % 2
        zz = jnp.where(up == 1, z - dist, z + dist)
        return zz, dist, up, (zz >= 0) & (zz < NZ)

    def z_copy(c, zz, way, hop):
        to = jnp.clip(z + 1 - 2 * way, 0, NZ - 1)
        b = zz * ny + y
        return copy(qd.at[c, b], qd.at[c, b], s_z.at[c, way, hop], r_z.at[c, way, hop], to * ny + y, h)

    def y_copy(c, zz, slot, k):
        b = zz * ny + y
        p = z * ny + (y + k) % ny
        return copy(qd.at[c, b], qd.at[c, b], s_y.at[c, slot, k - 1], r_y.at[c, slot, k - 1], p, h)

    def st_copy(c, b):
        return copy(st.at[c, b], st_in.at[c, t], s_st.at[c, b], r_st.at[c, t], b, h)

    def head_cols(i):
        return pl.ds(pl.multiple_of(i * HS, HS), HS)

    def nt_dot(a, b):
        return lax.dot_general(a, b, (((1,), (1,)), ((), ())), preferred_element_type=jnp.float32)

    def pass1(c, b):
        for i in range(hpc):
            hc, lc = head_cols(c * hpc + i), slice(i * HS, (i + 1) * HS)
            s = nt_dot(kv[0, :, hc], qd[c, b, 0, :, lc]) * scale2 + bias[:, :cur]
            g = nt_dot(kv[1, :, hc], qd[c, b, 1, :, lc])
            m = jnp.max(s, axis=0, keepdims=True)
            w = jnp.exp2(s - m)
            st[c, b, i : i + 1, :] = m
            st[c, b, hpc + i : hpc + i + 1, :] = jnp.sum(w, axis=0, keepdims=True)
            st[c, b, 2 * hpc + i : 2 * hpc + i + 1, :] = jnp.sum(w * g, axis=0, keepdims=True)

        @pl.when(b != t)
        def _():
            st_copy(c, b).start()

    def own_sends(c):
        for i in range(2):
            own_copy(c, i).wait()
            for k in range(1, nh):
                a_copy(c, k, i).wait_recv()

        @pl.when(z + 1 < NZ)
        def _():
            z_copy(c, z, 0, 0).start()

        @pl.when(z > 0)
        def _():
            z_copy(c, z, 1, 0).start()

        for k in range(1, ny):
            y_copy(c, z, 0, k).start()

    def event(step, e):
        c, hop = step // 2 - e, step % 2 + 2 * e
        return c, hop, (c >= 0) & (c < nc)

    def block_at(hop, way):
        zz = jnp.where(way == 0, z - hop, z + hop)
        return zz, jnp.maximum(2 * hop - 1 + way, 0), (zz >= 0) & (zz < NZ) & ((hop > 0) | (way == 0))

    def forward(step, e):
        c, hop, ok = event(step, e)

        @pl.when(ok & (hop == 0))
        def _():
            own_sends(c)

        def one(way, cc):
            zz, slot, there = block_at(hop, way)

            @pl.when(ok & there & (hop > 0))
            def _():
                z_copy(c, zz, way, hop - 1).wait_recv()
                to = z + 1 - 2 * way

                @pl.when((to >= 0) & (to < NZ))
                def _():
                    z_copy(c, zz, way, hop).start()

                for k in range(1, ny):
                    y_copy(c, zz, slot, k).start()

            return cc

        lax.fori_loop(0, 2, one, 0)

    def own_pass(step, e):
        c, hop, ok = event(step, e)

        @pl.when(ok & (hop == 0))
        def _():
            for k in range(1, nh):
                for i in range(2):
                    kv_copy(c, k, i).wait_recv()

        def one(way, cc):
            zz, _, there = block_at(hop, way)

            @pl.when(ok & there)
            def _():
                pass1(c, zz * ny + y)

            return cc

        lax.fori_loop(0, 2, one, 0)

    def peer_pass(step, e):
        c, hop, ok = event(step, e)

        def one(way, cc):
            zz, slot, there = block_at(hop, way)

            @pl.when(ok & there)
            def _():
                def from_peer(k, ccc):
                    y_copy(c, zz, slot, k).wait_recv()
                    pass1(c, zz * ny + (y + ny - k) % ny)
                    return ccc

                lax.fori_loop(1, ny, from_peer, 0)

            return cc

        lax.fori_loop(0, 2, one, 0)

    def f_copy(c, k):
        return copy(fin.at[c, t], fin.at[c, t], s_f.at[c, k - 1], r_f.at[c, k - 1], (t + k) % nt, h)

    def join(c):
        st_in[c, t] = st[c, t]
        for k in range(1, nt):
            src = (t + nt - k) % nt
            copy(st.at[c, t], st_in.at[c, src], s_st.at[c, src], r_st.at[c, src], src, h).wait_recv()
        local = st_in[c]
        top = jnp.max(local[:, :hpc], axis=0)
        back = jnp.exp2(local[:, :hpc] - top[None])
        total = jnp.sum(local[:, hpc : 2 * hpc] * back, axis=0)
        dots = jnp.sum(local[:, 2 * hpc : 3 * hpc] * back, axis=0)
        fin[c, t] = jnp.zeros_like(fin[c, t])
        fin[c, t, :hpc, :] = top
        fin[c, t, hpc : 2 * hpc, :] = 1.0 / total
        fin[c, t, 2 * hpc : 3 * hpc, :] = dots / total
        for k in range(1, nt):
            f_copy(c, k).start()

    def order(i):
        return jnp.where(z < NZ // 2, NZ - 1 - i, i)

    def ry_copy(c, d, k):
        p = (y + k) % ny
        return copy(
            dq.at[c, d * ny + p], ry.at[c, d, k - 1], s_ry.at[c, d, k - 1], r_ry.at[c, d, k - 1], z * ny + p, h
        )

    def b_copy(c, k, i):
        p = (h + k) % nh
        dst = (out_k, out_v)[i]
        return copy(
            fkv.at[i, band(p), part(c)], dst.at[:, cols(h, c)], s_b.at[c, k - 1, i], r_b.at[c, k - 1, i], t, p
        )

    def pass2(c):
        for k in range(1, nt):
            f_copy(c, k).wait_recv()

        def group(n, cc):
            d = order(n)

            def pair(j, ccc):
                b = d * ny + 2 * j
                for i in range(hpc):
                    hc, lc = head_cols(c * hpc + i), slice(i * HS, (i + 1) * HS)
                    key, val = kv[0, :, hc], kv[1, :, hc]
                    q = jnp.concatenate([qd[c, b, 0, :, lc], qd[c, b + 1, 0, :, lc]], axis=0)
                    do = jnp.concatenate([qd[c, b, 1, :, lc], qd[c, b + 1, 1, :, lc]], axis=0)

                    def stat(r):
                        row = r * hpc + i
                        return jnp.concatenate(
                            [fin[c, b, row : row + 1, :], fin[c, b + 1, row : row + 1, :]], axis=1
                        )

                    s = nt_dot(key, q) * scale2 + bias[...]
                    g = nt_dot(val, do)
                    p = jnp.exp2(s - stat(0)) * stat(1)
                    sg = (p * scale * (g - stat(2))).astype(jnp.bfloat16)
                    dkv[0, :, hc] += jnp.dot(sg, q, preferred_element_type=jnp.float32)
                    dkv[1, :, hc] += jnp.dot(p.astype(jnp.bfloat16), do, preferred_element_type=jnp.float32)
                    term = lax.dot_general(
                        sg, key, (((0,), (0,)), ((), ())), preferred_element_type=jnp.float32
                    ).astype(jnp.bfloat16)
                    dq[c, b, :, lc] = term[:cur]
                    dq[c, b + 1, :, lc] = term[cur:]
                return ccc

            lax.fori_loop(0, ny // 2, pair, 0)
            for k in range(1, ny):
                ry_copy(c, d, k).start()
            return cc

        lax.fori_loop(0, NZ, group, 0)
        for i in range(2):
            fkv[i, :, part(c)] = dkv[i, :cur, part(c)].astype(jnp.bfloat16)
            for k in range(1, nh):
                b_copy(c, k, i).start()
            out = (out_k, out_v)[i]
            out[:, cols(h, c)] = fkv[i, band(h), part(c)]
            out = (out_kh, out_vh)[i]
            out[:, part(c)] = dkv[i, cur:, part(c)].astype(jnp.bfloat16)

    def rz_copy(c, d, way):
        to = jnp.clip(z + (1 if way == 0 else -1), 0, NZ - 1)
        return copy(sz.at[c, d], rz.at[c, way, d], s_rz.at[c, way, d], r_rz.at[c, way, d], to * ny + y, h)

    def own_sum(c, d):
        acc[...] = dq[c, d * ny + y].astype(jnp.float32)
        for k in range(1, ny):
            ry_copy(c, d, k).wait_recv()
            acc[...] += ry[c, d, k - 1].astype(jnp.float32)

        @pl.when((z <= d) & (z > 0))
        def _():
            rz_copy(c, d, 0).wait_recv()
            acc[...] += rz[c, 0, d].astype(jnp.float32)

        @pl.when((z >= d) & (z < NZ - 1))
        def _():
            rz_copy(c, d, 1).wait_recv()
            acc[...] += rz[c, 1, d].astype(jnp.float32)

    def c_copy(c, k):
        p = (h + k) % nh
        return copy(fq.at[c, band(p), :], out_q.at[:, cols(h, c)], s_c.at[c, k - 1], r_c.at[c, k - 1], t, p)

    def chain(c, n):
        d = order(n)

        @pl.when(d != z)
        def _():
            own_sum(c, d)
            sz[c, d] = acc[...].astype(jnp.bfloat16)

            @pl.when(z < d)
            def _():
                rz_copy(c, d, 0).start()

            @pl.when(z > d)
            def _():
                rz_copy(c, d, 1).start()

    def query_back(c):
        own_sum(c, z)
        fq[c] = acc[...].astype(jnp.bfloat16)
        for k in range(1, nh):
            c_copy(c, k).start()
        out_q[:, cols(h, c)] = fq[c, band(h), :]

    def stage(step, cc):
        def each(f, at):
            def run(i, ccc):
                f(at, 1 - i)
                return ccc

            lax.fori_loop(0, 2, run, 0)

        each(forward, step)
        each(own_pass, step)

        @pl.when(step > 0)
        def _():
            each(peer_pass, step - 1)

        half, odd = step // 2, step % 2

        @pl.when((odd == 1) & (half >= 2) & (half - 2 < nc))
        def _():
            pass2(half - 2)

        @pl.when((odd == 0) & (half >= 2) & (half - 2 < nc))
        def _():
            join(half - 2)

        @pl.when((half >= 3) & (half - 3 < nc))
        def _():
            def link(n, ccc):
                chain(half - 3, 2 * odd + n)
                return ccc

            lax.fori_loop(0, 2, link, 0)

            @pl.when(odd == 1)
            def _():
                query_back(half - 3)

        return cc

    lax.fori_loop(0, 2 * nc + 6, stage, 0)

    def finish(c, cc):
        for k in range(1, nh):
            c_copy(c, k).wait()
            for i in range(2):
                b_copy(c, k, i).wait()
                a_copy(c, k, i).wait_send()
                kv_copy(c, k, i).wait_send()
        for k in range(1, nt):
            f_copy(c, k).wait_send()
            st_copy(c, (t + k) % nt).wait_send()

        def sent(n, ccc):
            zz, dist, up, ok = at_slot(n)

            @pl.when(ok)
            def _():
                for k in range(1, ny):
                    y_copy(c, zz, n, k).wait_send()
                for way in range(2):
                    @pl.when(((n == 0) | (up == 1 - way)) & ((z + 1 < NZ) if way == 0 else (z > 0)))
                    def _():
                        z_copy(c, zz, way, dist).wait_send()

            return ccc

        lax.fori_loop(0, n_slot, sent, 0)

        def reduced(d, ccc):
            for k in range(1, ny):
                ry_copy(c, d, k).wait_send()

            @pl.when(z < d)
            def _():
                rz_copy(c, d, 0).wait_send()

            @pl.when(z > d)
            def _():
                rz_copy(c, d, 1).wait_send()

            return ccc

        lax.fori_loop(0, NZ, reduced, 0)
        return cc

    lax.fori_loop(0, nc, finish, 0)


def shards(query, key_cur, value_cur, d_out, key_hist, value_hist, hist_len):
    nt, nh = lax.axis_size("tm"), lax.axis_size("head")
    ny = nt // NZ
    rows, width = query.shape
    feat = width // nh
    cur = rows * nh
    n_k = cur + key_hist.shape[0]
    nc = 3 if feat % (3 * HS) == 0 else 1
    wide = feat // nc
    hbm = pl.BlockSpec(memory_space=pl.ANY)
    bf, f32 = jnp.bfloat16, jnp.float32
    vmem = pl.BlockSpec(memory_space=pltpu.VMEM)

    def sems(*dims):
        return pltpu.SemaphoreType.DMA(dims)

    out = jax.ShapeDtypeStruct
    return pl.pallas_call(
        functools.partial(kernel, nt, nh, nc),
        out_shape=(
            out((rows, width), bf), out((rows, width), bf), out((rows, width), bf),
            out(key_hist.shape, bf), out(value_hist.shape, bf),
        ),
        in_specs=[pl.BlockSpec(memory_space=pltpu.SMEM)] + [hbm] * 6,
        out_specs=(vmem,) * 5,
        scratch_shapes=[
            pltpu.VMEM((nc, nt, 2, cur, wide), bf),
            pltpu.VMEM((2, n_k, feat), bf),
            pltpu.VMEM((2, n_k, feat), f32),
            pltpu.VMEM((nc, nt, cur, wide), bf),
            pltpu.VMEM((nc, NZ, ny - 1, cur, wide), bf),
            pltpu.VMEM((nc, 2, NZ, cur, wide), bf),
            pltpu.VMEM((nc, NZ, cur, wide), bf),
            pltpu.VMEM((nc, nt, SLOTS, cur), f32),
            pltpu.VMEM((nc, nt, SLOTS, cur), f32),
            pltpu.VMEM((nc, nt, SLOTS, cur), f32),
            pltpu.VMEM((cur, wide), f32),
            pltpu.VMEM((nc, cur, wide), bf),
            pltpu.VMEM((2, cur, feat), bf),
            pltpu.VMEM((n_k, 2 * cur), f32),
            sems(nc, nh - 1, 2), sems(nc, nh - 1, 2), sems(nc, nh - 1, 2), sems(nc, nh - 1, 2),
            sems(nc, 2, NZ), sems(nc, 2, NZ), sems(nc, 2 * NZ - 1, ny - 1), sems(nc, 2 * NZ - 1, ny - 1),
            sems(nc, nt), sems(nc, nt), sems(nc, nt - 1), sems(nc, nt - 1),
            sems(nc, NZ, ny - 1), sems(nc, NZ, ny - 1), sems(nc, 2, NZ), sems(nc, 2, NZ),
            sems(nc, nh - 1, 2), sems(nc, nh - 1, 2), sems(nc, nh - 1), sems(nc, nh - 1),
            sems(nc, 2), sems(2), sems(2),
        ],
        compiler_params=pltpu.CompilerParams(
            collective_id=0, has_side_effects=True, vmem_limit_bytes=63 * 1024 * 1024
        ),
        name="attention_backward",
    )(hist_len, query, d_out, key_cur, value_cur, key_hist, value_hist)


def solution(mesh):
    tok, hist = P(("tm", "head"), None), P("tm", "head")
    return jax.shard_map(
        shards,
        mesh=mesh,
        in_specs=(tok, tok, tok, tok, hist, hist, P("tm")),
        out_specs=(tok, tok, tok, hist, hist),
        check_vma=False,
    )
```

```python
import functools
import math

import jax
import jax.numpy as jnp
from jax import lax
from jax.experimental import pallas as pl
from jax.experimental.pallas import tpu as pltpu
from jax.sharding import PartitionSpec as P

HS = 128
NZ = 4
SLOTS = 8
MESH = pl.DeviceIdType.MESH


def kernel(
    nt, nh, nc, keep,
    hist_len, query, d_out, key_cur, value_cur, key_hist, value_hist,
    out_q, out_k, out_v, out_kh, out_vh,
    qd, kv, dkv, dq, ry, rz, sz, st, st_in, fin, acc, fq, fkv, bias, kt, kept,
    s_a, r_a, s_kv, r_kv, s_z, r_z, s_y, r_y, s_st, r_st, s_f, r_f,
    s_ry, r_ry, s_rz, r_rz, s_b, r_b, s_c, r_c, s_own, s_hist, s_oc,
):
    ny = nt // NZ
    rows = query.shape[0]
    feat = query.shape[1] // nh
    heads = feat // HS
    hpc = heads // nc
    width = hpc * HS
    cur = rows * nh
    n_k = kv.shape[1]
    scale = 1.0 / math.sqrt(HS)
    scale2 = scale * math.log2(math.e)
    t, h = lax.axis_index("tm"), lax.axis_index("head")
    z, y = t // ny, t % ny

    def copy(src, dst, ss, rs, tm, hd):
        return pltpu.make_async_remote_copy(
            src_ref=src, dst_ref=dst, send_sem=ss, recv_sem=rs,
            device_id=(tm, hd), device_id_type=MESH,
        )

    def cols(i, c):
        return pl.ds(pl.multiple_of(i * feat + c * width, HS), width)

    def part(c):
        return pl.ds(pl.multiple_of(c * width, HS), width)

    def band(i):
        return pl.ds(pl.multiple_of(i * rows, rows), rows)

    def own_copy(c, i):
        src = (query, d_out)[i]
        return pltpu.make_async_copy(src.at[:, cols(h, c)], qd.at[c, t, i, band(h), :], s_own.at[c, i])

    def own_kv(i):
        src = (key_cur, value_cur)[i]
        return pltpu.make_async_copy(
            src.at[:, pl.ds(pl.multiple_of(h * feat, HS), feat)], kv.at[i, band(h), :], s_oc.at[i]
        )

    def hist_copy(i):
        return pltpu.make_async_copy((key_hist, value_hist)[i], kv.at[i, pl.ds(cur, n_k - cur), :], s_hist.at[i])

    def a_copy(c, k, i):
        src = (query, d_out)[i]
        p = (h + k) % nh
        return copy(
            src.at[:, cols(p, c)], qd.at[c, t, i, band(h), :], s_a.at[c, k - 1, i], r_a.at[c, k - 1, i], t, p
        )

    def kv_copy(c, k, i):
        src = (key_cur, value_cur)[i]
        p = (h + k) % nh
        return copy(
            src.at[:, cols(p, c)], kv.at[i, band(h), part(c)], s_kv.at[c, k - 1, i], r_kv.at[c, k - 1, i], t, p
        )

    for i in range(2):
        for c in range(nc):
            own_copy(c, i).start()
        own_kv(i).start()
        hist_copy(i).start()

    barrier = pltpu.get_barrier_semaphore()
    for k in range(1, nt):
        pl.semaphore_signal(barrier, inc=1, device_id=((t + k) % nt, h), device_id_type=MESH)
    for k in range(1, nh):
        pl.semaphore_signal(barrier, inc=1, device_id=(t, (h + k) % nh), device_id_type=MESH)
    pl.semaphore_wait(barrier, nt + nh - 2)

    def exchange(c, cc):
        for start in (a_copy, kv_copy):
            for k in range(1, nh):
                for i in range(2):
                    start(c, k, i).start()
        return cc

    lax.fori_loop(0, nc, exchange, 0)
    st[...] = jnp.zeros_like(st)
    dkv[...] = jnp.zeros_like(dkv)
    slot_row = lax.broadcasted_iota(jnp.int32, bias.shape, 0)
    bias[...] = jnp.where(slot_row < cur + hist_len[0], 0.0, -1e30)
    for i in range(2):
        own_kv(i).wait()
        hist_copy(i).wait()

    n_slot = 2 * NZ - 1

    def at_slot(slot):
        dist = (slot + 1) // 2
        up = slot % 2
        zz = jnp.where(up == 1, z - dist, z + dist)
        return zz, dist, up, (zz >= 0) & (zz < NZ)

    def z_copy(c, zz, way, hop):
        to = jnp.clip(z + 1 - 2 * way, 0, NZ - 1)
        b = zz * ny + y
        return copy(qd.at[c, b], qd.at[c, b], s_z.at[c, way, hop], r_z.at[c, way, hop], to * ny + y, h)

    def y_copy(c, zz, slot, k):
        b = zz * ny + y
        p = z * ny + (y + k) % ny
        return copy(qd.at[c, b], qd.at[c, b], s_y.at[c, slot, k - 1], r_y.at[c, slot, k - 1], p, h)

    def st_copy(c, b):
        return copy(st.at[c, b], st_in.at[c, t], s_st.at[c, b], r_st.at[c, t], b, h)

    def head_cols(i):
        return pl.ds(pl.multiple_of(i * HS, HS), HS)

    def nt_dot(a, b):
        return lax.dot_general(a, b, (((1,), (1,)), ((), ())), preferred_element_type=jnp.float32)

    def pass1(c, b):
        for i in range(hpc):
            hc, lc = head_cols(c * hpc + i), slice(i * HS, (i + 1) * HS)
            s = nt_dot(kv[0, :, hc], qd[c, b, 0, :, lc]) * scale2 + bias[:, :cur]
            g = nt_dot(kv[1, :, hc], qd[c, b, 1, :, lc])
            m = jnp.max(s, axis=0, keepdims=True)
            w = jnp.exp2(s - m)
            if keep:
                kept[c, b, 0, i] = w
                kept[c, b, 1, i] = g
            st[c, b, i : i + 1, :] = m
            st[c, b, hpc + i : hpc + i + 1, :] = jnp.sum(w, axis=0, keepdims=True)
            st[c, b, 2 * hpc + i : 2 * hpc + i + 1, :] = jnp.sum(w * g, axis=0, keepdims=True)

        @pl.when(b != t)
        def _():
            st_copy(c, b).start()

    def own_sends(c):
        for i in range(2):
            own_copy(c, i).wait()
            for k in range(1, nh):
                a_copy(c, k, i).wait_recv()

        @pl.when(z + 1 < NZ)
        def _():
            z_copy(c, z, 0, 0).start()

        @pl.when(z > 0)
        def _():
            z_copy(c, z, 1, 0).start()

        for k in range(1, ny):
            y_copy(c, z, 0, k).start()

    def event(step, e):
        c, hop = step // 2 - e, step % 2 + 2 * e
        return c, hop, (c >= 0) & (c < nc)

    def block_at(hop, way):
        zz = jnp.where(way == 0, z - hop, z + hop)
        return zz, jnp.maximum(2 * hop - 1 + way, 0), (zz >= 0) & (zz < NZ) & ((hop > 0) | (way == 0))

    def forward(step, e):
        c, hop, ok = event(step, e)

        @pl.when(ok & (hop == 0))
        def _():
            own_sends(c)

        def one(way, cc):
            zz, slot, there = block_at(hop, way)

            @pl.when(ok & there & (hop > 0))
            def _():
                z_copy(c, zz, way, hop - 1).wait_recv()
                to = z + 1 - 2 * way

                @pl.when((to >= 0) & (to < NZ))
                def _():
                    z_copy(c, zz, way, hop).start()

                for k in range(1, ny):
                    y_copy(c, zz, slot, k).start()

            return cc

        lax.fori_loop(0, 2, one, 0)

    def own_pass(step, e):
        c, hop, ok = event(step, e)

        @pl.when(ok & (hop == 0))
        def _():
            for k in range(1, nh):
                for i in range(2):
                    kv_copy(c, k, i).wait_recv()
            kt[part(c), :] = kv[0, :, part(c)].T

        def one(way, cc):
            zz, _, there = block_at(hop, way)

            @pl.when(ok & there)
            def _():
                pass1(c, zz * ny + y)

            return cc

        lax.fori_loop(0, 2, one, 0)

    def peer_pass(step, e):
        c, hop, ok = event(step, e)

        def one(way, cc):
            zz, slot, there = block_at(hop, way)

            @pl.when(ok & there)
            def _():
                def from_peer(k, ccc):
                    y_copy(c, zz, slot, k).wait_recv()
                    pass1(c, zz * ny + (y + ny - k) % ny)
                    return ccc

                lax.fori_loop(1, ny, from_peer, 0)

            return cc

        lax.fori_loop(0, 2, one, 0)

    def f_copy(c, k):
        return copy(fin.at[c, t], fin.at[c, t], s_f.at[c, k - 1], r_f.at[c, k - 1], (t + k) % nt, h)

    def join(c):
        st_in[c, t] = st[c, t]
        for k in range(1, nt):
            src = (t + nt - k) % nt
            copy(st.at[c, t], st_in.at[c, src], s_st.at[c, src], r_st.at[c, src], src, h).wait_recv()
        local = st_in[c]
        top = jnp.max(local[:, :hpc], axis=0)
        back = jnp.exp2(local[:, :hpc] - top[None])
        total = jnp.sum(local[:, hpc : 2 * hpc] * back, axis=0)
        dots = jnp.sum(local[:, 2 * hpc : 3 * hpc] * back, axis=0)
        fin[c, t] = jnp.zeros_like(fin[c, t])
        fin[c, t, :hpc, :] = top
        fin[c, t, hpc : 2 * hpc, :] = 1.0 / total
        fin[c, t, 2 * hpc : 3 * hpc, :] = dots / total
        for k in range(1, nt):
            f_copy(c, k).start()

    def order(i):
        return jnp.where(z < NZ // 2, NZ - 1 - i, i)

    def ry_copy(c, d, k):
        p = (y + k) % ny
        return copy(
            dq.at[c, d * ny + p], ry.at[c, d, k - 1], s_ry.at[c, d, k - 1], r_ry.at[c, d, k - 1], z * ny + p, h
        )

    def b_copy(c, k, i):
        p = (h + k) % nh
        dst = (out_k, out_v)[i]
        return copy(
            fkv.at[i, band(p), part(c)], dst.at[:, cols(h, c)], s_b.at[c, k - 1, i], r_b.at[c, k - 1, i], t, p
        )

    def pass2(c):
        for k in range(1, nt):
            f_copy(c, k).wait_recv()

        def group(n, cc):
            d = order(n)

            def pair(j, ccc):
                b = d * ny + 2 * j
                for i in range(hpc):
                    hc, lc = head_cols(c * hpc + i), slice(i * HS, (i + 1) * HS)
                    key, val = kv[0, :, hc], kv[1, :, hc]
                    q = jnp.concatenate([qd[c, b, 0, :, lc], qd[c, b + 1, 0, :, lc]], axis=0)
                    do = jnp.concatenate([qd[c, b, 1, :, lc], qd[c, b + 1, 1, :, lc]], axis=0)

                    def row(ref, r):
                        at = slice(r * hpc + i, r * hpc + i + 1)
                        return jnp.concatenate([ref[c, b, at, :], ref[c, b + 1, at, :]], axis=1)

                    if keep:
                        share = jnp.exp2(row(st, 0) - row(fin, 0)) * row(fin, 1)
                        p = jnp.concatenate([kept[c, b, 0, i], kept[c, b + 1, 0, i]], axis=1) * share
                        g = jnp.concatenate([kept[c, b, 1, i], kept[c, b + 1, 1, i]], axis=1)
                    else:
                        s = nt_dot(key, q) * scale2 + bias[...]
                        g = nt_dot(val, do)
                        p = jnp.exp2(s - row(fin, 0)) * row(fin, 1)
                    sg = (p * scale * (g - row(fin, 2))).astype(jnp.bfloat16)
                    dkv[0, :, hc] += jnp.dot(sg, q, preferred_element_type=jnp.float32)
                    dkv[1, :, hc] += jnp.dot(p.astype(jnp.bfloat16), do, preferred_element_type=jnp.float32)
                    term = jnp.dot(kt[hc, :], sg, preferred_element_type=jnp.float32).astype(jnp.bfloat16)
                    dq[c, b, lc, :] = term[:, :cur]
                    dq[c, b + 1, lc, :] = term[:, cur:]
                return ccc

            lax.fori_loop(0, ny // 2, pair, 0)
            for k in range(1, ny):
                ry_copy(c, d, k).start()
            return cc

        lax.fori_loop(0, NZ, group, 0)
        for i in range(2):
            fkv[i, :, part(c)] = dkv[i, :cur, part(c)].astype(jnp.bfloat16)
            for k in range(1, nh):
                b_copy(c, k, i).start()
            out = (out_k, out_v)[i]
            out[:, cols(h, c)] = fkv[i, band(h), part(c)]
            out = (out_kh, out_vh)[i]
            out[:, part(c)] = dkv[i, cur:, part(c)].astype(jnp.bfloat16)

    def rz_copy(c, d, way):
        to = jnp.clip(z + (1 if way == 0 else -1), 0, NZ - 1)
        return copy(sz.at[c, d], rz.at[c, way, d], s_rz.at[c, way, d], r_rz.at[c, way, d], to * ny + y, h)

    def own_sum(c, d):
        acc[...] = dq[c, d * ny + y].astype(jnp.float32)
        for k in range(1, ny):
            ry_copy(c, d, k).wait_recv()
            acc[...] += ry[c, d, k - 1].astype(jnp.float32)

        @pl.when((z <= d) & (z > 0))
        def _():
            rz_copy(c, d, 0).wait_recv()
            acc[...] += rz[c, 0, d].astype(jnp.float32)

        @pl.when((z >= d) & (z < NZ - 1))
        def _():
            rz_copy(c, d, 1).wait_recv()
            acc[...] += rz[c, 1, d].astype(jnp.float32)

    def c_copy(c, k):
        p = (h + k) % nh
        return copy(fq.at[c, band(p), :], out_q.at[:, cols(h, c)], s_c.at[c, k - 1], r_c.at[c, k - 1], t, p)

    def chain(c, n):
        d = order(n)

        @pl.when(d != z)
        def _():
            own_sum(c, d)
            sz[c, d] = acc[...].astype(jnp.bfloat16)

            @pl.when(z < d)
            def _():
                rz_copy(c, d, 0).start()

            @pl.when(z > d)
            def _():
                rz_copy(c, d, 1).start()

    def query_back(c):
        own_sum(c, z)
        fq[c] = acc[...].T.astype(jnp.bfloat16)
        for k in range(1, nh):
            c_copy(c, k).start()
        out_q[:, cols(h, c)] = fq[c, band(h), :]

    def stage(step, cc):
        def each(f, at):
            def run(i, ccc):
                f(at, 1 - i)
                return ccc

            lax.fori_loop(0, 2, run, 0)

        each(forward, step)
        each(own_pass, step)

        @pl.when(step > 0)
        def _():
            each(peer_pass, step - 1)

        half, odd = step // 2, step % 2

        @pl.when((odd == 1) & (half >= 2) & (half - 2 < nc))
        def _():
            pass2(half - 2)

        @pl.when((odd == 0) & (half >= 2) & (half - 2 < nc))
        def _():
            join(half - 2)

        @pl.when((half >= 3) & (half - 3 < nc))
        def _():
            def link(n, ccc):
                chain(half - 3, 2 * odd + n)
                return ccc

            lax.fori_loop(0, 2, link, 0)

            @pl.when(odd == 1)
            def _():
                query_back(half - 3)

        return cc

    lax.fori_loop(0, 2 * nc + 6, stage, 0)

    def finish(c, cc):
        for k in range(1, nh):
            c_copy(c, k).wait()
            for i in range(2):
                b_copy(c, k, i).wait()
                a_copy(c, k, i).wait_send()
                kv_copy(c, k, i).wait_send()
        for k in range(1, nt):
            f_copy(c, k).wait_send()
            st_copy(c, (t + k) % nt).wait_send()

        def sent(n, ccc):
            zz, dist, up, ok = at_slot(n)

            @pl.when(ok)
            def _():
                for k in range(1, ny):
                    y_copy(c, zz, n, k).wait_send()
                for way in range(2):
                    @pl.when(((n == 0) | (up == 1 - way)) & ((z + 1 < NZ) if way == 0 else (z > 0)))
                    def _():
                        z_copy(c, zz, way, dist).wait_send()

            return ccc

        lax.fori_loop(0, n_slot, sent, 0)

        def reduced(d, ccc):
            for k in range(1, ny):
                ry_copy(c, d, k).wait_send()

            @pl.when(z < d)
            def _():
                rz_copy(c, d, 0).wait_send()

            @pl.when(z > d)
            def _():
                rz_copy(c, d, 1).wait_send()

            return ccc

        lax.fori_loop(0, NZ, reduced, 0)
        return cc

    lax.fori_loop(0, nc, finish, 0)


def shards(query, key_cur, value_cur, d_out, key_hist, value_hist, hist_len):
    nt, nh = lax.axis_size("tm"), lax.axis_size("head")
    ny = nt // NZ
    rows, width = query.shape
    feat = width // nh
    cur = rows * nh
    n_k = cur + key_hist.shape[0]
    nc = 3 if feat % (3 * HS) == 0 else 1
    wide = feat // nc
    store = (nc, nt, 2, wide // HS, n_k, cur)
    keep = math.prod(store) * 4 <= 24 * 1024 * 1024
    if not keep:
        store = (SLOTS, HS)
    hbm = pl.BlockSpec(memory_space=pl.ANY)
    bf, f32 = jnp.bfloat16, jnp.float32
    vmem = pl.BlockSpec(memory_space=pltpu.VMEM)

    def sems(*dims):
        return pltpu.SemaphoreType.DMA(dims)

    out = jax.ShapeDtypeStruct
    return pl.pallas_call(
        functools.partial(kernel, nt, nh, nc, keep),
        out_shape=(
            out((rows, width), bf), out((rows, width), bf), out((rows, width), bf),
            out(key_hist.shape, bf), out(value_hist.shape, bf),
        ),
        in_specs=[pl.BlockSpec(memory_space=pltpu.SMEM)] + [hbm] * 6,
        out_specs=(vmem,) * 5,
        scratch_shapes=[
            pltpu.VMEM((nc, nt, 2, cur, wide), bf),
            pltpu.VMEM((2, n_k, feat), bf),
            pltpu.VMEM((2, n_k, feat), f32),
            pltpu.VMEM((nc, nt, wide, cur), bf),
            pltpu.VMEM((nc, NZ, ny - 1, wide, cur), bf),
            pltpu.VMEM((nc, 2, NZ, wide, cur), bf),
            pltpu.VMEM((nc, NZ, wide, cur), bf),
            pltpu.VMEM((nc, nt, SLOTS, cur), f32),
            pltpu.VMEM((nc, nt, SLOTS, cur), f32),
            pltpu.VMEM((nc, nt, SLOTS, cur), f32),
            pltpu.VMEM((wide, cur), f32),
            pltpu.VMEM((nc, cur, wide), bf),
            pltpu.VMEM((2, cur, feat), bf),
            pltpu.VMEM((n_k, 2 * cur), f32),
            pltpu.VMEM((feat, n_k), bf),
            pltpu.VMEM(store, f32),
            sems(nc, nh - 1, 2), sems(nc, nh - 1, 2), sems(nc, nh - 1, 2), sems(nc, nh - 1, 2),
            sems(nc, 2, NZ), sems(nc, 2, NZ), sems(nc, 2 * NZ - 1, ny - 1), sems(nc, 2 * NZ - 1, ny - 1),
            sems(nc, nt), sems(nc, nt), sems(nc, nt - 1), sems(nc, nt - 1),
            sems(nc, NZ, ny - 1), sems(nc, NZ, ny - 1), sems(nc, 2, NZ), sems(nc, 2, NZ),
            sems(nc, nh - 1, 2), sems(nc, nh - 1, 2), sems(nc, nh - 1), sems(nc, nh - 1),
            sems(nc, 2), sems(2), sems(2),
        ],
        compiler_params=pltpu.CompilerParams(
            collective_id=0, has_side_effects=True, vmem_limit_bytes=63 * 1024 * 1024
        ),
        name="attention_backward",
    )(hist_len, query, d_out, key_cur, value_cur, key_hist, value_hist)


def solution(mesh):
    tok, hist = P(("tm", "head"), None), P("tm", "head")
    return jax.shard_map(
        shards,
        mesh=mesh,
        in_specs=(tok, tok, tok, tok, hist, hist, P("tm")),
        out_specs=(tok, tok, tok, hist, hist),
        check_vma=False,
    )
```

```python
import functools
import math

import jax
import jax.numpy as jnp
from jax import lax
from jax.experimental import pallas as pl
from jax.experimental.pallas import tpu as pltpu
from jax.sharding import PartitionSpec as P

HS = 128
NZ = 4
SLOTS = 8
MESH = pl.DeviceIdType.MESH


def kernel(
    nt, nh, nc, keep,
    hist_len, query, d_out, key_cur, value_cur, key_hist, value_hist,
    out_q, out_k, out_v, out_kh, out_vh,
    qd, kv, dkv, dq, ry, rz, sz, st, st_in, fin, acc, fq, fkv, bias, kt, kept,
    s_a, r_a, s_kv, r_kv, s_z, r_z, s_y, r_y, s_st, r_st, s_f, r_f,
    s_ry, r_ry, s_rz, r_rz, s_b, r_b, s_c, r_c, s_own, s_hist, s_oc,
):
    ny = nt // NZ
    rows = query.shape[0]
    feat = query.shape[1] // nh
    heads = feat // HS
    hpc = heads // nc
    width = hpc * HS
    cur = rows * nh
    n_k = kv.shape[1]
    scale = 1.0 / math.sqrt(HS)
    scale2 = scale * math.log2(math.e)
    t, h = lax.axis_index("tm"), lax.axis_index("head")
    z, y = t // ny, t % ny

    def copy(src, dst, ss, rs, tm, hd):
        return pltpu.make_async_remote_copy(
            src_ref=src, dst_ref=dst, send_sem=ss, recv_sem=rs,
            device_id=(tm, hd), device_id_type=MESH,
        )

    def cols(i, c):
        return pl.ds(pl.multiple_of(i * feat + c * width, HS), width)

    def part(c):
        return pl.ds(pl.multiple_of(c * width, HS), width)

    def band(i):
        return pl.ds(pl.multiple_of(i * rows, rows), rows)

    def own_copy(c, i):
        src = (query, d_out)[i]
        return pltpu.make_async_copy(src.at[:, cols(h, c)], qd.at[c, t, i, band(h), :], s_own.at[c, i])

    def own_kv(i):
        src = (key_cur, value_cur)[i]
        return pltpu.make_async_copy(
            src.at[:, pl.ds(pl.multiple_of(h * feat, HS), feat)], kv.at[i, band(h), :], s_oc.at[i]
        )

    def hist_copy(i):
        return pltpu.make_async_copy((key_hist, value_hist)[i], kv.at[i, pl.ds(cur, n_k - cur), :], s_hist.at[i])

    def a_copy(c, k, i):
        src = (query, d_out)[i]
        p = (h + k) % nh
        return copy(
            src.at[:, cols(p, c)], qd.at[c, t, i, band(h), :], s_a.at[c, k - 1, i], r_a.at[c, k - 1, i], t, p
        )

    def kv_copy(c, k, i):
        src = (key_cur, value_cur)[i]
        p = (h + k) % nh
        return copy(
            src.at[:, cols(p, c)], kv.at[i, band(h), part(c)], s_kv.at[c, k - 1, i], r_kv.at[c, k - 1, i], t, p
        )

    for i in range(2):
        for c in range(nc):
            own_copy(c, i).start()
        own_kv(i).start()
        hist_copy(i).start()

    barrier = pltpu.get_barrier_semaphore()
    for k in range(1, nt):
        pl.semaphore_signal(barrier, inc=1, device_id=((t + k) % nt, h), device_id_type=MESH)
    for k in range(1, nh):
        pl.semaphore_signal(barrier, inc=1, device_id=(t, (h + k) % nh), device_id_type=MESH)
    pl.semaphore_wait(barrier, nt + nh - 2)

    def exchange(c, cc):
        for start in (a_copy, kv_copy):
            for k in range(1, nh):
                for i in range(2):
                    start(c, k, i).start()
        return cc

    lax.fori_loop(0, nc, exchange, 0)
    st[...] = jnp.zeros_like(st)
    dkv[...] = jnp.zeros_like(dkv)
    slot_row = lax.broadcasted_iota(jnp.int32, bias.shape, 0)
    bias[...] = jnp.where(slot_row < cur + hist_len[0], 0.0, -1e30)
    for i in range(2):
        own_kv(i).wait()
        hist_copy(i).wait()

    n_slot = 2 * NZ - 1

    def at_slot(slot):
        dist = (slot + 1) // 2
        up = slot % 2
        zz = jnp.where(up == 1, z - dist, z + dist)
        return zz, dist, up, (zz >= 0) & (zz < NZ)

    def z_copy(c, zz, way, hop):
        to = jnp.clip(z + 1 - 2 * way, 0, NZ - 1)
        b = zz * ny + y
        return copy(qd.at[c, b], qd.at[c, b], s_z.at[c, way, hop], r_z.at[c, way, hop], to * ny + y, h)

    def y_copy(c, zz, slot, k):
        b = zz * ny + y
        p = z * ny + (y + k) % ny
        return copy(qd.at[c, b], qd.at[c, b], s_y.at[c, slot, k - 1], r_y.at[c, slot, k - 1], p, h)

    def st_copy(c, b):
        return copy(st.at[c, b], st_in.at[c, t], s_st.at[c, b], r_st.at[c, t], b, h)

    def head_cols(i):
        return pl.ds(pl.multiple_of(i * HS, HS), HS)

    def nt_dot(a, b):
        return lax.dot_general(a, b, (((1,), (1,)), ((), ())), preferred_element_type=jnp.float32)

    def pass1(c, b):
        for i in range(hpc):
            hc, lc = head_cols(c * hpc + i), slice(i * HS, (i + 1) * HS)
            s = nt_dot(kv[0, :, hc], qd[c, b, 0, :, lc]) * scale2 + bias[:, :cur]
            g = nt_dot(kv[1, :, hc], qd[c, b, 1, :, lc])
            m = jnp.max(s, axis=0, keepdims=True)
            w = jnp.exp2(s - m)
            if keep:
                kept[c, b, 0, i] = w
                kept[c, b, 1, i] = g
            st[c, b, i : i + 1, :] = m
            st[c, b, hpc + i : hpc + i + 1, :] = jnp.sum(w, axis=0, keepdims=True)
            st[c, b, 2 * hpc + i : 2 * hpc + i + 1, :] = jnp.sum(w * g, axis=0, keepdims=True)

        @pl.when(b != t)
        def _():
            st_copy(c, b).start()

    def own_sends(c):
        for i in range(2):
            own_copy(c, i).wait()
            for k in range(1, nh):
                a_copy(c, k, i).wait_recv()

        @pl.when(z + 1 < NZ)
        def _():
            z_copy(c, z, 0, 0).start()

        @pl.when(z > 0)
        def _():
            z_copy(c, z, 1, 0).start()

        for k in range(1, ny):
            y_copy(c, z, 0, k).start()

    def event(step, e):
        c, hop = step // 2 - e, step % 2 + 2 * e
        return c, hop, (c >= 0) & (c < nc)

    def block_at(hop, way):
        zz = jnp.where(way == 0, z - hop, z + hop)
        return zz, jnp.maximum(2 * hop - 1 + way, 0), (zz >= 0) & (zz < NZ) & ((hop > 0) | (way == 0))

    def forward(step, e):
        c, hop, ok = event(step, e)

        @pl.when(ok & (hop == 0))
        def _():
            own_sends(c)

        def one(way, cc):
            zz, slot, there = block_at(hop, way)

            @pl.when(ok & there & (hop > 0))
            def _():
                z_copy(c, zz, way, hop - 1).wait_recv()
                to = z + 1 - 2 * way

                @pl.when((to >= 0) & (to < NZ))
                def _():
                    z_copy(c, zz, way, hop).start()

                for k in range(1, ny):
                    y_copy(c, zz, slot, k).start()

            return cc

        lax.fori_loop(0, 2, one, 0)

    def own_pass(step, e):
        c, hop, ok = event(step, e)

        @pl.when(ok & (hop == 0))
        def _():
            for k in range(1, nh):
                for i in range(2):
                    kv_copy(c, k, i).wait_recv()
            kt[part(c), :] = kv[0, :, part(c)].T

        def one(way, cc):
            zz, _, there = block_at(hop, way)

            @pl.when(ok & there)
            def _():
                pass1(c, zz * ny + y)

            return cc

        lax.fori_loop(0, 2, one, 0)

    def peer_pass(step, e):
        c, hop, ok = event(step, e)

        def one(way, cc):
            zz, slot, there = block_at(hop, way)

            @pl.when(ok & there)
            def _():
                def from_peer(k, ccc):
                    y_copy(c, zz, slot, k).wait_recv()
                    pass1(c, zz * ny + (y + ny - k) % ny)
                    return ccc

                lax.fori_loop(1, ny, from_peer, 0)

            return cc

        lax.fori_loop(0, 2, one, 0)

    def f_copy(c, k):
        return copy(fin.at[c, t], fin.at[c, t], s_f.at[c, k - 1], r_f.at[c, k - 1], (t + k) % nt, h)

    def join(c):
        st_in[c, t] = st[c, t]
        for k in range(1, nt):
            src = (t + nt - k) % nt
            copy(st.at[c, t], st_in.at[c, src], s_st.at[c, src], r_st.at[c, src], src, h).wait_recv()
        local = st_in[c]
        top = jnp.max(local[:, :hpc], axis=0)
        back = jnp.exp2(local[:, :hpc] - top[None])
        total = jnp.sum(local[:, hpc : 2 * hpc] * back, axis=0)
        dots = jnp.sum(local[:, 2 * hpc : 3 * hpc] * back, axis=0)
        fin[c, t] = jnp.zeros_like(fin[c, t])
        fin[c, t, :hpc, :] = top
        fin[c, t, hpc : 2 * hpc, :] = 1.0 / total
        fin[c, t, 2 * hpc : 3 * hpc, :] = dots / total
        for k in range(1, nt):
            f_copy(c, k).start()

    def order(i):
        return jnp.where(z < NZ // 2, NZ - 1 - i, i)

    def ry_copy(c, d, k):
        p = (y + k) % ny
        return copy(
            dq.at[c, d * ny + p], ry.at[c, d, k - 1], s_ry.at[c, d, k - 1], r_ry.at[c, d, k - 1], z * ny + p, h
        )

    def b_copy(c, k, i):
        p = (h + k) % nh
        dst = (out_k, out_v)[i]
        return copy(
            fkv.at[i, band(p), part(c)], dst.at[:, cols(h, c)], s_b.at[c, k - 1, i], r_b.at[c, k - 1, i], t, p
        )

    def pass2(c):
        for k in range(1, nt):
            f_copy(c, k).wait_recv()

        def group(n, cc):
            d = order(n)

            def pair(j, ccc):
                b = d * ny + 2 * j
                for i in range(hpc):
                    hc, lc = head_cols(c * hpc + i), slice(i * HS, (i + 1) * HS)
                    key, val = kv[0, :, hc], kv[1, :, hc]
                    q = jnp.concatenate([qd[c, b, 0, :, lc], qd[c, b + 1, 0, :, lc]], axis=0)
                    do = jnp.concatenate([qd[c, b, 1, :, lc], qd[c, b + 1, 1, :, lc]], axis=0)

                    def row(ref, r):
                        at = slice(r * hpc + i, r * hpc + i + 1)
                        return jnp.concatenate([ref[c, b, at, :], ref[c, b + 1, at, :]], axis=1)

                    if keep:
                        share = jnp.exp2(row(st, 0) - row(fin, 0)) * row(fin, 1)
                        p = jnp.concatenate([kept[c, b, 0, i], kept[c, b + 1, 0, i]], axis=1) * share
                        g = jnp.concatenate([kept[c, b, 1, i], kept[c, b + 1, 1, i]], axis=1)
                    else:
                        s = nt_dot(key, q) * scale2 + bias[...]
                        g = nt_dot(val, do)
                        p = jnp.exp2(s - row(fin, 0)) * row(fin, 1)
                    sg = (p * scale * (g - row(fin, 2))).astype(jnp.bfloat16)
                    dkv[0, :, hc] += jnp.dot(sg, q, preferred_element_type=jnp.float32)
                    dkv[1, :, hc] += jnp.dot(p.astype(jnp.bfloat16), do, preferred_element_type=jnp.float32)
                    term = jnp.dot(kt[hc, :], sg, preferred_element_type=jnp.float32).astype(jnp.bfloat16)
                    dq[c, b, lc, :] = term[:, :cur]
                    dq[c, b + 1, lc, :] = term[:, cur:]
                return ccc

            lax.fori_loop(0, ny // 2, pair, 0)
            for k in range(1, ny):
                ry_copy(c, d, k).start()
            return cc

        lax.fori_loop(0, NZ, group, 0)
        for i in range(2):
            fkv[i, :, part(c)] = dkv[i, :cur, part(c)].astype(jnp.bfloat16)
            for k in range(1, nh):
                b_copy(c, k, i).start()
            out = (out_k, out_v)[i]
            out[:, cols(h, c)] = fkv[i, band(h), part(c)]
            out = (out_kh, out_vh)[i]
            out[:, part(c)] = dkv[i, cur:, part(c)].astype(jnp.bfloat16)

    def rz_copy(c, d, way):
        to = jnp.clip(z + (1 if way == 0 else -1), 0, NZ - 1)
        return copy(sz.at[c, d], rz.at[c, way, d], s_rz.at[c, way, d], r_rz.at[c, way, d], to * ny + y, h)

    def own_sum(c, d):
        acc[...] = dq[c, d * ny + y].astype(jnp.float32)
        for k in range(1, ny):
            ry_copy(c, d, k).wait_recv()
            acc[...] += ry[c, d, k - 1].astype(jnp.float32)

        @pl.when((z <= d) & (z > 0))
        def _():
            rz_copy(c, d, 0).wait_recv()
            acc[...] += rz[c, 0, d].astype(jnp.float32)

        @pl.when((z >= d) & (z < NZ - 1))
        def _():
            rz_copy(c, d, 1).wait_recv()
            acc[...] += rz[c, 1, d].astype(jnp.float32)

    def c_copy(c, k):
        p = (h + k) % nh
        return copy(fq.at[c, band(p), :], out_q.at[:, cols(h, c)], s_c.at[c, k - 1], r_c.at[c, k - 1], t, p)

    def chain(c, n):
        d = order(n)

        @pl.when(d != z)
        def _():
            own_sum(c, d)
            sz[c, d] = acc[...].astype(jnp.bfloat16)

            @pl.when(z < d)
            def _():
                rz_copy(c, d, 0).start()

            @pl.when(z > d)
            def _():
                rz_copy(c, d, 1).start()

    def query_back(c):
        own_sum(c, z)
        fq[c] = acc[...].T.astype(jnp.bfloat16)
        for k in range(1, nh):
            c_copy(c, k).start()
        out_q[:, cols(h, c)] = fq[c, band(h), :]

    def stage(step, cc):
        def each(f, at):
            def run(i, ccc):
                f(at, 1 - i)
                return ccc

            lax.fori_loop(0, 2, run, 0)

        each(forward, step)
        each(own_pass, step)

        @pl.when(step > 0)
        def _():
            each(peer_pass, step - 1)

        half, odd = step // 2, step % 2

        @pl.when((odd == 1) & (half >= 2) & (half - 2 < nc))
        def _():
            pass2(half - 2)

        @pl.when((odd == 0) & (half >= 2) & (half - 2 < nc))
        def _():
            join(half - 2)

        @pl.when((half >= 3) & (half - 3 < nc))
        def _():
            def link(n, ccc):
                chain(half - 3, 2 * odd + n)
                return ccc

            lax.fori_loop(0, 2, link, 0)

            @pl.when(odd == 1)
            def _():
                query_back(half - 3)

        return cc

    lax.fori_loop(0, 2 * nc + 6, stage, 0)

    def finish(c, cc):
        for k in range(1, nh):
            c_copy(c, k).wait()
            for i in range(2):
                b_copy(c, k, i).wait()
                a_copy(c, k, i).wait_send()
                kv_copy(c, k, i).wait_send()
        for k in range(1, nt):
            f_copy(c, k).wait_send()
            st_copy(c, (t + k) % nt).wait_send()

        def sent(n, ccc):
            zz, dist, up, ok = at_slot(n)

            @pl.when(ok)
            def _():
                for k in range(1, ny):
                    y_copy(c, zz, n, k).wait_send()
                for way in range(2):
                    @pl.when(((n == 0) | (up == 1 - way)) & ((z + 1 < NZ) if way == 0 else (z > 0)))
                    def _():
                        z_copy(c, zz, way, dist).wait_send()

            return ccc

        lax.fori_loop(0, n_slot, sent, 0)

        def reduced(d, ccc):
            for k in range(1, ny):
                ry_copy(c, d, k).wait_send()

            @pl.when(z < d)
            def _():
                rz_copy(c, d, 0).wait_send()

            @pl.when(z > d)
            def _():
                rz_copy(c, d, 1).wait_send()

            return ccc

        lax.fori_loop(0, NZ, reduced, 0)
        return cc

    lax.fori_loop(0, nc, finish, 0)


def kernel_split(
    nt, nh, nc,
    hist_len, query, d_out, key_cur, value_cur, key_hist, value_hist,
    out_q, out_k, out_v, out_kh, out_vh,
    qd, kv, dkv, dq, rz, sz, st, st_in, fin, acc, fq, fkv, bias, kt, kept, lens,
    s_a, r_a, s_kv, r_kv, s_z, r_z, s_st, r_st, s_f, r_f,
    s_rz, r_rz, s_b, r_b, s_c, r_c, s_own, s_hist, s_oc, s_h, r_h, s_hb, r_hb, s_l, r_l,
):
    ny = nt // NZ
    rows = query.shape[0]
    feat = query.shape[1] // nh
    part_w = feat // ny
    heads = part_w // HS
    hpc = heads // nc
    width = hpc * HS
    ng = nh * ny
    cur = rows * ng
    hist = key_hist.shape[0]
    n_k = kv.shape[1]
    scale = 1.0 / math.sqrt(HS)
    scale2 = scale * math.log2(math.e)
    t, h = lax.axis_index("tm"), lax.axis_index("head")
    z, y = t // ny, t % ny
    g = y * nh + h

    def copy(src, dst, ss, rs, tm, hd):
        return pltpu.make_async_remote_copy(
            src_ref=src, dst_ref=dst, send_sem=ss, recv_sem=rs,
            device_id=(tm, hd), device_id_type=MESH,
        )

    def peer(k):
        p = (g + k) % ng
        return p, p // nh, p % nh

    def cols(py, ph, c):
        return pl.ds(pl.multiple_of(ph * feat + py * part_w + c * width, HS), width)

    def hist_cols(py, c):
        return pl.ds(pl.multiple_of(py * part_w + c * width, HS), width)

    def hist_rows(py):
        return pl.ds(pl.multiple_of(cur + py * hist, HS), hist)

    def part(c):
        return pl.ds(pl.multiple_of(c * width, HS), width)

    def band(i):
        return pl.ds(pl.multiple_of(i * rows, rows), rows)

    def own_copy(c, i):
        src = (query, d_out)[i]
        return pltpu.make_async_copy(src.at[:, cols(y, h, c)], qd.at[c, z, i, band(g), :], s_own.at[c, i])

    def own_kv(i):
        src = (key_cur, value_cur)[i]
        return pltpu.make_async_copy(
            src.at[:, pl.ds(pl.multiple_of(h * feat + y * part_w, HS), part_w)], kv.at[i, band(g), :], s_oc.at[i]
        )

    def hist_copy(i):
        src = (key_hist, value_hist)[i]
        return pltpu.make_async_copy(
            src.at[:, pl.ds(pl.multiple_of(y * part_w, HS), part_w)], kv.at[i, hist_rows(y), :], s_hist.at[i]
        )

    def a_copy(c, k, i):
        src = (query, d_out)[i]
        p, py, ph = peer(k)
        return copy(
            src.at[:, cols(py, ph, c)], qd.at[c, z, i, band(g), :],
            s_a.at[c, k - 1, i], r_a.at[c, k - 1, i], z * ny + py, ph,
        )

    def kv_copy(c, k, i):
        src = (key_cur, value_cur)[i]
        p, py, ph = peer(k)
        return copy(
            src.at[:, cols(py, ph, c)], kv.at[i, band(g), part(c)],
            s_kv.at[c, k - 1, i], r_kv.at[c, k - 1, i], z * ny + py, ph,
        )

    def h_copy(c, k, i):
        src = (key_hist, value_hist)[i]
        py = (y + k) % ny
        return copy(
            src.at[:, hist_cols(py, c)], kv.at[i, hist_rows(y), part(c)],
            s_h.at[c, k - 1, i], r_h.at[c, k - 1, i], z * ny + py, h,
        )

    def l_copy(k):
        py = (y + k) % ny
        return copy(lens.at[y], lens.at[y], s_l.at[k - 1], r_l.at[k - 1], z * ny + py, h)

    for i in range(2):
        for c in range(nc):
            own_copy(c, i).start()
        own_kv(i).start()
        hist_copy(i).start()

    barrier = pltpu.get_barrier_semaphore()
    lens[y] = jnp.full(lens.shape[1:], hist_len[0], jnp.int32)
    for k in range(1, NZ):
        to = (z + k) % NZ
        pl.semaphore_signal(barrier, inc=1, device_id=(to * ny + y, h), device_id_type=MESH)
    for k in range(1, ng):
        _, py, ph = peer(k)
        pl.semaphore_signal(barrier, inc=1, device_id=(z * ny + py, ph), device_id_type=MESH)
    pl.semaphore_wait(barrier, NZ + ng - 2)

    for k in range(1, ny):
        l_copy(k).start()

    def exchange(c, cc):
        for i in range(2):
            for k in range(1, ng):
                a_copy(c, k, i).start()
        for i in range(2):
            for k in range(1, ng):
                kv_copy(c, k, i).start()
            for k in range(1, ny):
                h_copy(c, k, i).start()
        return cc

    lax.fori_loop(0, nc, exchange, 0)
    st[...] = jnp.zeros_like(st)
    dkv[...] = jnp.zeros_like(dkv)
    for k in range(1, ny):
        l_copy(k).wait_recv()
    bias[:cur, :] = jnp.zeros((cur, cur), jnp.float32)
    slot_row = lax.broadcasted_iota(jnp.int32, (hist, cur), 0)
    for j in range(ny):
        bias[cur + j * hist : cur + (j + 1) * hist, :] = jnp.where(slot_row < lens[j, :1, :], 0.0, -1e30)
    for i in range(2):
        own_kv(i).wait()
        hist_copy(i).wait()

    def z_copy(c, zz, way, hop):
        to = jnp.clip(z + 1 - 2 * way, 0, NZ - 1)
        return copy(qd.at[c, zz], qd.at[c, zz], s_z.at[c, way, hop], r_z.at[c, way, hop], to * ny + y, h)

    def st_copy(c, b):
        return copy(st.at[c, b], st_in.at[c, z], s_st.at[c, b], r_st.at[c, z], b * ny + y, h)

    def head_cols(i):
        return pl.ds(pl.multiple_of(i * HS, HS), HS)

    def nt_dot(a, b):
        return lax.dot_general(a, b, (((1,), (1,)), ((), ())), preferred_element_type=jnp.float32)

    def pass1(c, b):
        for i in range(hpc):
            hc, lc = head_cols(c * hpc + i), slice(i * HS, (i + 1) * HS)
            s = nt_dot(kv[0, :, hc], qd[c, b, 0, :, lc]) * scale2 + bias[...]
            gs = nt_dot(kv[1, :, hc], qd[c, b, 1, :, lc])
            m = jnp.max(s, axis=0, keepdims=True)
            w = jnp.exp2(s - m)
            kept[c, b, 0, i] = w
            kept[c, b, 1, i] = gs
            st[c, b, i : i + 1, :] = m
            st[c, b, hpc + i : hpc + i + 1, :] = jnp.sum(w, axis=0, keepdims=True)
            st[c, b, 2 * hpc + i : 2 * hpc + i + 1, :] = jnp.sum(w * gs, axis=0, keepdims=True)

        @pl.when(b != z)
        def _():
            st_copy(c, b).start()

    def own_sends(c):
        for i in range(2):
            own_copy(c, i).wait()
            for k in range(1, ng):
                a_copy(c, k, i).wait_recv()

        @pl.when(z + 1 < NZ)
        def _():
            z_copy(c, z, 0, 0).start()

        @pl.when(z > 0)
        def _():
            z_copy(c, z, 1, 0).start()

    def event(step, e):
        c, hop = step // 2 - e, step % 2 + 2 * e
        return c, hop, (c >= 0) & (c < nc)

    def block_at(hop, way):
        zz = jnp.where(way == 0, z - hop, z + hop)
        return zz, (zz >= 0) & (zz < NZ) & ((hop > 0) | (way == 0))

    def forward(step, e):
        c, hop, ok = event(step, e)

        @pl.when(ok & (hop == 0))
        def _():
            own_sends(c)

        def one(way, cc):
            zz, there = block_at(hop, way)

            @pl.when(ok & there & (hop > 0))
            def _():
                z_copy(c, zz, way, hop - 1).wait_recv()
                to = z + 1 - 2 * way

                @pl.when((to >= 0) & (to < NZ))
                def _():
                    z_copy(c, zz, way, hop).start()

            return cc

        lax.fori_loop(0, 2, one, 0)

    def own_pass(step, e):
        c, hop, ok = event(step, e)

        @pl.when(ok & (hop == 0))
        def _():
            for i in range(2):
                for k in range(1, ng):
                    kv_copy(c, k, i).wait_recv()
                for k in range(1, ny):
                    h_copy(c, k, i).wait_recv()
            kt[part(c), :] = kv[0, :, part(c)].T

        def one(way, cc):
            zz, there = block_at(hop, way)

            @pl.when(ok & there)
            def _():
                pass1(c, zz)

            return cc

        lax.fori_loop(0, 2, one, 0)

    def f_copy(c, k):
        to = (z + k) % NZ
        return copy(fin.at[c, z], fin.at[c, z], s_f.at[c, k - 1], r_f.at[c, k - 1], to * ny + y, h)

    def join(c):
        st_in[c, z] = st[c, z]
        for k in range(1, NZ):
            src = (z + NZ - k) % NZ
            copy(st.at[c, z], st_in.at[c, src], s_st.at[c, src], r_st.at[c, src], src * ny + y, h).wait_recv()
        local = st_in[c]
        top = jnp.max(local[:, :hpc], axis=0)
        back = jnp.exp2(local[:, :hpc] - top[None])
        total = jnp.sum(local[:, hpc : 2 * hpc] * back, axis=0)
        dots = jnp.sum(local[:, 2 * hpc : 3 * hpc] * back, axis=0)
        fin[c, z] = jnp.zeros_like(fin[c, z])
        fin[c, z, :hpc, :] = top
        fin[c, z, hpc : 2 * hpc, :] = 1.0 / total
        fin[c, z, 2 * hpc : 3 * hpc, :] = dots / total
        for k in range(1, NZ):
            f_copy(c, k).start()

    def order(i):
        return jnp.where(z < NZ // 2, NZ - 1 - i, i)

    def b_copy(c, k, i):
        p, py, ph = peer(k)
        dst = (out_k, out_v)[i]
        return copy(
            fkv.at[i, band(p), part(c)], dst.at[:, cols(y, h, c)],
            s_b.at[c, k - 1, i], r_b.at[c, k - 1, i], z * ny + py, ph,
        )

    def hb_copy(c, k, i):
        py = (y + k) % ny
        dst = (out_kh, out_vh)[i]
        return copy(
            fkv.at[i, hist_rows(py), part(c)], dst.at[:, hist_cols(y, c)],
            s_hb.at[c, k - 1, i], r_hb.at[c, k - 1, i], z * ny + py, h,
        )

    def pass2(c):
        for k in range(1, NZ):
            f_copy(c, k).wait_recv()

        def group(n, cc):
            d = order(n)
            for i in range(hpc):
                hc, lc = head_cols(c * hpc + i), slice(i * HS, (i + 1) * HS)
                q, do = qd[c, d, 0, :, lc], qd[c, d, 1, :, lc]

                def row(ref, r):
                    return ref[c, d, r * hpc + i : r * hpc + i + 1, :]

                share = jnp.exp2(row(st, 0) - row(fin, 0)) * row(fin, 1)
                p = kept[c, d, 0, i] * share
                sg = (p * scale * (kept[c, d, 1, i] - row(fin, 2))).astype(jnp.bfloat16)
                dkv[0, :, hc] += jnp.dot(sg, q, preferred_element_type=jnp.float32)
                dkv[1, :, hc] += jnp.dot(p.astype(jnp.bfloat16), do, preferred_element_type=jnp.float32)
                dq[c, d, lc, :] = jnp.dot(kt[hc, :], sg, preferred_element_type=jnp.float32).astype(jnp.bfloat16)
            return cc

        lax.fori_loop(0, NZ, group, 0)
        for i in range(2):
            fkv[i, :, part(c)] = dkv[i, :, part(c)].astype(jnp.bfloat16)
            for k in range(1, ny):
                hb_copy(c, k, i).start()
            for k in range(1, ng):
                b_copy(c, k, i).start()
            out = (out_k, out_v)[i]
            out[:, cols(y, h, c)] = fkv[i, band(g), part(c)]
            out = (out_kh, out_vh)[i]
            out[:, hist_cols(y, c)] = fkv[i, hist_rows(y), part(c)]

    def rz_copy(c, d, way):
        to = jnp.clip(z + (1 if way == 0 else -1), 0, NZ - 1)
        return copy(sz.at[c, d], rz.at[c, way, d], s_rz.at[c, way, d], r_rz.at[c, way, d], to * ny + y, h)

    def own_sum(c, d):
        acc[...] = dq[c, d].astype(jnp.float32)

        @pl.when((z <= d) & (z > 0))
        def _():
            rz_copy(c, d, 0).wait_recv()
            acc[...] += rz[c, 0, d].astype(jnp.float32)

        @pl.when((z >= d) & (z < NZ - 1))
        def _():
            rz_copy(c, d, 1).wait_recv()
            acc[...] += rz[c, 1, d].astype(jnp.float32)

    def c_copy(c, k):
        p, py, ph = peer(k)
        return copy(
            fq.at[c, band(p), :], out_q.at[:, cols(y, h, c)], s_c.at[c, k - 1], r_c.at[c, k - 1], z * ny + py, ph
        )

    def chain(c, n):
        d = order(n)

        @pl.when(d != z)
        def _():
            own_sum(c, d)
            sz[c, d] = acc[...].astype(jnp.bfloat16)

            @pl.when(z < d)
            def _():
                rz_copy(c, d, 0).start()

            @pl.when(z > d)
            def _():
                rz_copy(c, d, 1).start()

    def query_back(c):
        own_sum(c, z)
        fq[c] = acc[...].T.astype(jnp.bfloat16)
        for k in range(1, ng):
            c_copy(c, k).start()
        out_q[:, cols(y, h, c)] = fq[c, band(g), :]

    def stage(step, cc):
        def each(f, at):
            def run(i, ccc):
                f(at, 1 - i)
                return ccc

            lax.fori_loop(0, 2, run, 0)

        each(forward, step)
        each(own_pass, step)

        half, odd = step // 2, step % 2

        @pl.when((odd == 0) & (half >= 2) & (half - 2 < nc))
        def _():
            pass2(half - 2)

        @pl.when((odd == 1) & (half >= 1) & (half - 1 < nc))
        def _():
            join(half - 1)

        late = (step - 5) // 2

        @pl.when((step >= 5) & (late < nc))
        def _():
            def link(n, ccc):
                chain(late, 2 * (1 - odd) + n)
                return ccc

            lax.fori_loop(0, 2, link, 0)

            @pl.when(odd == 0)
            def _():
                query_back(late)

        return cc

    lax.fori_loop(0, 2 * nc + 5, stage, 0)

    def finish(c, cc):
        for k in range(1, ng):
            c_copy(c, k).wait()
            for i in range(2):
                b_copy(c, k, i).wait()
                a_copy(c, k, i).wait_send()
                kv_copy(c, k, i).wait_send()
        for k in range(1, ny):
            for i in range(2):
                hb_copy(c, k, i).wait()
                h_copy(c, k, i).wait_send()
        for k in range(1, NZ):
            f_copy(c, k).wait_send()
            st_copy(c, (z + k) % NZ).wait_send()

        def sent(hop, ccc):
            def one(way, cccc):
                zz, there = block_at(hop, way)
                to = z + 1 - 2 * way
                there = there | ((hop == 0) & (way == 1))

                @pl.when(there & (to >= 0) & (to < NZ))
                def _():
                    z_copy(c, zz, way, hop).wait_send()

                return cccc

            lax.fori_loop(0, 2, one, 0)
            return ccc

        lax.fori_loop(0, NZ, sent, 0)

        def reduced(d, ccc):
            @pl.when(z < d)
            def _():
                rz_copy(c, d, 0).wait_send()

            @pl.when(z > d)
            def _():
                rz_copy(c, d, 1).wait_send()

            return ccc

        lax.fori_loop(0, NZ, reduced, 0)
        return cc

    for k in range(1, ny):
        l_copy(k).wait_send()
    lax.fori_loop(0, nc, finish, 0)


def shards(query, key_cur, value_cur, d_out, key_hist, value_hist, hist_len):
    nt, nh = lax.axis_size("tm"), lax.axis_size("head")
    ny = nt // NZ
    rows, width = query.shape
    feat = width // nh
    cur = rows * nh
    n_k = cur + key_hist.shape[0]
    nc = 3 if feat % (3 * HS) == 0 else 1
    wide = feat // nc
    store = (nc, nt, 2, wide // HS, n_k, cur)
    keep = math.prod(store) * 4 <= 24 * 1024 * 1024
    if not keep:
        store = (SLOTS, HS)
    hbm = pl.BlockSpec(memory_space=pl.ANY)
    bf, f32 = jnp.bfloat16, jnp.float32
    vmem = pl.BlockSpec(memory_space=pltpu.VMEM)

    def sems(*dims):
        return pltpu.SemaphoreType.DMA(dims)

    out = jax.ShapeDtypeStruct
    out_shape = (
        out((rows, width), bf), out((rows, width), bf), out((rows, width), bf),
        out(key_hist.shape, bf), out(value_hist.shape, bf),
    )
    if feat % (ny * HS) == 0:
        ng, part_w, hist = nh * ny, feat // ny, key_hist.shape[0]
        cur, n_k = rows * ng, rows * ng + ny * hist
        nc = part_w // HS
        wide = HS
        return pl.pallas_call(
            functools.partial(kernel_split, nt, nh, nc),
            out_shape=out_shape,
            in_specs=[pl.BlockSpec(memory_space=pltpu.SMEM)] + [hbm] * 6,
            out_specs=(vmem,) * 5,
            scratch_shapes=[
                pltpu.VMEM((nc, NZ, 2, cur, wide), bf),
                pltpu.VMEM((2, n_k, part_w), bf),
                pltpu.VMEM((2, n_k, part_w), f32),
                pltpu.VMEM((nc, NZ, wide, cur), bf),
                pltpu.VMEM((nc, 2, NZ, wide, cur), bf),
                pltpu.VMEM((nc, NZ, wide, cur), bf),
                pltpu.VMEM((nc, NZ, SLOTS, cur), f32),
                pltpu.VMEM((nc, NZ, SLOTS, cur), f32),
                pltpu.VMEM((nc, NZ, SLOTS, cur), f32),
                pltpu.VMEM((wide, cur), f32),
                pltpu.VMEM((nc, cur, wide), bf),
                pltpu.VMEM((2, n_k, part_w), bf),
                pltpu.VMEM((n_k, cur), f32),
                pltpu.VMEM((part_w, n_k), bf),
                pltpu.VMEM((nc, NZ, 2, 1, n_k, cur), f32),
                pltpu.VMEM((ny, SLOTS, cur), jnp.int32),
                sems(nc, ng - 1, 2), sems(nc, ng - 1, 2), sems(nc, ng - 1, 2), sems(nc, ng - 1, 2),
                sems(nc, 2, NZ), sems(nc, 2, NZ),
                sems(nc, NZ), sems(nc, NZ), sems(nc, NZ - 1), sems(nc, NZ - 1),
                sems(nc, 2, NZ), sems(nc, 2, NZ),
                sems(nc, ng - 1, 2), sems(nc, ng - 1, 2), sems(nc, ng - 1), sems(nc, ng - 1),
                sems(nc, 2), sems(2), sems(2),
                sems(nc, ny - 1, 2), sems(nc, ny - 1, 2), sems(nc, ny - 1, 2), sems(nc, ny - 1, 2),
                sems(ny - 1), sems(ny - 1),
            ],
            compiler_params=pltpu.CompilerParams(
                collective_id=0, has_side_effects=True, vmem_limit_bytes=63 * 1024 * 1024
            ),
            name="attention_backward_split",
        )(hist_len, query, d_out, key_cur, value_cur, key_hist, value_hist)
    return pl.pallas_call(
        functools.partial(kernel, nt, nh, nc, keep),
        out_shape=(
            out((rows, width), bf), out((rows, width), bf), out((rows, width), bf),
            out(key_hist.shape, bf), out(value_hist.shape, bf),
        ),
        in_specs=[pl.BlockSpec(memory_space=pltpu.SMEM)] + [hbm] * 6,
        out_specs=(vmem,) * 5,
        scratch_shapes=[
            pltpu.VMEM((nc, nt, 2, cur, wide), bf),
            pltpu.VMEM((2, n_k, feat), bf),
            pltpu.VMEM((2, n_k, feat), f32),
            pltpu.VMEM((nc, nt, wide, cur), bf),
            pltpu.VMEM((nc, NZ, ny - 1, wide, cur), bf),
            pltpu.VMEM((nc, 2, NZ, wide, cur), bf),
            pltpu.VMEM((nc, NZ, wide, cur), bf),
            pltpu.VMEM((nc, nt, SLOTS, cur), f32),
            pltpu.VMEM((nc, nt, SLOTS, cur), f32),
            pltpu.VMEM((nc, nt, SLOTS, cur), f32),
            pltpu.VMEM((wide, cur), f32),
            pltpu.VMEM((nc, cur, wide), bf),
            pltpu.VMEM((2, cur, feat), bf),
            pltpu.VMEM((n_k, 2 * cur), f32),
            pltpu.VMEM((feat, n_k), bf),
            pltpu.VMEM(store, f32),
            sems(nc, nh - 1, 2), sems(nc, nh - 1, 2), sems(nc, nh - 1, 2), sems(nc, nh - 1, 2),
            sems(nc, 2, NZ), sems(nc, 2, NZ), sems(nc, 2 * NZ - 1, ny - 1), sems(nc, 2 * NZ - 1, ny - 1),
            sems(nc, nt), sems(nc, nt), sems(nc, nt - 1), sems(nc, nt - 1),
            sems(nc, NZ, ny - 1), sems(nc, NZ, ny - 1), sems(nc, 2, NZ), sems(nc, 2, NZ),
            sems(nc, nh - 1, 2), sems(nc, nh - 1, 2), sems(nc, nh - 1), sems(nc, nh - 1),
            sems(nc, 2), sems(2), sems(2),
        ],
        compiler_params=pltpu.CompilerParams(
            collective_id=0, has_side_effects=True, vmem_limit_bytes=63 * 1024 * 1024
        ),
        name="attention_backward",
    )(hist_len, query, d_out, key_cur, value_cur, key_hist, value_hist)


def solution(mesh):
    tok, hist = P(("tm", "head"), None), P("tm", "head")
    return jax.shard_map(
        shards,
        mesh=mesh,
        in_specs=(tok, tok, tok, tok, hist, hist, P("tm")),
        out_specs=(tok, tok, tok, hist, hist),
        check_vma=False,
    )
```

```python
import functools
import math

import jax
import jax.numpy as jnp
from jax import lax
from jax.experimental import pallas as pl
from jax.experimental.pallas import tpu as pltpu
from jax.sharding import PartitionSpec as P

HS = 128
NZ = 4
SLOTS = 8
MESH = pl.DeviceIdType.MESH


def kernel(
    nt, nh, nc, keep,
    hist_len, query, d_out, key_cur, value_cur, key_hist, value_hist,
    out_q, out_k, out_v, out_kh, out_vh,
    qd, kv, dkv, dq, ry, rz, sz, st, st_in, fin, acc, fq, fkv, bias, kt, kept,
    s_a, r_a, s_kv, r_kv, s_z, r_z, s_y, r_y, s_st, r_st, s_f, r_f,
    s_ry, r_ry, s_rz, r_rz, s_b, r_b, s_c, r_c, s_own, s_hist, s_oc,
):
    ny = nt // NZ
    rows = query.shape[0]
    feat = query.shape[1] // nh
    heads = feat // HS
    hpc = heads // nc
    width = hpc * HS
    cur = rows * nh
    n_k = kv.shape[1]
    scale = 1.0 / math.sqrt(HS)
    scale2 = scale * math.log2(math.e)
    t, h = lax.axis_index("tm"), lax.axis_index("head")
    z, y = t // ny, t % ny

    def copy(src, dst, ss, rs, tm, hd):
        return pltpu.make_async_remote_copy(
            src_ref=src, dst_ref=dst, send_sem=ss, recv_sem=rs,
            device_id=(tm, hd), device_id_type=MESH,
        )

    def cols(i, c):
        return pl.ds(pl.multiple_of(i * feat + c * width, HS), width)

    def part(c):
        return pl.ds(pl.multiple_of(c * width, HS), width)

    def band(i):
        return pl.ds(pl.multiple_of(i * rows, rows), rows)

    def own_copy(c, i):
        src = (query, d_out)[i]
        return pltpu.make_async_copy(src.at[:, cols(h, c)], qd.at[c, t, i, band(h), :], s_own.at[c, i])

    def own_kv(i):
        src = (key_cur, value_cur)[i]
        return pltpu.make_async_copy(
            src.at[:, pl.ds(pl.multiple_of(h * feat, HS), feat)], kv.at[i, band(h), :], s_oc.at[i]
        )

    def hist_copy(i):
        return pltpu.make_async_copy((key_hist, value_hist)[i], kv.at[i, pl.ds(cur, n_k - cur), :], s_hist.at[i])

    def a_copy(c, k, i):
        src = (query, d_out)[i]
        p = (h + k) % nh
        return copy(
            src.at[:, cols(p, c)], qd.at[c, t, i, band(h), :], s_a.at[c, k - 1, i], r_a.at[c, k - 1, i], t, p
        )

    def kv_copy(c, k, i):
        src = (key_cur, value_cur)[i]
        p = (h + k) % nh
        return copy(
            src.at[:, cols(p, c)], kv.at[i, band(h), part(c)], s_kv.at[c, k - 1, i], r_kv.at[c, k - 1, i], t, p
        )

    for i in range(2):
        for c in range(nc):
            own_copy(c, i).start()
        own_kv(i).start()
        hist_copy(i).start()

    barrier = pltpu.get_barrier_semaphore()
    for k in range(1, nt):
        pl.semaphore_signal(barrier, inc=1, device_id=((t + k) % nt, h), device_id_type=MESH)
    for k in range(1, nh):
        pl.semaphore_signal(barrier, inc=1, device_id=(t, (h + k) % nh), device_id_type=MESH)
    pl.semaphore_wait(barrier, nt + nh - 2)

    def exchange(c, cc):
        for start in (a_copy, kv_copy):
            for k in range(1, nh):
                for i in range(2):
                    start(c, k, i).start()
        return cc

    lax.fori_loop(0, nc, exchange, 0)
    st[...] = jnp.zeros_like(st)
    dkv[...] = jnp.zeros_like(dkv)
    slot_row = lax.broadcasted_iota(jnp.int32, bias.shape, 0)
    bias[...] = jnp.where(slot_row < cur + hist_len[0], 0.0, -1e30)
    for i in range(2):
        own_kv(i).wait()
        hist_copy(i).wait()

    n_slot = 2 * NZ - 1

    def at_slot(slot):
        dist = (slot + 1) // 2
        up = slot % 2
        zz = jnp.where(up == 1, z - dist, z + dist)
        return zz, dist, up, (zz >= 0) & (zz < NZ)

    def z_copy(c, zz, way, hop):
        to = jnp.clip(z + 1 - 2 * way, 0, NZ - 1)
        b = zz * ny + y
        return copy(qd.at[c, b], qd.at[c, b], s_z.at[c, way, hop], r_z.at[c, way, hop], to * ny + y, h)

    def y_copy(c, zz, slot, k):
        b = zz * ny + y
        p = z * ny + (y + k) % ny
        return copy(qd.at[c, b], qd.at[c, b], s_y.at[c, slot, k - 1], r_y.at[c, slot, k - 1], p, h)

    def st_copy(c, b):
        return copy(st.at[c, b], st_in.at[c, t], s_st.at[c, b], r_st.at[c, t], b, h)

    def head_cols(i):
        return pl.ds(pl.multiple_of(i * HS, HS), HS)

    def nt_dot(a, b):
        return lax.dot_general(a, b, (((1,), (1,)), ((), ())), preferred_element_type=jnp.float32)

    def pass1(c, b):
        for i in range(hpc):
            hc, lc = head_cols(c * hpc + i), slice(i * HS, (i + 1) * HS)
            s = nt_dot(kv[0, :, hc], qd[c, b, 0, :, lc]) * scale2 + bias[:, :cur]
            g = nt_dot(kv[1, :, hc], qd[c, b, 1, :, lc])
            m = jnp.max(s, axis=0, keepdims=True)
            w = jnp.exp2(s - m)
            if keep:
                kept[c, b, 0, i] = w
                kept[c, b, 1, i] = g
            st[c, b, i : i + 1, :] = m
            st[c, b, hpc + i : hpc + i + 1, :] = jnp.sum(w, axis=0, keepdims=True)
            st[c, b, 2 * hpc + i : 2 * hpc + i + 1, :] = jnp.sum(w * g, axis=0, keepdims=True)

        @pl.when(b != t)
        def _():
            st_copy(c, b).start()

    def own_sends(c):
        for i in range(2):
            own_copy(c, i).wait()
            for k in range(1, nh):
                a_copy(c, k, i).wait_recv()

        @pl.when(z + 1 < NZ)
        def _():
            z_copy(c, z, 0, 0).start()

        @pl.when(z > 0)
        def _():
            z_copy(c, z, 1, 0).start()

        for k in range(1, ny):
            y_copy(c, z, 0, k).start()

    def event(step, e):
        c, hop = step // 2 - e, step % 2 + 2 * e
        return c, hop, (c >= 0) & (c < nc)

    def block_at(hop, way):
        zz = jnp.where(way == 0, z - hop, z + hop)
        return zz, jnp.maximum(2 * hop - 1 + way, 0), (zz >= 0) & (zz < NZ) & ((hop > 0) | (way == 0))

    def forward(step, e):
        c, hop, ok = event(step, e)

        @pl.when(ok & (hop == 0))
        def _():
            own_sends(c)

        def one(way, cc):
            zz, slot, there = block_at(hop, way)

            @pl.when(ok & there & (hop > 0))
            def _():
                z_copy(c, zz, way, hop - 1).wait_recv()
                to = z + 1 - 2 * way

                @pl.when((to >= 0) & (to < NZ))
                def _():
                    z_copy(c, zz, way, hop).start()

                for k in range(1, ny):
                    y_copy(c, zz, slot, k).start()

            return cc

        lax.fori_loop(0, 2, one, 0)

    def own_pass(step, e):
        c, hop, ok = event(step, e)

        @pl.when(ok & (hop == 0))
        def _():
            for k in range(1, nh):
                for i in range(2):
                    kv_copy(c, k, i).wait_recv()
            kt[part(c), :] = kv[0, :, part(c)].T

        def one(way, cc):
            zz, _, there = block_at(hop, way)

            @pl.when(ok & there)
            def _():
                pass1(c, zz * ny + y)

            return cc

        lax.fori_loop(0, 2, one, 0)

    def peer_pass(step, e):
        c, hop, ok = event(step, e)

        def one(way, cc):
            zz, slot, there = block_at(hop, way)

            @pl.when(ok & there)
            def _():
                def from_peer(k, ccc):
                    y_copy(c, zz, slot, k).wait_recv()
                    pass1(c, zz * ny + (y + ny - k) % ny)
                    return ccc

                lax.fori_loop(1, ny, from_peer, 0)

            return cc

        lax.fori_loop(0, 2, one, 0)

    def f_copy(c, k):
        return copy(fin.at[c, t], fin.at[c, t], s_f.at[c, k - 1], r_f.at[c, k - 1], (t + k) % nt, h)

    def join(c):
        st_in[c, t] = st[c, t]
        for k in range(1, nt):
            src = (t + nt - k) % nt
            copy(st.at[c, t], st_in.at[c, src], s_st.at[c, src], r_st.at[c, src], src, h).wait_recv()
        local = st_in[c]
        top = jnp.max(local[:, :hpc], axis=0)
        back = jnp.exp2(local[:, :hpc] - top[None])
        total = jnp.sum(local[:, hpc : 2 * hpc] * back, axis=0)
        dots = jnp.sum(local[:, 2 * hpc : 3 * hpc] * back, axis=0)
        fin[c, t] = jnp.zeros_like(fin[c, t])
        fin[c, t, :hpc, :] = top
        fin[c, t, hpc : 2 * hpc, :] = 1.0 / total
        fin[c, t, 2 * hpc : 3 * hpc, :] = dots / total
        for k in range(1, nt):
            f_copy(c, k).start()

    def order(i):
        return jnp.where(z < NZ // 2, NZ - 1 - i, i)

    def ry_copy(c, d, k):
        p = (y + k) % ny
        return copy(
            dq.at[c, d * ny + p], ry.at[c, d, k - 1], s_ry.at[c, d, k - 1], r_ry.at[c, d, k - 1], z * ny + p, h
        )

    def b_copy(c, k, i):
        p = (h + k) % nh
        dst = (out_k, out_v)[i]
        return copy(
            fkv.at[i, band(p), part(c)], dst.at[:, cols(h, c)], s_b.at[c, k - 1, i], r_b.at[c, k - 1, i], t, p
        )

    def pass2(c):
        for k in range(1, nt):
            f_copy(c, k).wait_recv()

        def group(n, cc):
            d = order(n)

            def pair(j, ccc):
                b = d * ny + 2 * j
                for i in range(hpc):
                    hc, lc = head_cols(c * hpc + i), slice(i * HS, (i + 1) * HS)
                    key, val = kv[0, :, hc], kv[1, :, hc]
                    q = jnp.concatenate([qd[c, b, 0, :, lc], qd[c, b + 1, 0, :, lc]], axis=0)
                    do = jnp.concatenate([qd[c, b, 1, :, lc], qd[c, b + 1, 1, :, lc]], axis=0)

                    def row(ref, r):
                        at = slice(r * hpc + i, r * hpc + i + 1)
                        return jnp.concatenate([ref[c, b, at, :], ref[c, b + 1, at, :]], axis=1)

                    if keep:
                        share = jnp.exp2(row(st, 0) - row(fin, 0)) * row(fin, 1)
                        p = jnp.concatenate([kept[c, b, 0, i], kept[c, b + 1, 0, i]], axis=1) * share
                        g = jnp.concatenate([kept[c, b, 1, i], kept[c, b + 1, 1, i]], axis=1)
                    else:
                        s = nt_dot(key, q) * scale2 + bias[...]
                        g = nt_dot(val, do)
                        p = jnp.exp2(s - row(fin, 0)) * row(fin, 1)
                    sg = (p * scale * (g - row(fin, 2))).astype(jnp.bfloat16)
                    dkv[0, :, hc] += jnp.dot(sg, q, preferred_element_type=jnp.float32)
                    dkv[1, :, hc] += jnp.dot(p.astype(jnp.bfloat16), do, preferred_element_type=jnp.float32)
                    term = jnp.dot(kt[hc, :], sg, preferred_element_type=jnp.float32).astype(jnp.bfloat16)
                    dq[c, b, lc, :] = term[:, :cur]
                    dq[c, b + 1, lc, :] = term[:, cur:]
                return ccc

            lax.fori_loop(0, ny // 2, pair, 0)
            for k in range(1, ny):
                ry_copy(c, d, k).start()
            return cc

        lax.fori_loop(0, NZ, group, 0)
        for i in range(2):
            fkv[i, :, part(c)] = dkv[i, :cur, part(c)].astype(jnp.bfloat16)
            for k in range(1, nh):
                b_copy(c, k, i).start()
            out = (out_k, out_v)[i]
            out[:, cols(h, c)] = fkv[i, band(h), part(c)]
            out = (out_kh, out_vh)[i]
            out[:, part(c)] = dkv[i, cur:, part(c)].astype(jnp.bfloat16)

    def rz_copy(c, d, way):
        to = jnp.clip(z + (1 if way == 0 else -1), 0, NZ - 1)
        return copy(sz.at[c, d], rz.at[c, way, d], s_rz.at[c, way, d], r_rz.at[c, way, d], to * ny + y, h)

    def own_sum(c, d):
        acc[...] = dq[c, d * ny + y].astype(jnp.float32)
        for k in range(1, ny):
            ry_copy(c, d, k).wait_recv()
            acc[...] += ry[c, d, k - 1].astype(jnp.float32)

        @pl.when((z <= d) & (z > 0))
        def _():
            rz_copy(c, d, 0).wait_recv()
            acc[...] += rz[c, 0, d].astype(jnp.float32)

        @pl.when((z >= d) & (z < NZ - 1))
        def _():
            rz_copy(c, d, 1).wait_recv()
            acc[...] += rz[c, 1, d].astype(jnp.float32)

    def c_copy(c, k):
        p = (h + k) % nh
        return copy(fq.at[c, band(p), :], out_q.at[:, cols(h, c)], s_c.at[c, k - 1], r_c.at[c, k - 1], t, p)

    def chain(c, n):
        d = order(n)

        @pl.when(d != z)
        def _():
            own_sum(c, d)
            sz[c, d] = acc[...].astype(jnp.bfloat16)

            @pl.when(z < d)
            def _():
                rz_copy(c, d, 0).start()

            @pl.when(z > d)
            def _():
                rz_copy(c, d, 1).start()

    def query_back(c):
        own_sum(c, z)
        fq[c] = acc[...].T.astype(jnp.bfloat16)
        for k in range(1, nh):
            c_copy(c, k).start()
        out_q[:, cols(h, c)] = fq[c, band(h), :]

    def stage(step, cc):
        def each(f, at):
            def run(i, ccc):
                f(at, 1 - i)
                return ccc

            lax.fori_loop(0, 2, run, 0)

        each(forward, step)
        each(own_pass, step)

        @pl.when(step > 0)
        def _():
            each(peer_pass, step - 1)

        half, odd = step // 2, step % 2

        @pl.when((odd == 1) & (half >= 2) & (half - 2 < nc))
        def _():
            pass2(half - 2)

        @pl.when((odd == 0) & (half >= 2) & (half - 2 < nc))
        def _():
            join(half - 2)

        @pl.when((half >= 3) & (half - 3 < nc))
        def _():
            def link(n, ccc):
                chain(half - 3, 2 * odd + n)
                return ccc

            lax.fori_loop(0, 2, link, 0)

            @pl.when(odd == 1)
            def _():
                query_back(half - 3)

        return cc

    lax.fori_loop(0, 2 * nc + 6, stage, 0)

    def finish(c, cc):
        for k in range(1, nh):
            c_copy(c, k).wait()
            for i in range(2):
                b_copy(c, k, i).wait()
                a_copy(c, k, i).wait_send()
                kv_copy(c, k, i).wait_send()
        for k in range(1, nt):
            f_copy(c, k).wait_send()
            st_copy(c, (t + k) % nt).wait_send()

        def sent(n, ccc):
            zz, dist, up, ok = at_slot(n)

            @pl.when(ok)
            def _():
                for k in range(1, ny):
                    y_copy(c, zz, n, k).wait_send()
                for way in range(2):
                    @pl.when(((n == 0) | (up == 1 - way)) & ((z + 1 < NZ) if way == 0 else (z > 0)))
                    def _():
                        z_copy(c, zz, way, dist).wait_send()

            return ccc

        lax.fori_loop(0, n_slot, sent, 0)

        def reduced(d, ccc):
            for k in range(1, ny):
                ry_copy(c, d, k).wait_send()

            @pl.when(z < d)
            def _():
                rz_copy(c, d, 0).wait_send()

            @pl.when(z > d)
            def _():
                rz_copy(c, d, 1).wait_send()

            return ccc

        lax.fori_loop(0, NZ, reduced, 0)
        return cc

    lax.fori_loop(0, nc, finish, 0)


def kernel_split(
    nt, nh, nc,
    hist_len, query, d_out, key_cur, value_cur, key_hist, value_hist,
    out_q, out_k, out_v, out_kh, out_vh,
    qd, kv, dkv, dq, rz, sz, st, st_in, fin, acc, fq, fkv, bias, kt, kept, lens,
    s_a, r_a, s_kv, r_kv, s_z, r_z, s_st, r_st, s_f, r_f,
    s_rz, r_rz, s_b, r_b, s_c, r_c, s_own, s_hist, s_oc, s_h, r_h, s_hb, r_hb, s_l, r_l,
):
    ny = nt // NZ
    rows = query.shape[0]
    feat = query.shape[1] // nh
    part_w = feat // ny
    heads = part_w // HS
    hpc = heads // nc
    width = hpc * HS
    ng = nh * ny
    cur = rows * ng
    hist = key_hist.shape[0]
    n_k = kv.shape[1]
    scale = 1.0 / math.sqrt(HS)
    scale2 = scale * math.log2(math.e)
    t, h = lax.axis_index("tm"), lax.axis_index("head")
    z, y = t // ny, t % ny
    g = y * nh + h

    def copy(src, dst, ss, rs, tm, hd):
        return pltpu.make_async_remote_copy(
            src_ref=src, dst_ref=dst, send_sem=ss, recv_sem=rs,
            device_id=(tm, hd), device_id_type=MESH,
        )

    def peer(k):
        p = (g + k) % ng
        return p, p // nh, p % nh

    def cols(py, ph, c):
        return pl.ds(pl.multiple_of(ph * feat + py * part_w + c * width, HS), width)

    def wide_cols(py, ph):
        return pl.ds(pl.multiple_of(ph * feat + py * part_w, HS), part_w)

    def hist_cols(py, c):
        return pl.ds(pl.multiple_of(py * part_w + c * width, HS), width)

    def hist_rows(py):
        return pl.ds(pl.multiple_of(cur + py * hist, HS), hist)

    def part(c):
        return pl.ds(pl.multiple_of(c * width, HS), width)

    def band(i):
        return pl.ds(pl.multiple_of(i * rows, rows), rows)

    def own_copy(i):
        src = (query, d_out)[i]
        return pltpu.make_async_copy(src.at[:, wide_cols(y, h)], qd.at[z, i, band(g), :], s_own.at[i])

    def own_kv(i):
        src = (key_cur, value_cur)[i]
        return pltpu.make_async_copy(
            src.at[:, pl.ds(pl.multiple_of(h * feat + y * part_w, HS), part_w)], kv.at[i, band(g), :], s_oc.at[i]
        )

    def hist_copy(i):
        src = (key_hist, value_hist)[i]
        return pltpu.make_async_copy(
            src.at[:, pl.ds(pl.multiple_of(y * part_w, HS), part_w)], kv.at[i, hist_rows(y), :], s_hist.at[i]
        )

    def a_copy(k, i):
        src = (query, d_out)[i]
        p, py, ph = peer(k)
        return copy(
            src.at[:, wide_cols(py, ph)], qd.at[z, i, band(g), :],
            s_a.at[k - 1, i], r_a.at[k - 1, i], z * ny + py, ph,
        )

    def kv_copy(k, i):
        src = (key_cur, value_cur)[i]
        p, py, ph = peer(k)
        return copy(
            src.at[:, wide_cols(py, ph)], kv.at[i, band(g), :],
            s_kv.at[k - 1, i], r_kv.at[k - 1, i], z * ny + py, ph,
        )

    def h_copy(k, i):
        src = (key_hist, value_hist)[i]
        py = (y + k) % ny
        return copy(
            src.at[:, pl.ds(pl.multiple_of(py * part_w, HS), part_w)], kv.at[i, hist_rows(y), :],
            s_h.at[k - 1, i], r_h.at[k - 1, i], z * ny + py, h,
        )

    def l_copy(k):
        py = (y + k) % ny
        return copy(lens.at[y], lens.at[y], s_l.at[k - 1], r_l.at[k - 1], z * ny + py, h)

    for i in range(2):
        own_copy(i).start()
        own_kv(i).start()
        hist_copy(i).start()

    barrier = pltpu.get_barrier_semaphore()
    lens[y] = jnp.full(lens.shape[1:], hist_len[0], jnp.int32)
    for k in range(1, NZ):
        to = (z + k) % NZ
        pl.semaphore_signal(barrier, inc=1, device_id=(to * ny + y, h), device_id_type=MESH)
    for k in range(1, ng):
        _, py, ph = peer(k)
        pl.semaphore_signal(barrier, inc=1, device_id=(z * ny + py, ph), device_id_type=MESH)
    pl.semaphore_wait(barrier, NZ + ng - 2)

    for k in range(1, ny):
        l_copy(k).start()

    for i in range(2):
        for k in range(1, ng):
            a_copy(k, i).start()
    for i in range(2):
        for k in range(1, ny):
            h_copy(k, i).start()
        for k in range(1, ng):
            kv_copy(k, i).start()

    st[...] = jnp.zeros_like(st)
    dkv[...] = jnp.zeros_like(dkv)
    for k in range(1, ny):
        l_copy(k).wait_recv()
    bias[:cur, :] = jnp.zeros((cur, cur), jnp.float32)
    slot_row = lax.broadcasted_iota(jnp.int32, (hist, cur), 0)
    for j in range(ny):
        bias[cur + j * hist : cur + (j + 1) * hist, :] = jnp.where(slot_row < lens[j, :1, :], 0.0, -1e30)
    for i in range(2):
        own_kv(i).wait()
        hist_copy(i).wait()

    def z_copy(c, zz, way, hop):
        to = jnp.clip(z + 1 - 2 * way, 0, NZ - 1)
        return copy(qd.at[zz, :, :, part(c)], qd.at[zz, :, :, part(c)], s_z.at[c, way, hop], r_z.at[c, way, hop], to * ny + y, h)

    def st_copy(c, b):
        return copy(st.at[c, b], st_in.at[c, z], s_st.at[c, b], r_st.at[c, z], b * ny + y, h)

    def head_cols(i):
        return pl.ds(pl.multiple_of(i * HS, HS), HS)

    def nt_dot(a, b):
        return lax.dot_general(a, b, (((1,), (1,)), ((), ())), preferred_element_type=jnp.float32)

    def pass1(c, b):
        for i in range(hpc):
            hc = head_cols(c * hpc + i)
            s = nt_dot(kv[0, :, hc], qd[b, 0, :, hc]) * scale2 + bias[...]
            gs = nt_dot(kv[1, :, hc], qd[b, 1, :, hc])
            m = jnp.max(s, axis=0, keepdims=True)
            w = jnp.exp2(s - m)
            kept[c, b, 0, i] = w
            kept[c, b, 1, i] = gs
            st[c, b, i : i + 1, :] = m
            st[c, b, hpc + i : hpc + i + 1, :] = jnp.sum(w, axis=0, keepdims=True)
            st[c, b, 2 * hpc + i : 2 * hpc + i + 1, :] = jnp.sum(w * gs, axis=0, keepdims=True)

        @pl.when(b != z)
        def _():
            st_copy(c, b).start()

    def own_sends(c):
        @pl.when(c == 0)
        def _():
            for i in range(2):
                own_copy(i).wait()
                for k in range(1, ng):
                    a_copy(k, i).wait_recv()

        @pl.when(z + 1 < NZ)
        def _():
            z_copy(c, z, 0, 0).start()

        @pl.when(z > 0)
        def _():
            z_copy(c, z, 1, 0).start()

    def event(step, e):
        c, hop = step // 2 - e, step % 2 + 2 * e
        return c, hop, (c >= 0) & (c < nc)

    def block_at(hop, way):
        zz = jnp.where(way == 0, z - hop, z + hop)
        return zz, (zz >= 0) & (zz < NZ) & ((hop > 0) | (way == 0))

    def forward(step, e):
        c, hop, ok = event(step, e)

        @pl.when(ok & (hop == 0))
        def _():
            own_sends(c)

        def one(way, cc):
            zz, there = block_at(hop, way)

            @pl.when(ok & there & (hop > 0))
            def _():
                z_copy(c, zz, way, hop - 1).wait_recv()
                to = z + 1 - 2 * way

                @pl.when((to >= 0) & (to < NZ))
                def _():
                    z_copy(c, zz, way, hop).start()

            return cc

        lax.fori_loop(0, 2, one, 0)

    def own_pass(step, e):
        c, hop, ok = event(step, e)

        @pl.when(ok & (hop == 0) & (c == 0))
        def _():
            for i in range(2):
                for k in range(1, ng):
                    kv_copy(k, i).wait_recv()
                for k in range(1, ny):
                    h_copy(k, i).wait_recv()
            kt[...] = kv[0].T

        def one(way, cc):
            zz, there = block_at(hop, way)

            @pl.when(ok & there)
            def _():
                pass1(c, zz)

            return cc

        lax.fori_loop(0, 2, one, 0)

    def f_copy(c, k):
        to = (z + k) % NZ
        return copy(fin.at[c, z], fin.at[c, z], s_f.at[c, k - 1], r_f.at[c, k - 1], to * ny + y, h)

    def join(c):
        st_in[c, z] = st[c, z]
        for k in range(1, NZ):
            src = (z + NZ - k) % NZ
            copy(st.at[c, z], st_in.at[c, src], s_st.at[c, src], r_st.at[c, src], src * ny + y, h).wait_recv()
        local = st_in[c]
        top = jnp.max(local[:, :hpc], axis=0)
        back = jnp.exp2(local[:, :hpc] - top[None])
        total = jnp.sum(local[:, hpc : 2 * hpc] * back, axis=0)
        dots = jnp.sum(local[:, 2 * hpc : 3 * hpc] * back, axis=0)
        fin[c, z] = jnp.zeros_like(fin[c, z])
        fin[c, z, :hpc, :] = top
        fin[c, z, hpc : 2 * hpc, :] = 1.0 / total
        fin[c, z, 2 * hpc : 3 * hpc, :] = dots / total
        for k in range(1, NZ):
            f_copy(c, k).start()

    def order(i):
        return jnp.where(z < NZ // 2, NZ - 1 - i, i)

    def b_copy(k, i):
        p, py, ph = peer(k)
        dst = (out_k, out_v)[i]
        return copy(
            fkv.at[i, band(p), :], dst.at[:, wide_cols(y, h)],
            s_b.at[k - 1, i], r_b.at[k - 1, i], z * ny + py, ph,
        )

    def hb_copy(c, k, i):
        py = (y + k) % ny
        dst = (out_kh, out_vh)[i]
        return copy(
            fkv.at[i, hist_rows(py), part(c)], dst.at[:, hist_cols(y, c)],
            s_hb.at[c, k - 1, i], r_hb.at[c, k - 1, i], z * ny + py, h,
        )

    def pass2(c):
        for k in range(1, NZ):
            f_copy(c, k).wait_recv()

        def group(n, cc):
            d = order(n)
            for i in range(hpc):
                hc, lc = head_cols(c * hpc + i), slice(i * HS, (i + 1) * HS)
                q, do = qd[d, 0, :, hc], qd[d, 1, :, hc]

                def row(ref, r):
                    return ref[c, d, r * hpc + i : r * hpc + i + 1, :]

                share = jnp.exp2(row(st, 0) - row(fin, 0)) * row(fin, 1)
                p = kept[c, d, 0, i] * share
                sg = (p * scale * (kept[c, d, 1, i] - row(fin, 2))).astype(jnp.bfloat16)
                dkv[0, :, hc] += jnp.dot(sg, q, preferred_element_type=jnp.float32)
                dkv[1, :, hc] += jnp.dot(p.astype(jnp.bfloat16), do, preferred_element_type=jnp.float32)
                dq[c, d, lc, :] = jnp.dot(kt[hc, :], sg, preferred_element_type=jnp.float32).astype(jnp.bfloat16)
            return cc

        lax.fori_loop(0, NZ, group, 0)
        for i in range(2):
            fkv[i, :, part(c)] = dkv[i, :, part(c)].astype(jnp.bfloat16)
            for k in range(1, ny):
                hb_copy(c, k, i).start()
            out = (out_kh, out_vh)[i]
            out[:, hist_cols(y, c)] = fkv[i, hist_rows(y), part(c)]

        @pl.when(c == nc - 1)
        def _():
            for i in range(2):
                for k in range(1, ng):
                    b_copy(k, i).start()
                out = (out_k, out_v)[i]
                out[:, wide_cols(y, h)] = fkv[i, band(g), :]

    def rz_copy(c, d, way):
        to = jnp.clip(z + (1 if way == 0 else -1), 0, NZ - 1)
        return copy(sz.at[c, d], rz.at[c, way, d], s_rz.at[c, way, d], r_rz.at[c, way, d], to * ny + y, h)

    def own_sum(c, d):
        acc[...] = dq[c, d].astype(jnp.float32)

        @pl.when((z <= d) & (z > 0))
        def _():
            rz_copy(c, d, 0).wait_recv()
            acc[...] += rz[c, 0, d].astype(jnp.float32)

        @pl.when((z >= d) & (z < NZ - 1))
        def _():
            rz_copy(c, d, 1).wait_recv()
            acc[...] += rz[c, 1, d].astype(jnp.float32)

    def c_copy(c, k):
        p, py, ph = peer(k)
        return copy(
            fq.at[c, band(p), :], out_q.at[:, cols(y, h, c)], s_c.at[c, k - 1], r_c.at[c, k - 1], z * ny + py, ph
        )

    def chain(c, n):
        d = order(n)

        @pl.when(d != z)
        def _():
            own_sum(c, d)
            sz[c, d] = acc[...].astype(jnp.bfloat16)

            @pl.when(z < d)
            def _():
                rz_copy(c, d, 0).start()

            @pl.when(z > d)
            def _():
                rz_copy(c, d, 1).start()

    def query_back(c):
        own_sum(c, z)
        fq[c] = acc[...].T.astype(jnp.bfloat16)
        for k in range(1, ng):
            c_copy(c, k).start()
        out_q[:, cols(y, h, c)] = fq[c, band(g), :]

    def stage(step, cc):
        def each(f, at):
            def run(i, ccc):
                f(at, 1 - i)
                return ccc

            lax.fori_loop(0, 2, run, 0)

        each(forward, step)
        each(own_pass, step)

        half, odd = step // 2, step % 2

        @pl.when((odd == 0) & (half >= 2) & (half - 2 < nc))
        def _():
            pass2(half - 2)

        @pl.when((odd == 1) & (half >= 1) & (half - 1 < nc))
        def _():
            join(half - 1)

        late = (step - 5) // 2

        @pl.when((step >= 5) & (late < nc))
        def _():
            def link(n, ccc):
                chain(late, 2 * (1 - odd) + n)
                return ccc

            lax.fori_loop(0, 2, link, 0)

            @pl.when(odd == 0)
            def _():
                query_back(late)

        return cc

    lax.fori_loop(0, 2 * nc + 5, stage, 0)

    def finish(c, cc):
        for k in range(1, ng):
            c_copy(c, k).wait()
        for k in range(1, ny):
            for i in range(2):
                hb_copy(c, k, i).wait()
        for k in range(1, NZ):
            f_copy(c, k).wait_send()
            st_copy(c, (z + k) % NZ).wait_send()

        def sent(hop, ccc):
            def one(way, cccc):
                zz, there = block_at(hop, way)
                to = z + 1 - 2 * way
                there = there | ((hop == 0) & (way == 1))

                @pl.when(there & (to >= 0) & (to < NZ))
                def _():
                    z_copy(c, zz, way, hop).wait_send()

                return cccc

            lax.fori_loop(0, 2, one, 0)
            return ccc

        lax.fori_loop(0, NZ, sent, 0)

        def reduced(d, ccc):
            @pl.when(z < d)
            def _():
                rz_copy(c, d, 0).wait_send()

            @pl.when(z > d)
            def _():
                rz_copy(c, d, 1).wait_send()

            return ccc

        lax.fori_loop(0, NZ, reduced, 0)
        return cc

    for k in range(1, ny):
        l_copy(k).wait_send()
        for i in range(2):
            h_copy(k, i).wait_send()
    for k in range(1, ng):
        for i in range(2):
            b_copy(k, i).wait()
            a_copy(k, i).wait_send()
            kv_copy(k, i).wait_send()
    lax.fori_loop(0, nc, finish, 0)


def shards(query, key_cur, value_cur, d_out, key_hist, value_hist, hist_len):
    nt, nh = lax.axis_size("tm"), lax.axis_size("head")
    ny = nt // NZ
    rows, width = query.shape
    feat = width // nh
    cur = rows * nh
    n_k = cur + key_hist.shape[0]
    nc = 3 if feat % (3 * HS) == 0 else 1
    wide = feat // nc
    store = (nc, nt, 2, wide // HS, n_k, cur)
    keep = math.prod(store) * 4 <= 24 * 1024 * 1024
    if not keep:
        store = (SLOTS, HS)
    hbm = pl.BlockSpec(memory_space=pl.ANY)
    bf, f32 = jnp.bfloat16, jnp.float32
    vmem = pl.BlockSpec(memory_space=pltpu.VMEM)

    def sems(*dims):
        return pltpu.SemaphoreType.DMA(dims)

    out = jax.ShapeDtypeStruct
    out_shape = (
        out((rows, width), bf), out((rows, width), bf), out((rows, width), bf),
        out(key_hist.shape, bf), out(value_hist.shape, bf),
    )
    if feat % (ny * HS) == 0:
        ng, part_w, hist = nh * ny, feat // ny, key_hist.shape[0]
        cur, n_k = rows * ng, rows * ng + ny * hist
        nc = part_w // HS
        wide = HS
        return pl.pallas_call(
            functools.partial(kernel_split, nt, nh, nc),
            out_shape=out_shape,
            in_specs=[pl.BlockSpec(memory_space=pltpu.SMEM)] + [hbm] * 6,
            out_specs=(vmem,) * 5,
            scratch_shapes=[
                pltpu.VMEM((NZ, 2, cur, part_w), bf),
                pltpu.VMEM((2, n_k, part_w), bf),
                pltpu.VMEM((2, n_k, part_w), f32),
                pltpu.VMEM((nc, NZ, wide, cur), bf),
                pltpu.VMEM((nc, 2, NZ, wide, cur), bf),
                pltpu.VMEM((nc, NZ, wide, cur), bf),
                pltpu.VMEM((nc, NZ, SLOTS, cur), f32),
                pltpu.VMEM((nc, NZ, SLOTS, cur), f32),
                pltpu.VMEM((nc, NZ, SLOTS, cur), f32),
                pltpu.VMEM((wide, cur), f32),
                pltpu.VMEM((nc, cur, wide), bf),
                pltpu.VMEM((2, n_k, part_w), bf),
                pltpu.VMEM((n_k, cur), f32),
                pltpu.VMEM((part_w, n_k), bf),
                pltpu.VMEM((nc, NZ, 2, 1, n_k, cur), f32),
                pltpu.VMEM((ny, SLOTS, cur), jnp.int32),
                sems(ng - 1, 2), sems(ng - 1, 2), sems(ng - 1, 2), sems(ng - 1, 2),
                sems(nc, 2, NZ), sems(nc, 2, NZ),
                sems(nc, NZ), sems(nc, NZ), sems(nc, NZ - 1), sems(nc, NZ - 1),
                sems(nc, 2, NZ), sems(nc, 2, NZ),
                sems(ng - 1, 2), sems(ng - 1, 2), sems(nc, ng - 1), sems(nc, ng - 1),
                sems(2), sems(2), sems(2),
                sems(ny - 1, 2), sems(ny - 1, 2), sems(nc, ny - 1, 2), sems(nc, ny - 1, 2),
                sems(ny - 1), sems(ny - 1),
            ],
            compiler_params=pltpu.CompilerParams(
                collective_id=0, has_side_effects=True, vmem_limit_bytes=63 * 1024 * 1024
            ),
            name="attention_backward_split",
        )(hist_len, query, d_out, key_cur, value_cur, key_hist, value_hist)
    return pl.pallas_call(
        functools.partial(kernel, nt, nh, nc, keep),
        out_shape=(
            out((rows, width), bf), out((rows, width), bf), out((rows, width), bf),
            out(key_hist.shape, bf), out(value_hist.shape, bf),
        ),
        in_specs=[pl.BlockSpec(memory_space=pltpu.SMEM)] + [hbm] * 6,
        out_specs=(vmem,) * 5,
        scratch_shapes=[
            pltpu.VMEM((nc, nt, 2, cur, wide), bf),
            pltpu.VMEM((2, n_k, feat), bf),
            pltpu.VMEM((2, n_k, feat), f32),
            pltpu.VMEM((nc, nt, wide, cur), bf),
            pltpu.VMEM((nc, NZ, ny - 1, wide, cur), bf),
            pltpu.VMEM((nc, 2, NZ, wide, cur), bf),
            pltpu.VMEM((nc, NZ, wide, cur), bf),
            pltpu.VMEM((nc, nt, SLOTS, cur), f32),
            pltpu.VMEM((nc, nt, SLOTS, cur), f32),
            pltpu.VMEM((nc, nt, SLOTS, cur), f32),
            pltpu.VMEM((wide, cur), f32),
            pltpu.VMEM((nc, cur, wide), bf),
            pltpu.VMEM((2, cur, feat), bf),
            pltpu.VMEM((n_k, 2 * cur), f32),
            pltpu.VMEM((feat, n_k), bf),
            pltpu.VMEM(store, f32),
            sems(nc, nh - 1, 2), sems(nc, nh - 1, 2), sems(nc, nh - 1, 2), sems(nc, nh - 1, 2),
            sems(nc, 2, NZ), sems(nc, 2, NZ), sems(nc, 2 * NZ - 1, ny - 1), sems(nc, 2 * NZ - 1, ny - 1),
            sems(nc, nt), sems(nc, nt), sems(nc, nt - 1), sems(nc, nt - 1),
            sems(nc, NZ, ny - 1), sems(nc, NZ, ny - 1), sems(nc, 2, NZ), sems(nc, 2, NZ),
            sems(nc, nh - 1, 2), sems(nc, nh - 1, 2), sems(nc, nh - 1), sems(nc, nh - 1),
            sems(nc, 2), sems(2), sems(2),
        ],
        compiler_params=pltpu.CompilerParams(
            collective_id=0, has_side_effects=True, vmem_limit_bytes=63 * 1024 * 1024
        ),
        name="attention_backward",
    )(hist_len, query, d_out, key_cur, value_cur, key_hist, value_hist)


def solution(mesh):
    tok, hist = P(("tm", "head"), None), P("tm", "head")
    return jax.shard_map(
        shards,
        mesh=mesh,
        in_specs=(tok, tok, tok, tok, hist, hist, P("tm")),
        out_specs=(tok, tok, tok, hist, hist),
        check_vma=False,
    )
```

```python
import functools
import math

import jax
import jax.numpy as jnp
from jax import lax
from jax.experimental import pallas as pl
from jax.experimental.pallas import tpu as pltpu
from jax.sharding import PartitionSpec as P

HS = 128
NZ = 4
SLOTS = 8
MESH = pl.DeviceIdType.MESH


def kernel(
    nt, nh, nc, keep,
    hist_len, query, d_out, key_cur, value_cur, key_hist, value_hist,
    out_q, out_k, out_v, out_kh, out_vh,
    qd, kv, dkv, dq, ry, rz, sz, st, st_in, fin, acc, fq, fkv, bias, kt, kept,
    s_a, r_a, s_kv, r_kv, s_z, r_z, s_y, r_y, s_st, r_st, s_f, r_f,
    s_ry, r_ry, s_rz, r_rz, s_b, r_b, s_c, r_c, s_own, s_hist, s_oc,
):
    ny = nt // NZ
    rows = query.shape[0]
    feat = query.shape[1] // nh
    heads = feat // HS
    hpc = heads // nc
    width = hpc * HS
    cur = rows * nh
    n_k = kv.shape[1]
    scale = 1.0 / math.sqrt(HS)
    scale2 = scale * math.log2(math.e)
    t, h = lax.axis_index("tm"), lax.axis_index("head")
    z, y = t // ny, t % ny

    def copy(src, dst, ss, rs, tm, hd):
        return pltpu.make_async_remote_copy(
            src_ref=src, dst_ref=dst, send_sem=ss, recv_sem=rs,
            device_id=(tm, hd), device_id_type=MESH,
        )

    def cols(i, c):
        return pl.ds(pl.multiple_of(i * feat + c * width, HS), width)

    def part(c):
        return pl.ds(pl.multiple_of(c * width, HS), width)

    def band(i):
        return pl.ds(pl.multiple_of(i * rows, rows), rows)

    def own_copy(c, i):
        src = (query, d_out)[i]
        return pltpu.make_async_copy(src.at[:, cols(h, c)], qd.at[c, t, i, band(h), :], s_own.at[c, i])

    def own_kv(i):
        src = (key_cur, value_cur)[i]
        return pltpu.make_async_copy(
            src.at[:, pl.ds(pl.multiple_of(h * feat, HS), feat)], kv.at[i, band(h), :], s_oc.at[i]
        )

    def hist_copy(i):
        return pltpu.make_async_copy((key_hist, value_hist)[i], kv.at[i, pl.ds(cur, n_k - cur), :], s_hist.at[i])

    def a_copy(c, k, i):
        src = (query, d_out)[i]
        p = (h + k) % nh
        return copy(
            src.at[:, cols(p, c)], qd.at[c, t, i, band(h), :], s_a.at[c, k - 1, i], r_a.at[c, k - 1, i], t, p
        )

    def kv_copy(c, k, i):
        src = (key_cur, value_cur)[i]
        p = (h + k) % nh
        return copy(
            src.at[:, cols(p, c)], kv.at[i, band(h), part(c)], s_kv.at[c, k - 1, i], r_kv.at[c, k - 1, i], t, p
        )

    for i in range(2):
        for c in range(nc):
            own_copy(c, i).start()
        own_kv(i).start()
        hist_copy(i).start()

    barrier = pltpu.get_barrier_semaphore()
    for k in range(1, nt):
        pl.semaphore_signal(barrier, inc=1, device_id=((t + k) % nt, h), device_id_type=MESH)
    for k in range(1, nh):
        pl.semaphore_signal(barrier, inc=1, device_id=(t, (h + k) % nh), device_id_type=MESH)
    pl.semaphore_wait(barrier, nt + nh - 2)

    def exchange(c, cc):
        for start in (a_copy, kv_copy):
            for k in range(1, nh):
                for i in range(2):
                    start(c, k, i).start()
        return cc

    lax.fori_loop(0, nc, exchange, 0)
    st[...] = jnp.zeros_like(st)
    dkv[...] = jnp.zeros_like(dkv)
    slot_row = lax.broadcasted_iota(jnp.int32, bias.shape, 0)
    bias[...] = jnp.where(slot_row < cur + hist_len[0], 0.0, -1e30)
    for i in range(2):
        own_kv(i).wait()
        hist_copy(i).wait()

    n_slot = 2 * NZ - 1

    def at_slot(slot):
        dist = (slot + 1) // 2
        up = slot % 2
        zz = jnp.where(up == 1, z - dist, z + dist)
        return zz, dist, up, (zz >= 0) & (zz < NZ)

    def z_copy(c, zz, way, hop):
        to = jnp.clip(z + 1 - 2 * way, 0, NZ - 1)
        b = zz * ny + y
        return copy(qd.at[c, b], qd.at[c, b], s_z.at[c, way, hop], r_z.at[c, way, hop], to * ny + y, h)

    def y_copy(c, zz, slot, k):
        b = zz * ny + y
        p = z * ny + (y + k) % ny
        return copy(qd.at[c, b], qd.at[c, b], s_y.at[c, slot, k - 1], r_y.at[c, slot, k - 1], p, h)

    def st_copy(c, b):
        return copy(st.at[c, b], st_in.at[c, t], s_st.at[c, b], r_st.at[c, t], b, h)

    def head_cols(i):
        return pl.ds(pl.multiple_of(i * HS, HS), HS)

    def nt_dot(a, b):
        return lax.dot_general(a, b, (((1,), (1,)), ((), ())), preferred_element_type=jnp.float32)

    def pass1(c, b):
        for i in range(hpc):
            hc, lc = head_cols(c * hpc + i), slice(i * HS, (i + 1) * HS)
            s = nt_dot(kv[0, :, hc], qd[c, b, 0, :, lc]) * scale2 + bias[:, :cur]
            g = nt_dot(kv[1, :, hc], qd[c, b, 1, :, lc])
            m = jnp.max(s, axis=0, keepdims=True)
            w = jnp.exp2(s - m)
            if keep:
                kept[c, b, 0, i] = w
                kept[c, b, 1, i] = g
            st[c, b, i : i + 1, :] = m
            st[c, b, hpc + i : hpc + i + 1, :] = jnp.sum(w, axis=0, keepdims=True)
            st[c, b, 2 * hpc + i : 2 * hpc + i + 1, :] = jnp.sum(w * g, axis=0, keepdims=True)

        @pl.when(b != t)
        def _():
            st_copy(c, b).start()

    def own_sends(c):
        for i in range(2):
            own_copy(c, i).wait()
            for k in range(1, nh):
                a_copy(c, k, i).wait_recv()

        @pl.when(z + 1 < NZ)
        def _():
            z_copy(c, z, 0, 0).start()

        @pl.when(z > 0)
        def _():
            z_copy(c, z, 1, 0).start()

        for k in range(1, ny):
            y_copy(c, z, 0, k).start()

    def event(step, e):
        c, hop = step // 2 - e, step % 2 + 2 * e
        return c, hop, (c >= 0) & (c < nc)

    def block_at(hop, way):
        zz = jnp.where(way == 0, z - hop, z + hop)
        return zz, jnp.maximum(2 * hop - 1 + way, 0), (zz >= 0) & (zz < NZ) & ((hop > 0) | (way == 0))

    def forward(step, e):
        c, hop, ok = event(step, e)

        @pl.when(ok & (hop == 0))
        def _():
            own_sends(c)

        def one(way, cc):
            zz, slot, there = block_at(hop, way)

            @pl.when(ok & there & (hop > 0))
            def _():
                z_copy(c, zz, way, hop - 1).wait_recv()
                to = z + 1 - 2 * way

                @pl.when((to >= 0) & (to < NZ))
                def _():
                    z_copy(c, zz, way, hop).start()

                for k in range(1, ny):
                    y_copy(c, zz, slot, k).start()

            return cc

        lax.fori_loop(0, 2, one, 0)

    def own_pass(step, e):
        c, hop, ok = event(step, e)

        @pl.when(ok & (hop == 0))
        def _():
            for k in range(1, nh):
                for i in range(2):
                    kv_copy(c, k, i).wait_recv()
            kt[part(c), :] = kv[0, :, part(c)].T

        def one(way, cc):
            zz, _, there = block_at(hop, way)

            @pl.when(ok & there)
            def _():
                pass1(c, zz * ny + y)

            return cc

        lax.fori_loop(0, 2, one, 0)

    def peer_pass(step, e):
        c, hop, ok = event(step, e)

        def one(way, cc):
            zz, slot, there = block_at(hop, way)

            @pl.when(ok & there)
            def _():
                def from_peer(k, ccc):
                    y_copy(c, zz, slot, k).wait_recv()
                    pass1(c, zz * ny + (y + ny - k) % ny)
                    return ccc

                lax.fori_loop(1, ny, from_peer, 0)

            return cc

        lax.fori_loop(0, 2, one, 0)

    def f_copy(c, k):
        return copy(fin.at[c, t], fin.at[c, t], s_f.at[c, k - 1], r_f.at[c, k - 1], (t + k) % nt, h)

    def join(c):
        st_in[c, t] = st[c, t]
        for k in range(1, nt):
            src = (t + nt - k) % nt
            copy(st.at[c, t], st_in.at[c, src], s_st.at[c, src], r_st.at[c, src], src, h).wait_recv()
        local = st_in[c]
        top = jnp.max(local[:, :hpc], axis=0)
        back = jnp.exp2(local[:, :hpc] - top[None])
        total = jnp.sum(local[:, hpc : 2 * hpc] * back, axis=0)
        dots = jnp.sum(local[:, 2 * hpc : 3 * hpc] * back, axis=0)
        fin[c, t] = jnp.zeros_like(fin[c, t])
        fin[c, t, :hpc, :] = top
        fin[c, t, hpc : 2 * hpc, :] = 1.0 / total
        fin[c, t, 2 * hpc : 3 * hpc, :] = dots / total
        for k in range(1, nt):
            f_copy(c, k).start()

    def order(i):
        return jnp.where(z < NZ // 2, NZ - 1 - i, i)

    def ry_copy(c, d, k):
        p = (y + k) % ny
        return copy(
            dq.at[c, d * ny + p], ry.at[c, d, k - 1], s_ry.at[c, d, k - 1], r_ry.at[c, d, k - 1], z * ny + p, h
        )

    def b_copy(c, k, i):
        p = (h + k) % nh
        dst = (out_k, out_v)[i]
        return copy(
            fkv.at[i, band(p), part(c)], dst.at[:, cols(h, c)], s_b.at[c, k - 1, i], r_b.at[c, k - 1, i], t, p
        )

    def pass2(c):
        for k in range(1, nt):
            f_copy(c, k).wait_recv()

        def group(n, cc):
            d = order(n)

            def pair(j, ccc):
                b = d * ny + 2 * j
                for i in range(hpc):
                    hc, lc = head_cols(c * hpc + i), slice(i * HS, (i + 1) * HS)
                    key, val = kv[0, :, hc], kv[1, :, hc]
                    q = jnp.concatenate([qd[c, b, 0, :, lc], qd[c, b + 1, 0, :, lc]], axis=0)
                    do = jnp.concatenate([qd[c, b, 1, :, lc], qd[c, b + 1, 1, :, lc]], axis=0)

                    def row(ref, r):
                        at = slice(r * hpc + i, r * hpc + i + 1)
                        return jnp.concatenate([ref[c, b, at, :], ref[c, b + 1, at, :]], axis=1)

                    if keep:
                        share = jnp.exp2(row(st, 0) - row(fin, 0)) * row(fin, 1)
                        p = jnp.concatenate([kept[c, b, 0, i], kept[c, b + 1, 0, i]], axis=1) * share
                        g = jnp.concatenate([kept[c, b, 1, i], kept[c, b + 1, 1, i]], axis=1)
                    else:
                        s = nt_dot(key, q) * scale2 + bias[...]
                        g = nt_dot(val, do)
                        p = jnp.exp2(s - row(fin, 0)) * row(fin, 1)
                    sg = (p * scale * (g - row(fin, 2))).astype(jnp.bfloat16)
                    dkv[0, :, hc] += jnp.dot(sg, q, preferred_element_type=jnp.float32)
                    dkv[1, :, hc] += jnp.dot(p.astype(jnp.bfloat16), do, preferred_element_type=jnp.float32)
                    term = jnp.dot(kt[hc, :], sg, preferred_element_type=jnp.float32).astype(jnp.bfloat16)
                    dq[c, b, lc, :] = term[:, :cur]
                    dq[c, b + 1, lc, :] = term[:, cur:]
                return ccc

            lax.fori_loop(0, ny // 2, pair, 0)
            for k in range(1, ny):
                ry_copy(c, d, k).start()
            return cc

        lax.fori_loop(0, NZ, group, 0)
        for i in range(2):
            fkv[i, :, part(c)] = dkv[i, :cur, part(c)].astype(jnp.bfloat16)
            for k in range(1, nh):
                b_copy(c, k, i).start()
            out = (out_k, out_v)[i]
            out[:, cols(h, c)] = fkv[i, band(h), part(c)]
            out = (out_kh, out_vh)[i]
            out[:, part(c)] = dkv[i, cur:, part(c)].astype(jnp.bfloat16)

    def rz_copy(c, d, way):
        to = jnp.clip(z + (1 if way == 0 else -1), 0, NZ - 1)
        return copy(sz.at[c, d], rz.at[c, way, d], s_rz.at[c, way, d], r_rz.at[c, way, d], to * ny + y, h)

    def own_sum(c, d):
        acc[...] = dq[c, d * ny + y].astype(jnp.float32)
        for k in range(1, ny):
            ry_copy(c, d, k).wait_recv()
            acc[...] += ry[c, d, k - 1].astype(jnp.float32)

        @pl.when((z <= d) & (z > 0))
        def _():
            rz_copy(c, d, 0).wait_recv()
            acc[...] += rz[c, 0, d].astype(jnp.float32)

        @pl.when((z >= d) & (z < NZ - 1))
        def _():
            rz_copy(c, d, 1).wait_recv()
            acc[...] += rz[c, 1, d].astype(jnp.float32)

    def c_copy(c, k):
        p = (h + k) % nh
        return copy(fq.at[c, band(p), :], out_q.at[:, cols(h, c)], s_c.at[c, k - 1], r_c.at[c, k - 1], t, p)

    def chain(c, n):
        d = order(n)

        @pl.when(d != z)
        def _():
            own_sum(c, d)
            sz[c, d] = acc[...].astype(jnp.bfloat16)

            @pl.when(z < d)
            def _():
                rz_copy(c, d, 0).start()

            @pl.when(z > d)
            def _():
                rz_copy(c, d, 1).start()

    def query_back(c):
        own_sum(c, z)
        fq[c] = acc[...].T.astype(jnp.bfloat16)
        for k in range(1, nh):
            c_copy(c, k).start()
        out_q[:, cols(h, c)] = fq[c, band(h), :]

    def stage(step, cc):
        def each(f, at):
            def run(i, ccc):
                f(at, 1 - i)
                return ccc

            lax.fori_loop(0, 2, run, 0)

        each(forward, step)
        each(own_pass, step)

        @pl.when(step > 0)
        def _():
            each(peer_pass, step - 1)

        half, odd = step // 2, step % 2

        @pl.when((odd == 1) & (half >= 2) & (half - 2 < nc))
        def _():
            pass2(half - 2)

        @pl.when((odd == 0) & (half >= 2) & (half - 2 < nc))
        def _():
            join(half - 2)

        @pl.when((half >= 3) & (half - 3 < nc))
        def _():
            def link(n, ccc):
                chain(half - 3, 2 * odd + n)
                return ccc

            lax.fori_loop(0, 2, link, 0)

            @pl.when(odd == 1)
            def _():
                query_back(half - 3)

        return cc

    lax.fori_loop(0, 2 * nc + 6, stage, 0)

    def finish(c, cc):
        for k in range(1, nh):
            c_copy(c, k).wait()
            for i in range(2):
                b_copy(c, k, i).wait()
                a_copy(c, k, i).wait_send()
                kv_copy(c, k, i).wait_send()
        for k in range(1, nt):
            f_copy(c, k).wait_send()
            st_copy(c, (t + k) % nt).wait_send()

        def sent(n, ccc):
            zz, dist, up, ok = at_slot(n)

            @pl.when(ok)
            def _():
                for k in range(1, ny):
                    y_copy(c, zz, n, k).wait_send()
                for way in range(2):
                    @pl.when(((n == 0) | (up == 1 - way)) & ((z + 1 < NZ) if way == 0 else (z > 0)))
                    def _():
                        z_copy(c, zz, way, dist).wait_send()

            return ccc

        lax.fori_loop(0, n_slot, sent, 0)

        def reduced(d, ccc):
            for k in range(1, ny):
                ry_copy(c, d, k).wait_send()

            @pl.when(z < d)
            def _():
                rz_copy(c, d, 0).wait_send()

            @pl.when(z > d)
            def _():
                rz_copy(c, d, 1).wait_send()

            return ccc

        lax.fori_loop(0, NZ, reduced, 0)
        return cc

    lax.fori_loop(0, nc, finish, 0)


def kernel_split(
    nt, nh, nc,
    hist_len, query, d_out, key_cur, value_cur, key_hist, value_hist,
    out_q, out_k, out_v, out_kh, out_vh,
    qd, kv, dkv, dq, rz, sz, st, st_in, fin, acc, fq, fkv, bias, kt, kept, lens,
    s_a, r_a, s_kv, r_kv, s_z, r_z, s_st, r_st, s_f, r_f,
    s_rz, r_rz, s_b, r_b, s_c, r_c, s_own, s_hist, s_oc, s_h, r_h, s_hb, r_hb, s_l, r_l,
):
    ny = nt // NZ
    rows = query.shape[0]
    feat = query.shape[1] // nh
    part_w = feat // ny
    heads = part_w // HS
    hpc = heads // nc
    width = hpc * HS
    ng = nh * ny
    cur = rows * ng
    hist = key_hist.shape[0]
    n_k = kv.shape[1]
    scale = 1.0 / math.sqrt(HS)
    scale2 = scale * math.log2(math.e)
    t, h = lax.axis_index("tm"), lax.axis_index("head")
    z, y = t // ny, t % ny
    g = y * nh + h

    def copy(src, dst, ss, rs, tm, hd):
        return pltpu.make_async_remote_copy(
            src_ref=src, dst_ref=dst, send_sem=ss, recv_sem=rs,
            device_id=(tm, hd), device_id_type=MESH,
        )

    def peer(k):
        p = (g + k) % ng
        return p, p // nh, p % nh

    def cols(py, ph, c):
        return pl.ds(pl.multiple_of(ph * feat + py * part_w + c * width, HS), width)

    def hist_cols(py, c):
        return pl.ds(pl.multiple_of(py * part_w + c * width, HS), width)

    def hist_rows(py):
        return pl.ds(pl.multiple_of(cur + py * hist, HS), hist)

    def part(c):
        return pl.ds(pl.multiple_of(c * width, HS), width)

    def band(i):
        return pl.ds(pl.multiple_of(i * rows, rows), rows)

    def own_copy(c, i):
        src = (query, d_out)[i]
        return pltpu.make_async_copy(src.at[:, cols(y, h, c)], qd.at[c, z, i, band(g), :], s_own.at[c, i])

    def own_kv(i):
        src = (key_cur, value_cur)[i]
        return pltpu.make_async_copy(
            src.at[:, pl.ds(pl.multiple_of(h * feat + y * part_w, HS), part_w)], kv.at[i, band(g), :], s_oc.at[i]
        )

    def hist_copy(i):
        src = (key_hist, value_hist)[i]
        return pltpu.make_async_copy(
            src.at[:, pl.ds(pl.multiple_of(y * part_w, HS), part_w)], kv.at[i, hist_rows(y), :], s_hist.at[i]
        )

    def a_copy(c, k, i):
        src = (query, d_out)[i]
        p, py, ph = peer(k)
        return copy(
            src.at[:, cols(py, ph, c)], qd.at[c, z, i, band(g), :],
            s_a.at[c, k - 1, i], r_a.at[c, k - 1, i], z * ny + py, ph,
        )

    def kv_copy(c, k, i):
        src = (key_cur, value_cur)[i]
        p, py, ph = peer(k)
        return copy(
            src.at[:, cols(py, ph, c)], kv.at[i, band(g), part(c)],
            s_kv.at[c, k - 1, i], r_kv.at[c, k - 1, i], z * ny + py, ph,
        )

    def h_copy(c, k, i):
        src = (key_hist, value_hist)[i]
        py = (y + k) % ny
        return copy(
            src.at[:, hist_cols(py, c)], kv.at[i, hist_rows(y), part(c)],
            s_h.at[c, k - 1, i], r_h.at[c, k - 1, i], z * ny + py, h,
        )

    def l_copy(k):
        py = (y + k) % ny
        return copy(lens.at[y], lens.at[y], s_l.at[k - 1], r_l.at[k - 1], z * ny + py, h)

    for i in range(2):
        for c in range(nc):
            own_copy(c, i).start()
        own_kv(i).start()
        hist_copy(i).start()

    barrier = pltpu.get_barrier_semaphore()
    lens[y] = jnp.full(lens.shape[1:], hist_len[0], jnp.int32)
    for k in range(1, NZ):
        to = (z + k) % NZ
        pl.semaphore_signal(barrier, inc=1, device_id=(to * ny + y, h), device_id_type=MESH)
    for k in range(1, ng):
        _, py, ph = peer(k)
        pl.semaphore_signal(barrier, inc=1, device_id=(z * ny + py, ph), device_id_type=MESH)
    pl.semaphore_wait(barrier, NZ + ng - 2)

    for k in range(1, ny):
        l_copy(k).start()

    def exchange(c, cc):
        for i in range(2):
            for k in range(1, ng):
                a_copy(c, k, i).start()
        for i in range(2):
            for k in range(1, ng):
                kv_copy(c, k, i).start()
            for k in range(1, ny):
                h_copy(c, k, i).start()
        return cc

    exchange(0, 0)
    st[...] = jnp.zeros_like(st)
    dkv[...] = jnp.zeros_like(dkv)
    for k in range(1, ny):
        l_copy(k).wait_recv()
    bias[:cur, :] = jnp.zeros((cur, cur), jnp.float32)
    slot_row = lax.broadcasted_iota(jnp.int32, (hist, cur), 0)
    for j in range(ny):
        bias[cur + j * hist : cur + (j + 1) * hist, :] = jnp.where(slot_row < lens[j, :1, :], 0.0, -1e30)
    for i in range(2):
        own_kv(i).wait()
        hist_copy(i).wait()

    def z_copy(c, zz, way, hop):
        to = jnp.clip(z + 1 - 2 * way, 0, NZ - 1)
        return copy(qd.at[c, zz], qd.at[c, zz], s_z.at[c, way, hop], r_z.at[c, way, hop], to * ny + y, h)

    def st_copy(c, b):
        return copy(st.at[c, b], st_in.at[c, z], s_st.at[c, b], r_st.at[c, z], b * ny + y, h)

    def head_cols(i):
        return pl.ds(pl.multiple_of(i * HS, HS), HS)

    def nt_dot(a, b):
        return lax.dot_general(a, b, (((1,), (1,)), ((), ())), preferred_element_type=jnp.float32)

    def pass1(c, b):
        for i in range(hpc):
            hc, lc = head_cols(c * hpc + i), slice(i * HS, (i + 1) * HS)
            s = nt_dot(kv[0, :, hc], qd[c, b, 0, :, lc]) * scale2 + bias[...]
            gs = nt_dot(kv[1, :, hc], qd[c, b, 1, :, lc])
            m = jnp.max(s, axis=0, keepdims=True)
            w = jnp.exp2(s - m)
            kept[c, b, 0, i] = w
            kept[c, b, 1, i] = gs
            st[c, b, i : i + 1, :] = m
            st[c, b, hpc + i : hpc + i + 1, :] = jnp.sum(w, axis=0, keepdims=True)
            st[c, b, 2 * hpc + i : 2 * hpc + i + 1, :] = jnp.sum(w * gs, axis=0, keepdims=True)

        @pl.when(b != z)
        def _():
            st_copy(c, b).start()

    def own_sends(c):
        for i in range(2):
            own_copy(c, i).wait()
            for k in range(1, ng):
                a_copy(c, k, i).wait_recv()

        @pl.when(z + 1 < NZ)
        def _():
            z_copy(c, z, 0, 0).start()

        @pl.when(z > 0)
        def _():
            z_copy(c, z, 1, 0).start()

    def event(step, e):
        c, hop = step // 2 - e, step % 2 + 2 * e
        return c, hop, (c >= 0) & (c < nc)

    def block_at(hop, way):
        zz = jnp.where(way == 0, z - hop, z + hop)
        return zz, (zz >= 0) & (zz < NZ) & ((hop > 0) | (way == 0))

    def forward(step, e):
        c, hop, ok = event(step, e)

        @pl.when(ok & (hop == 0))
        def _():
            own_sends(c)

        def one(way, cc):
            zz, there = block_at(hop, way)

            @pl.when(ok & there & (hop > 0))
            def _():
                z_copy(c, zz, way, hop - 1).wait_recv()
                to = z + 1 - 2 * way

                @pl.when((to >= 0) & (to < NZ))
                def _():
                    z_copy(c, zz, way, hop).start()

            return cc

        lax.fori_loop(0, 2, one, 0)

    def own_pass(step, e):
        c, hop, ok = event(step, e)

        @pl.when(ok & (hop == 0))
        def _():
            for i in range(2):
                for k in range(1, ng):
                    kv_copy(c, k, i).wait_recv()
                for k in range(1, ny):
                    h_copy(c, k, i).wait_recv()
            kt[part(c), :] = kv[0, :, part(c)].T

        def one(way, cc):
            zz, there = block_at(hop, way)

            @pl.when(ok & there)
            def _():
                pass1(c, zz)

            return cc

        lax.fori_loop(0, 2, one, 0)

    def f_copy(c, k):
        to = (z + k) % NZ
        return copy(fin.at[c, z], fin.at[c, z], s_f.at[c, k - 1], r_f.at[c, k - 1], to * ny + y, h)

    def join(c):
        st_in[c, z] = st[c, z]
        for k in range(1, NZ):
            src = (z + NZ - k) % NZ
            copy(st.at[c, z], st_in.at[c, src], s_st.at[c, src], r_st.at[c, src], src * ny + y, h).wait_recv()
        local = st_in[c]
        top = jnp.max(local[:, :hpc], axis=0)
        back = jnp.exp2(local[:, :hpc] - top[None])
        total = jnp.sum(local[:, hpc : 2 * hpc] * back, axis=0)
        dots = jnp.sum(local[:, 2 * hpc : 3 * hpc] * back, axis=0)
        fin[c, z] = jnp.zeros_like(fin[c, z])
        fin[c, z, :hpc, :] = top
        fin[c, z, hpc : 2 * hpc, :] = 1.0 / total
        fin[c, z, 2 * hpc : 3 * hpc, :] = dots / total
        for k in range(1, NZ):
            f_copy(c, k).start()

    def order(i):
        return jnp.where(z < NZ // 2, NZ - 1 - i, i)

    def b_copy(c, k, i):
        p, py, ph = peer(k)
        dst = (out_k, out_v)[i]
        return copy(
            fkv.at[i, band(p), part(c)], dst.at[:, cols(y, h, c)],
            s_b.at[c, k - 1, i], r_b.at[c, k - 1, i], z * ny + py, ph,
        )

    def hb_copy(c, k, i):
        py = (y + k) % ny
        dst = (out_kh, out_vh)[i]
        return copy(
            fkv.at[i, hist_rows(py), part(c)], dst.at[:, hist_cols(y, c)],
            s_hb.at[c, k - 1, i], r_hb.at[c, k - 1, i], z * ny + py, h,
        )

    def pass2(c):
        for k in range(1, NZ):
            f_copy(c, k).wait_recv()

        def group(n, cc):
            d = order(n)
            for i in range(hpc):
                hc, lc = head_cols(c * hpc + i), slice(i * HS, (i + 1) * HS)
                q, do = qd[c, d, 0, :, lc], qd[c, d, 1, :, lc]

                def row(ref, r):
                    return ref[c, d, r * hpc + i : r * hpc + i + 1, :]

                share = jnp.exp2(row(st, 0) - row(fin, 0)) * row(fin, 1)
                p = kept[c, d, 0, i] * share
                sg = (p * scale * (kept[c, d, 1, i] - row(fin, 2))).astype(jnp.bfloat16)
                dkv[0, :, hc] += jnp.dot(sg, q, preferred_element_type=jnp.float32)
                dkv[1, :, hc] += jnp.dot(p.astype(jnp.bfloat16), do, preferred_element_type=jnp.float32)
                dq[c, d, lc, :] = jnp.dot(kt[hc, :], sg, preferred_element_type=jnp.float32).astype(jnp.bfloat16)
            return cc

        lax.fori_loop(0, NZ, group, 0)
        for i in range(2):
            fkv[i, :, part(c)] = dkv[i, :, part(c)].astype(jnp.bfloat16)
            for k in range(1, ny):
                hb_copy(c, k, i).start()
            for k in range(1, ng):
                b_copy(c, k, i).start()
            out = (out_k, out_v)[i]
            out[:, cols(y, h, c)] = fkv[i, band(g), part(c)]
            out = (out_kh, out_vh)[i]
            out[:, hist_cols(y, c)] = fkv[i, hist_rows(y), part(c)]

    def rz_copy(c, d, way):
        to = jnp.clip(z + (1 if way == 0 else -1), 0, NZ - 1)
        return copy(sz.at[c, d], rz.at[c, way, d], s_rz.at[c, way, d], r_rz.at[c, way, d], to * ny + y, h)

    def own_sum(c, d):
        acc[...] = dq[c, d].astype(jnp.float32)

        @pl.when((z <= d) & (z > 0))
        def _():
            rz_copy(c, d, 0).wait_recv()
            acc[...] += rz[c, 0, d].astype(jnp.float32)

        @pl.when((z >= d) & (z < NZ - 1))
        def _():
            rz_copy(c, d, 1).wait_recv()
            acc[...] += rz[c, 1, d].astype(jnp.float32)

    def c_copy(c, k):
        p, py, ph = peer(k)
        return copy(
            fq.at[c, band(p), :], out_q.at[:, cols(y, h, c)], s_c.at[c, k - 1], r_c.at[c, k - 1], z * ny + py, ph
        )

    def chain(c, n):
        d = order(n)

        @pl.when(d != z)
        def _():
            own_sum(c, d)
            sz[c, d] = acc[...].astype(jnp.bfloat16)

            @pl.when(z < d)
            def _():
                rz_copy(c, d, 0).start()

            @pl.when(z > d)
            def _():
                rz_copy(c, d, 1).start()

    def query_back(c):
        own_sum(c, z)
        fq[c] = acc[...].T.astype(jnp.bfloat16)
        for k in range(1, ng):
            c_copy(c, k).start()
        out_q[:, cols(y, h, c)] = fq[c, band(g), :]

    def stage(step, cc):
        def each(f, at):
            def run(i, ccc):
                f(at, 1 - i)
                return ccc

            lax.fori_loop(0, 2, run, 0)

        each(forward, step)

        @pl.when((step % 2 == 0) & (step // 2 + 1 < nc))
        def _():
            exchange(step // 2 + 1, 0)

        each(own_pass, step)

        half, odd = step // 2, step % 2

        @pl.when((odd == 0) & (half >= 2) & (half - 2 < nc))
        def _():
            pass2(half - 2)

        @pl.when((odd == 1) & (half >= 1) & (half - 1 < nc))
        def _():
            join(half - 1)

        late = (step - 5) // 2

        @pl.when((step >= 5) & (late < nc))
        def _():
            def link(n, ccc):
                chain(late, 2 * (1 - odd) + n)
                return ccc

            lax.fori_loop(0, 2, link, 0)

            @pl.when(odd == 0)
            def _():
                query_back(late)

        return cc

    lax.fori_loop(0, 2 * nc + 5, stage, 0)

    def finish(c, cc):
        for k in range(1, ng):
            c_copy(c, k).wait()
            for i in range(2):
                b_copy(c, k, i).wait()
                a_copy(c, k, i).wait_send()
                kv_copy(c, k, i).wait_send()
        for k in range(1, ny):
            for i in range(2):
                hb_copy(c, k, i).wait()
                h_copy(c, k, i).wait_send()
        for k in range(1, NZ):
            f_copy(c, k).wait_send()
            st_copy(c, (z + k) % NZ).wait_send()

        def sent(hop, ccc):
            def one(way, cccc):
                zz, there = block_at(hop, way)
                to = z + 1 - 2 * way
                there = there | ((hop == 0) & (way == 1))

                @pl.when(there & (to >= 0) & (to < NZ))
                def _():
                    z_copy(c, zz, way, hop).wait_send()

                return cccc

            lax.fori_loop(0, 2, one, 0)
            return ccc

        lax.fori_loop(0, NZ, sent, 0)

        def reduced(d, ccc):
            @pl.when(z < d)
            def _():
                rz_copy(c, d, 0).wait_send()

            @pl.when(z > d)
            def _():
                rz_copy(c, d, 1).wait_send()

            return ccc

        lax.fori_loop(0, NZ, reduced, 0)
        return cc

    for k in range(1, ny):
        l_copy(k).wait_send()
    lax.fori_loop(0, nc, finish, 0)


def shards(query, key_cur, value_cur, d_out, key_hist, value_hist, hist_len):
    nt, nh = lax.axis_size("tm"), lax.axis_size("head")
    ny = nt // NZ
    rows, width = query.shape
    feat = width // nh
    cur = rows * nh
    n_k = cur + key_hist.shape[0]
    nc = 3 if feat % (3 * HS) == 0 else 1
    wide = feat // nc
    store = (nc, nt, 2, wide // HS, n_k, cur)
    keep = math.prod(store) * 4 <= 24 * 1024 * 1024
    if not keep:
        store = (SLOTS, HS)
    hbm = pl.BlockSpec(memory_space=pl.ANY)
    bf, f32 = jnp.bfloat16, jnp.float32
    vmem = pl.BlockSpec(memory_space=pltpu.VMEM)

    def sems(*dims):
        return pltpu.SemaphoreType.DMA(dims)

    out = jax.ShapeDtypeStruct
    out_shape = (
        out((rows, width), bf), out((rows, width), bf), out((rows, width), bf),
        out(key_hist.shape, bf), out(value_hist.shape, bf),
    )
    if feat % (ny * HS) == 0:
        ng, part_w, hist = nh * ny, feat // ny, key_hist.shape[0]
        cur, n_k = rows * ng, rows * ng + ny * hist
        nc = part_w // HS
        wide = HS
        return pl.pallas_call(
            functools.partial(kernel_split, nt, nh, nc),
            out_shape=out_shape,
            in_specs=[pl.BlockSpec(memory_space=pltpu.SMEM)] + [hbm] * 6,
            out_specs=(vmem,) * 5,
            scratch_shapes=[
                pltpu.VMEM((nc, NZ, 2, cur, wide), bf),
                pltpu.VMEM((2, n_k, part_w), bf),
                pltpu.VMEM((2, n_k, part_w), f32),
                pltpu.VMEM((nc, NZ, wide, cur), bf),
                pltpu.VMEM((nc, 2, NZ, wide, cur), bf),
                pltpu.VMEM((nc, NZ, wide, cur), bf),
                pltpu.VMEM((nc, NZ, SLOTS, cur), f32),
                pltpu.VMEM((nc, NZ, SLOTS, cur), f32),
                pltpu.VMEM((nc, NZ, SLOTS, cur), f32),
                pltpu.VMEM((wide, cur), f32),
                pltpu.VMEM((nc, cur, wide), bf),
                pltpu.VMEM((2, n_k, part_w), bf),
                pltpu.VMEM((n_k, cur), f32),
                pltpu.VMEM((part_w, n_k), bf),
                pltpu.VMEM((nc, NZ, 2, 1, n_k, cur), f32),
                pltpu.VMEM((ny, SLOTS, cur), jnp.int32),
                sems(nc, ng - 1, 2), sems(nc, ng - 1, 2), sems(nc, ng - 1, 2), sems(nc, ng - 1, 2),
                sems(nc, 2, NZ), sems(nc, 2, NZ),
                sems(nc, NZ), sems(nc, NZ), sems(nc, NZ - 1), sems(nc, NZ - 1),
                sems(nc, 2, NZ), sems(nc, 2, NZ),
                sems(nc, ng - 1, 2), sems(nc, ng - 1, 2), sems(nc, ng - 1), sems(nc, ng - 1),
                sems(nc, 2), sems(2), sems(2),
                sems(nc, ny - 1, 2), sems(nc, ny - 1, 2), sems(nc, ny - 1, 2), sems(nc, ny - 1, 2),
                sems(ny - 1), sems(ny - 1),
            ],
            compiler_params=pltpu.CompilerParams(
                collective_id=0, has_side_effects=True, vmem_limit_bytes=63 * 1024 * 1024
            ),
            name="attention_backward_split",
        )(hist_len, query, d_out, key_cur, value_cur, key_hist, value_hist)
    return pl.pallas_call(
        functools.partial(kernel, nt, nh, nc, keep),
        out_shape=(
            out((rows, width), bf), out((rows, width), bf), out((rows, width), bf),
            out(key_hist.shape, bf), out(value_hist.shape, bf),
        ),
        in_specs=[pl.BlockSpec(memory_space=pltpu.SMEM)] + [hbm] * 6,
        out_specs=(vmem,) * 5,
        scratch_shapes=[
            pltpu.VMEM((nc, nt, 2, cur, wide), bf),
            pltpu.VMEM((2, n_k, feat), bf),
            pltpu.VMEM((2, n_k, feat), f32),
            pltpu.VMEM((nc, nt, wide, cur), bf),
            pltpu.VMEM((nc, NZ, ny - 1, wide, cur), bf),
            pltpu.VMEM((nc, 2, NZ, wide, cur), bf),
            pltpu.VMEM((nc, NZ, wide, cur), bf),
            pltpu.VMEM((nc, nt, SLOTS, cur), f32),
            pltpu.VMEM((nc, nt, SLOTS, cur), f32),
            pltpu.VMEM((nc, nt, SLOTS, cur), f32),
            pltpu.VMEM((wide, cur), f32),
            pltpu.VMEM((nc, cur, wide), bf),
            pltpu.VMEM((2, cur, feat), bf),
            pltpu.VMEM((n_k, 2 * cur), f32),
            pltpu.VMEM((feat, n_k), bf),
            pltpu.VMEM(store, f32),
            sems(nc, nh - 1, 2), sems(nc, nh - 1, 2), sems(nc, nh - 1, 2), sems(nc, nh - 1, 2),
            sems(nc, 2, NZ), sems(nc, 2, NZ), sems(nc, 2 * NZ - 1, ny - 1), sems(nc, 2 * NZ - 1, ny - 1),
            sems(nc, nt), sems(nc, nt), sems(nc, nt - 1), sems(nc, nt - 1),
            sems(nc, NZ, ny - 1), sems(nc, NZ, ny - 1), sems(nc, 2, NZ), sems(nc, 2, NZ),
            sems(nc, nh - 1, 2), sems(nc, nh - 1, 2), sems(nc, nh - 1), sems(nc, nh - 1),
            sems(nc, 2), sems(2), sems(2),
        ],
        compiler_params=pltpu.CompilerParams(
            collective_id=0, has_side_effects=True, vmem_limit_bytes=63 * 1024 * 1024
        ),
        name="attention_backward",
    )(hist_len, query, d_out, key_cur, value_cur, key_hist, value_hist)


def solution(mesh):
    tok, hist = P(("tm", "head"), None), P("tm", "head")
    return jax.shard_map(
        shards,
        mesh=mesh,
        in_specs=(tok, tok, tok, tok, hist, hist, P("tm")),
        out_specs=(tok, tok, tok, hist, hist),
        check_vma=False,
    )
```
